512 devices in a mesh: outer: 32 (over y, z_lo), inner: 16 (over x, z_hi, core).
Axes of the slice: x: 4, y: 8, z: 8 (z_hi: 2, z_lo: 4; z = z_hi * 4 + z_lo), core: 2. Of those that a mesh axis runs over, the one named last changes fastest.
Arguments:
- image_emb: bfloat16 [65536, 1152], P(('outer', 'inner')), may hold values from -0.4375 to 0.4375
- text_emb: bfloat16 [65536, 1152], P(('outer', 'inner')), may hold values from -0.4375 to 0.4375
- log_scale: float32 [1], replicated, may hold values from 1.8 to 2.8
- bias: float32 [1], replicated, may hold values from -5 to -3
Outputs:
- image_loss: float32 [65536], P(('outer', 'inner'))
- grad_image: float32 [65536, 1152], P(('outer', 'inner'))
- grad_text: float32 [65536, 1152], P(('outer', 'inner'))
The draws below stay inside these ranges and needn't reach their ends.
All inputs are finite; a program needn't handle non-finite values.
Results may differ from the reference program's by a relative error of at most 0.0042.
Values may be sent and summed in bfloat16 or wider, within the bound.
A program may use at most 64 MiB of HBM per device.

```python
import jax
import jax.numpy as jnp
from jax import lax

D = 1152
REACH = 1
STEPS = 3
GROUP = 2048
BATCH = 65536


def level_of(key, dims, shards, least, high):
    gain = 1.0
    for dim, shards_of in shards:
        draws = jax.random.uniform(jax.random.fold_in(jax.random.fold_in(key, 6), dim), (shards_of,), jnp.float32, least / len(shards), high / len(shards))
        gain = gain * jnp.repeat(jnp.exp(draws), dims[dim] // shards_of).reshape((-1,) + (1,) * (len(dims) - 1 - dim))
    return gain


def centred(rng, extent, width, limit, shards=(), kind=jnp.bfloat16):
    result = jax.random.normal(rng, extent, jnp.float32) * width
    if len(shards) > 0:
        result = level_of(rng, extent, shards, -0.22, 0.18) * result
    return jnp.clip(result, min=-limit, max=limit).astype(kind)


def setup_inputs(seed: int = 0) -> dict:
    key_list = jax.random.split(jax.random.key(seed), 5)
    return {
        "image_emb": centred(key_list[0], (BATCH, D), 0.03, 0.4375, ((0, 512),)),
        "text_emb": centred(key_list[1], (BATCH, D), 0.03, 0.4375, ((0, 512),)),
        "log_scale": jnp.clip(jax.random.uniform(key_list[2], (1,), jnp.float32, 1.8, 2.8), 1.8, 2.8),
        "bias": jnp.clip(jax.random.uniform(key_list[3], (1,), jnp.float32, -5.0, -3.0), -5.0, -3.0),
    }


EPS = 1e-06

def normalize(raw):
    wide = raw.astype(jnp.float32)
    inverse = lax.rsqrt(lax.optimization_barrier(jnp.sum(wide * wide, axis=1, keepdims=True)) + EPS)
    unit = wide * inverse
    return (unit, inverse, unit.astype(jnp.bfloat16))

def tile_terms(images, texts, positive, scale, offset):
    left = images.astype(jnp.float32)
    right = texts.astype(jnp.float32)
    dots = lax.dot_general(left, right, (((1,), (1,)), ((), ())), precision=lax.Precision.HIGHEST, preferred_element_type=jnp.float32)
    logits = scale * dots + offset
    signed = jnp.where(positive, logits, -logits)
    losses = lax.optimization_barrier(jnp.sum(jax.nn.softplus(-signed), axis=1))
    weights = (jax.nn.sigmoid(logits) - positive.astype(jnp.float32)).astype(jnp.bfloat16)
    grads = scale * jnp.dot(weights.astype(jnp.float32), right, precision=lax.Precision.HIGHEST, preferred_element_type=jnp.float32)
    return (losses, grads, weights)

def backprop(unit, inverse, grads):
    return (grads - unit * lax.optimization_barrier(jnp.sum(unit * grads, axis=1, keepdims=True))) * inverse

def reference(image_emb, text_emb, log_scale, bias):
    unit_i, inv_i, zi = normalize(image_emb)
    unit_t, inv_t, zt = normalize(text_emb)
    scale = jnp.exp(log_scale[0])
    offset = bias[0]
    groups = BATCH // GROUP
    zi_g = zi.reshape(groups, GROUP, D)
    zt_g = zt.reshape(groups, GROUP, D)
    offsets = jnp.arange(-REACH, REACH + 1, dtype=jnp.int32)
    columns = jnp.arange(STEPS * GROUP, dtype=jnp.int32)[None, :]
    local_rows = jnp.arange(GROUP, dtype=jnp.int32)[:, None]
    positive = columns == REACH * GROUP + local_rows

    def one_group(text_total, index):
        picks = ((index + offsets) % groups).astype(jnp.int32)
        window = zt_g[picks].reshape(STEPS * GROUP, D)
        rows_b = zi_g[index]
        losses, grads, weights = tile_terms(rows_b, window, positive, scale, offset)
        term = lax.dot_general(weights.astype(jnp.float32), rows_b.astype(jnp.float32), (((0,), (0,)), ((), ())), precision=lax.Precision.HIGHEST, preferred_element_type=jnp.float32)
        text_total = text_total.at[picks].add(scale * term.reshape(STEPS, GROUP, D))
        return (text_total, (losses, grads))
    text_zero = jnp.zeros((groups, GROUP, D), jnp.float32)
    text_total, (losses, grads) = lax.scan(one_group, text_zero, jnp.arange(groups, dtype=jnp.int32))
    image_loss = losses.reshape(BATCH)
    grad_image = backprop(unit_i, inv_i, grads.reshape(BATCH, D))
    grad_text = backprop(unit_t, inv_t, text_total.reshape(BATCH, D))
    return (image_loss, grad_image, grad_text)
```

```python
import jax
import jax.numpy as jnp
from jax import lax
from jax.experimental import pallas as pl
from jax.experimental.pallas import tpu as pltpu
from jax.sharding import PartitionSpec as P

MESH = pl.DeviceIdType.MESH
EPS = 1e-06

X_N = 4
Z_LO = 4
Z_N = 8

OWN, FAR, PREV, NEXT = 0, 1, 2, 3


def unit_of(raw):
    wide = raw.astype(jnp.float32)
    inverse = lax.rsqrt(jnp.sum(wide * wide, axis=1, keepdims=True) + EPS)
    return wide * inverse, inverse


def places(groups):
    outer = lax.axis_index("outer")
    inner = lax.axis_index("inner")
    y, z_lo = outer // Z_LO, outer % Z_LO
    x, z_hi, core = inner // 4, (inner // 2) % 2, inner % 2

    def inner_of(x, z_hi, core):
        return x * 4 + z_hi * 2 + core

    def along_z(by):
        z = (z_hi * Z_LO + z_lo + by + Z_N) % Z_N
        return (y * Z_LO + z % Z_LO, inner_of(x, z // Z_LO, core))

    last = (z_lo == Z_LO - 1).astype(jnp.int32)
    first = (z_lo == 0).astype(jnp.int32)
    return {
        "xn": (outer, inner_of((x + 1) % X_N, z_hi, core)),
        "xp": (outer, inner_of((x + X_N - 1) % X_N, z_hi, core)),
        "zn": along_z(2),
        "zp": along_z(-2),
        "sib": (outer, inner_of(x, z_hi, 1 - core)),
        "gn": ((outer + 1) % groups, inner_of(x, (z_hi + last) % 2, core)),
        "gp": ((outer + groups - 1) % groups, inner_of(x, (z_hi + first) % 2, core)),
    }


def kernel(
    groups, ls_ref, b_ref, img_ref, txt_ref, loss_ref, gi_ref, gt_ref,
    texts, images, wt, tg, ig, loss_acc, relay, far_s, far_r, row_s, row_r, col_s, back, col_r,
    sib_s, sib_r, sib_ls, sib_lr, ret_s, ret_r, ret_ls, ret_lr, ssem, rsem,
):
    rows, width = img_ref.shape
    half = rows // 2
    pair = 2 * rows
    tile = width // 3 if width % 384 == 0 else width
    halves = (pl.ds(0, half), pl.ds(half, half))
    peers = places(groups)
    messages = []

    def message(src, dst, peer):
        index = len(messages)
        messages.append(
            pltpu.make_async_remote_copy(
                src_ref=src, dst_ref=dst, send_sem=ssem.at[index], recv_sem=rsem.at[index],
                device_id=peers[peer], device_id_type=MESH,
            )
        )
        return messages[-1]

    def slot(r, k):
        return (r * 4 + k) * rows

    def text(r, k, h):
        return texts.at[pl.ds(slot(r, k) + h * half, half), :]

    def image(k):
        return images.at[pl.ds(k * rows, rows), :]

    z_out = [message(text(0, OWN, 0), relay.at[halves[0], :], "zn"), message(text(0, OWN, 1), relay.at[halves[1], :], "zp")]
    z_on = [message(relay.at[halves[0], :], text(1, OWN, 0), "zn"), message(relay.at[halves[1], :], text(1, OWN, 1), "zp")]
    to_next = [[message(text(r, OWN, h), text(r, PREV, h), "xn") for h in range(2)] for r in range(2)]
    to_prev = [[message(text(r, OWN, h), text(r, NEXT, h), "xp") for h in range(2)] for r in range(2)]
    far_on = [
        [message(text(r, PREV, 0), text(r, FAR, 0), "xn"), message(text(r, NEXT, 1), text(r, FAR, 1), "xp")]
        for r in range(2)
    ]
    img_next = message(image(0), image(1), "gn")
    img_prev = message(image(0), image(2), "gp")
    img_sib = [message(image(k), image(3 + k), "sib") for k in range(3)]
    far_back = [
        [message(far_s.at[r, halves[h], :], far_r.at[r, halves[h], :], "xp" if h == 0 else "xn") for h in range(2)]
        for r in range(2)
    ]
    row_back = [
        [[message(row_s.at[r, s, halves[h], :], row_r.at[r, s, halves[h], :], "xp" if s == 0 else "xn") for h in range(2)]
         for s in range(2)]
        for r in range(2)
    ]
    z_back = [message(col_s.at[halves[h], :], back.at[halves[h], :], "zp" if h == 0 else "zn") for h in range(2)]
    z_home = [message(back.at[halves[h], :], col_r.at[halves[h], :], "zp" if h == 0 else "zn") for h in range(2)]
    sib_back = [message(sib_s.at[k], sib_r.at[k], "sib") for k in range(3)]
    sib_loss = message(sib_ls, sib_lr, "sib")
    ret = [message(ret_s.at[0], ret_r.at[1], "gp"), message(ret_s.at[1], ret_r.at[0], "gn")]
    ret_loss = [message(ret_ls.at[0], ret_lr.at[1], "gp"), message(ret_ls.at[1], ret_lr.at[0], "gn")]

    barrier = pltpu.get_barrier_semaphore()
    for peer in peers.values():
        pl.semaphore_signal(barrier, inc=1, device_id=peer, device_id_type=MESH)

    texts[pl.ds(0, rows), :] = unit_of(txt_ref[...])[0].astype(jnp.bfloat16)
    images[pl.ds(0, rows), :] = unit_of(img_ref[...])[0].astype(jnp.bfloat16)
    loss_acc[...] = jnp.zeros_like(loss_acc)
    scale = jnp.exp(jnp.full((1, pair), ls_ref[0], jnp.float32))
    offset = b_ref[0]
    pl.semaphore_wait(barrier, len(peers))

    for h in range(2):
        z_out[h].start()
    to_next[0][0].start()
    to_prev[0][1].start()
    img_next.start()
    img_prev.start()
    img_sib[0].start()
    to_next[0][1].start()
    to_prev[0][0].start()

    def weigh(start, j, diagonal):
        columns = pl.ds(pl.multiple_of(j * pair, pair), pair)
        dots = lax.dot_general(
            texts[pl.ds(start, pair), :], images[columns, :], (((1,), (1,)), ((), ())),
            preferred_element_type=jnp.float32,
        )
        logits = scale * dots + offset
        grown = jnp.exp(logits)
        whole = 1.0 + grown
        weights = grown / whole
        if diagonal:
            row = lax.broadcasted_iota(jnp.int32, (pair, pair), 0)
            column = lax.broadcasted_iota(jnp.int32, (pair, pair), 1)
            positive = (row == column) & (row < rows)
            weights = weights - positive.astype(jnp.float32)
            whole = jnp.where(positive, 1.0 + jnp.exp(-logits), whole)
        wt[pl.ds(start, pair), columns] = weights.astype(jnp.bfloat16)
        q = pair // 4
        product = (whole[:q] * whole[q:2 * q]) * (whole[2 * q:3 * q] * whole[3 * q:])
        loss_acc[j] += jnp.sum(jnp.log(product).reshape(q // 8, 8, pair), axis=0)

    def text_partial(start):
        def step(n, carry):
            columns = pl.ds(pl.multiple_of(n * tile, 128), tile)
            tg[pl.ds(start, pair), columns] = jnp.dot(
                wt[pl.ds(start, pair), :], images[:, columns], preferred_element_type=jnp.float32
            )
            return carry
        lax.fori_loop(0, width // tile, step, 0)

    def both(start, diagonal):
        def step(j, carry):
            weigh(start, j, False)
            return carry
        if diagonal:
            weigh(start, 0, True)
        lax.fori_loop(1 if diagonal else 0, 3, step, 0)
        text_partial(start)

    def image_partial(first):
        def step(n, carry):
            columns = pl.ds(pl.multiple_of(n * tile, 128), tile)
            ig[pl.ds(first, 3 * rows), columns] = lax.dot_general(
                wt[:, pl.ds(first, 3 * rows)], texts[:, columns], (((0,), (0,)), ((), ())),
                preferred_element_type=jnp.float32,
            )
            return carry
        lax.fori_loop(0, width // tile, step, 0)

    def partial(r, k, h):
        return tg[pl.ds(slot(r, k) + h * half, half), :]

    def reduce_begin(r):
        far_s[r] = tg[pl.ds(slot(r, FAR), rows), :].astype(jnp.bfloat16)
        far_back[r][0].start()
        far_back[r][1].start()
        row_s[r, 0, halves[1], :] = partial(r, PREV, 1).astype(jnp.bfloat16)
        row_back[r][0][1].start()
        row_s[r, 1, halves[0], :] = partial(r, NEXT, 0).astype(jnp.bfloat16)
        row_back[r][1][0].start()

    def reduce_middle(r):
        far_back[r][0].wait_recv()
        row_s[r, 0, halves[0], :] = (partial(r, PREV, 0) + far_r[r, halves[0], :].astype(jnp.float32)).astype(jnp.bfloat16)
        row_back[r][0][0].start()
        far_back[r][1].wait_recv()
        row_s[r, 1, halves[1], :] = (partial(r, NEXT, 1) + far_r[r, halves[1], :].astype(jnp.float32)).astype(jnp.bfloat16)
        row_back[r][1][1].start()

    def reduce_end(r, h):
        row_back[r][0][h].wait_recv()
        row_back[r][1][h].wait_recv()
        return (
            partial(r, OWN, h)
            + row_r[r, 0, halves[h], :].astype(jnp.float32)
            + row_r[r, 1, halves[h], :].astype(jnp.float32)
        )

    def loss_of(k):
        block = loss_acc[k // 2]
        return jnp.sum(block[:, (k % 2) * rows:(k % 2 + 1) * rows], axis=0, keepdims=True)

    for h in range(2):
        z_out[h].wait_recv()
        z_on[h].start()
    to_next[0][0].wait_recv()
    far_on[0][0].start()
    to_prev[0][1].wait_recv()
    far_on[0][1].start()
    img_next.wait_recv()
    img_sib[1].start()
    img_prev.wait_recv()
    img_sib[2].start()
    to_next[0][1].wait_recv()
    to_prev[0][0].wait_recv()
    for k in range(3):
        img_sib[k].wait_recv()
    both(slot(0, PREV), False)
    for h in range(2):
        z_on[h].wait_recv()
        if h == 0:
            to_next[1][0].start()
            to_prev[1][0].start()
        else:
            to_prev[1][1].start()
            to_next[1][1].start()
    for h in range(2):
        far_on[0][h].wait_recv()
    both(slot(0, OWN), True)
    to_next[1][0].wait_recv()
    far_on[1][0].start()
    to_prev[1][1].wait_recv()
    far_on[1][1].start()
    to_next[1][1].wait_recv()
    to_prev[1][0].wait_recv()
    both(slot(1, PREV), False)
    for h in range(2):
        far_on[1][h].wait_recv()
    both(slot(1, OWN), False)

    reduce_begin(1)
    image_partial(3 * rows)
    for k in (1, 2, 0):
        sib_s[k] = ig[pl.ds((3 + k) * rows, rows), :].astype(jnp.bfloat16)
        sib_back[k].start()
    sib_ls[...] = jnp.zeros_like(sib_ls)
    for k in range(3):
        sib_ls[pl.ds(k, 1), :] = loss_of(3 + k)
    sib_loss.start()
    reduce_middle(1)
    image_partial(0)
    sib_loss.wait_recv()
    for s in range(2):
        sib_back[s + 1].wait_recv()
        ret_s[s] = (ig[pl.ds((s + 1) * rows, rows), :] + sib_r[s + 1].astype(jnp.float32)).astype(jnp.bfloat16)
        ret[s].start()
        ret_ls[s] = jnp.broadcast_to(loss_of(s + 1) + sib_lr[pl.ds(s + 1, 1), :], ret_ls.shape[1:])
        ret_loss[s].start()
    for h in range(2):
        col_s[halves[h], :] = reduce_end(1, h).astype(jnp.bfloat16)
        z_back[h].start()
    reduce_begin(0)
    reduce_middle(0)
    for h in range(2):
        z_back[h].wait_recv()
        z_home[h].start()

    scale_row = jnp.exp(jnp.full((1, width), ls_ref[0], jnp.float32))

    def backprop(raw, grads):
        unit, inverse = unit_of(raw)
        grads = scale_row * grads
        return (grads - unit * jnp.sum(unit * grads, axis=1, keepdims=True)) * inverse

    sib_back[0].wait_recv()
    for s in range(2):
        ret_loss[s].wait_recv()
        ret[s].wait_recv()
    loss_ref[...] = loss_of(0) + sib_lr[pl.ds(0, 1), :] + ret_lr[0, pl.ds(0, 1), :] + ret_lr[1, pl.ds(0, 1), :]
    for h in range(2):
        grads = (
            (ig[pl.ds(h * half, half), :] + sib_r[0, halves[h], :].astype(jnp.float32))
            + (ret_r[0, halves[h], :].astype(jnp.float32) + ret_r[1, halves[h], :].astype(jnp.float32))
        )
        gi_ref[halves[h], :] = backprop(img_ref[halves[h], :], grads)
    for h in range(2):
        near = reduce_end(0, h)
        z_home[h].wait_recv()
        gt_ref[halves[h], :] = backprop(txt_ref[halves[h], :], near + col_r[halves[h], :].astype(jnp.float32))
    for sent in messages:
        sent.wait_send()


N_MESSAGES = 45


def per_device(groups, image_emb, text_emb, log_scale, bias):
    rows, width = image_emb.shape
    half_type, full = jnp.bfloat16, jnp.float32
    vmem = pl.BlockSpec(memory_space=pltpu.VMEM)
    smem = pl.BlockSpec(memory_space=pltpu.SMEM)
    loss, grad_image, grad_text = pl.pallas_call(
        lambda *refs: kernel(groups, *refs),
        out_shape=(
            jax.ShapeDtypeStruct((1, rows), full),
            jax.ShapeDtypeStruct((rows, width), full),
            jax.ShapeDtypeStruct((rows, width), full),
        ),
        in_specs=[smem, smem, vmem, vmem],
        out_specs=(vmem, vmem, vmem),
        scratch_shapes=[
            pltpu.VMEM((8 * rows, width), half_type),
            pltpu.VMEM((6 * rows, width), half_type),
            pltpu.VMEM((8 * rows, 6 * rows), half_type),
            pltpu.VMEM((8 * rows, width), full),
            pltpu.VMEM((6 * rows, width), full),
            pltpu.VMEM((3, 8, 2 * rows), full),
            pltpu.VMEM((rows, width), half_type),
            pltpu.VMEM((2, rows, width), half_type),
            pltpu.VMEM((2, rows, width), half_type),
            pltpu.VMEM((2, 2, rows, width), half_type),
            pltpu.VMEM((2, 2, rows, width), half_type),
            pltpu.VMEM((rows, width), half_type),
            pltpu.VMEM((rows, width), half_type),
            pltpu.VMEM((rows, width), half_type),
            pltpu.VMEM((3, rows, width), half_type),
            pltpu.VMEM((3, rows, width), half_type),
            pltpu.VMEM((8, rows), full),
            pltpu.VMEM((8, rows), full),
            pltpu.VMEM((2, rows, width), half_type),
            pltpu.VMEM((2, rows, width), half_type),
            pltpu.VMEM((2, 8, rows), full),
            pltpu.VMEM((2, 8, rows), full),
            pltpu.SemaphoreType.DMA((N_MESSAGES,)),
            pltpu.SemaphoreType.DMA((N_MESSAGES,)),
        ],
        compiler_params=pltpu.CompilerParams(
            collective_id=0, has_side_effects=True, vmem_limit_bytes=48 * 1024 * 1024
        ),
    )(log_scale, bias, image_emb, text_emb)
    return (loss.reshape(rows), grad_image, grad_text)


def solution(mesh):
    groups = mesh.shape["outer"]
    in_specs = (P(("outer", "inner"), None), P(("outer", "inner"), None), P(), P())
    out_specs = (P(("outer", "inner")), P(("outer", "inner"), None), P(("outer", "inner"), None))
    return jax.shard_map(
        lambda *args: per_device(groups, *args),
        mesh=mesh, in_specs=in_specs, out_specs=out_specs, check_vma=False,
    )
```

```python
import jax
import jax.numpy as jnp
from jax import lax
from jax.experimental import pallas as pl
from jax.experimental.pallas import tpu as pltpu
from jax.sharding import PartitionSpec as P

MESH = pl.DeviceIdType.MESH
EPS = 1e-06

X_N = 4
Z_LO = 4
Z_N = 8

OWN, FAR, PREV, NEXT = 0, 1, 2, 3

CHUNKS = 2


def unit_of(raw):
    wide = raw.astype(jnp.float32)
    inverse = lax.rsqrt(jnp.sum(wide * wide, axis=1, keepdims=True) + EPS)
    return wide * inverse, inverse


def places(groups):
    outer = lax.axis_index("outer")
    inner = lax.axis_index("inner")
    y, z_lo = outer // Z_LO, outer % Z_LO
    x, z_hi, core = inner // 4, (inner // 2) % 2, inner % 2

    def inner_of(x, z_hi, core):
        return x * 4 + z_hi * 2 + core

    def along_z(by):
        z = (z_hi * Z_LO + z_lo + by + Z_N) % Z_N
        return (y * Z_LO + z % Z_LO, inner_of(x, z // Z_LO, core))

    last = (z_lo == Z_LO - 1).astype(jnp.int32)
    first = (z_lo == 0).astype(jnp.int32)
    return {
        "xn": (outer, inner_of((x + 1) % X_N, z_hi, core)),
        "xp": (outer, inner_of((x + X_N - 1) % X_N, z_hi, core)),
        "zn": along_z(2),
        "zp": along_z(-2),
        "sib": (outer, inner_of(x, z_hi, 1 - core)),
        "gn": ((outer + 1) % groups, inner_of(x, (z_hi + last) % 2, core)),
        "gp": ((outer + groups - 1) % groups, inner_of(x, (z_hi + first) % 2, core)),
    }


def kernel(
    groups, ls_ref, b_ref, img_ref, txt_ref, loss_ref, gi_ref, gt_ref,
    texts, images, wt, tg, ig, loss_acc, relay, far_s, far_r, row_s, row_r, col_s, back, col_r,
    sib_s, sib_r, sib_ls, sib_lr, ret_s, ret_r, ret_ls, ret_lr, ssem, rsem,
):
    rows, width = img_ref.shape
    sub = rows // CHUNKS
    half = sub // 2
    pair = 2 * rows
    unit = 4 * sub
    tile = width // 3 if width % 384 == 0 else width
    peers = places(groups)
    messages = []

    def message(src, dst, peer):
        index = len(messages)
        messages.append(
            pltpu.make_async_remote_copy(
                src_ref=src, dst_ref=dst, send_sem=ssem.at[index], recv_sem=rsem.at[index],
                device_id=peers[peer], device_id_type=MESH,
            )
        )
        return messages[-1]

    def base(r, c):
        return (r * CHUNKS + c) * unit

    def text(r, c, k, h):
        return texts.at[pl.ds(base(r, c) + k * sub + h * half, half), :]

    def piece(c, h):
        return pl.ds(c * sub + h * half, half)

    def image(k):
        return images.at[pl.ds(k * rows, rows), :]

    def each(make):
        return [[make(c, h) for h in range(2)] for c in range(CHUNKS)]

    def each_row(make):
        return [each(lambda c, h: make(r, c, h)) for r in range(2)]

    z_out = each(lambda c, h: message(text(0, c, OWN, h), relay.at[piece(c, h), :], ("zn", "zp")[h]))
    z_on = each(lambda c, h: message(relay.at[piece(c, h), :], text(1, c, OWN, h), ("zn", "zp")[h]))
    to_next = each_row(lambda r, c, h: message(text(r, c, OWN, h), text(r, c, PREV, h), "xn"))
    to_prev = each_row(lambda r, c, h: message(text(r, c, OWN, h), text(r, c, NEXT, h), "xp"))
    far_on = each_row(lambda r, c, h: message(text(r, c, (PREV, NEXT)[h], h), text(r, c, FAR, h), ("xn", "xp")[h]))
    img_next = message(image(0), image(1), "gn")
    img_prev = message(image(0), image(2), "gp")
    img_sib = [message(image(k), image(3 + k), "sib") for k in range(3)]
    far_back = each_row(lambda r, c, h: message(far_s.at[r, piece(c, h), :], far_r.at[r, piece(c, h), :], ("xp", "xn")[h]))
    row_back = [
        each_row(lambda r, c, h: message(row_s.at[r, s, piece(c, h), :], row_r.at[r, s, piece(c, h), :], ("xp", "xn")[s]))
        for s in range(2)
    ]
    z_back = each(lambda c, h: message(col_s.at[piece(c, h), :], back.at[piece(c, h), :], ("zp", "zn")[h]))
    z_home = each(lambda c, h: message(back.at[piece(c, h), :], col_r.at[piece(c, h), :], ("zp", "zn")[h]))
    sib_back = [message(sib_s.at[k], sib_r.at[k], "sib") for k in range(3)]
    sib_loss = message(sib_ls, sib_lr, "sib")
    ret = [message(ret_s.at[0], ret_r.at[1], "gp"), message(ret_s.at[1], ret_r.at[0], "gn")]
    ret_loss = [message(ret_ls.at[0], ret_lr.at[1], "gp"), message(ret_ls.at[1], ret_lr.at[0], "gn")]

    barrier = pltpu.get_barrier_semaphore()
    for peer in peers.values():
        pl.semaphore_signal(barrier, inc=1, device_id=peer, device_id_type=MESH)

    own = unit_of(txt_ref[...])[0].astype(jnp.bfloat16)
    for c in range(CHUNKS):
        texts[pl.ds(base(0, c), sub), :] = own[c * sub:(c + 1) * sub]
    images[pl.ds(0, rows), :] = unit_of(img_ref[...])[0].astype(jnp.bfloat16)
    loss_acc[...] = jnp.zeros_like(loss_acc)
    scale = jnp.exp(jnp.full((1, pair), ls_ref[0], jnp.float32))
    offset = b_ref[0]
    pl.semaphore_wait(barrier, len(peers))

    def start(*pairs):
        for one in pairs:
            for copy in one:
                copy.start()

    def arrive(*pairs):
        for one in pairs:
            for copy in one:
                copy.wait_recv()

    def weigh(c, start, j, diagonal):
        columns = pl.ds(j * pair, pair)
        dots = lax.dot_general(
            texts[pl.ds(start, unit), :], images[columns, :], (((1,), (1,)), ((), ())),
            preferred_element_type=jnp.float32,
        )
        logits = scale * dots + offset
        grown = jnp.exp(logits)
        whole = 1.0 + grown
        weights = grown / whole
        if diagonal:
            row = lax.broadcasted_iota(jnp.int32, (unit, pair), 0)
            column = lax.broadcasted_iota(jnp.int32, (unit, pair), 1)
            positive = (row + c * sub == column) & (row < sub)
            weights = weights - positive.astype(jnp.float32)
            whole = jnp.where(positive, 1.0 + jnp.exp(-logits), whole)
        wt[pl.ds(start, unit), columns] = weights.astype(jnp.bfloat16)
        q = unit // 4
        product = (whole[:q] * whole[q:2 * q]) * (whole[2 * q:3 * q] * whole[3 * q:])
        loss_acc[j] += jnp.sum(jnp.log(product).reshape(q // 8, 8, pair), axis=0)

    def both(r, c):
        begin = base(r, c)
        for j in range(3):
            weigh(c, begin, j, r == 0 and j == 0)
        for n in range(width // tile):
            columns = pl.ds(n * tile, tile)
            tg[pl.ds(begin, unit), columns] = jnp.dot(
                wt[pl.ds(begin, unit), :], images[:, columns], preferred_element_type=jnp.float32
            )

    def image_partial(first):
        for n in range(width // tile):
            columns = pl.ds(n * tile, tile)
            ig[pl.ds(first, 3 * rows), columns] = lax.dot_general(
                wt[:, pl.ds(first, 3 * rows)], texts[:, columns], (((0,), (0,)), ((), ())),
                preferred_element_type=jnp.float32,
            )

    def partial(r, c, k, h):
        return tg[pl.ds(base(r, c) + k * sub + h * half, half), :]

    def reduce_begin(r, c):
        for h in range(2):
            far_s[r, piece(c, h), :] = partial(r, c, FAR, h).astype(jnp.bfloat16)
            far_back[r][c][h].start()
        for s in range(2):
            row_s[r, s, piece(c, 1 - s), :] = partial(r, c, (PREV, NEXT)[s], 1 - s).astype(jnp.bfloat16)
            row_back[s][r][c][1 - s].start()

    def reduce_middle(r, c):
        for s in range(2):
            far_back[r][c][s].wait_recv()
            total = partial(r, c, (PREV, NEXT)[s], s) + far_r[r, piece(c, s), :].astype(jnp.float32)
            row_s[r, s, piece(c, s), :] = total.astype(jnp.bfloat16)
            row_back[s][r][c][s].start()

    def reduce_end(r, c, h):
        row_back[0][r][c][h].wait_recv()
        row_back[1][r][c][h].wait_recv()
        return (
            partial(r, c, OWN, h)
            + row_r[r, 0, piece(c, h), :].astype(jnp.float32)
            + row_r[r, 1, piece(c, h), :].astype(jnp.float32)
        )

    def column_home(c):
        for h in range(2):
            col_s[piece(c, h), :] = reduce_end(1, c, h).astype(jnp.bfloat16)
            z_back[c][h].start()

    def loss_of(k):
        block = loss_acc[k // 2]
        return jnp.sum(block[:, (k % 2) * rows:(k % 2 + 1) * rows], axis=0, keepdims=True)

    def far_forward(r, c):
        to_next[r][c][0].wait_recv()
        far_on[r][c][0].start()
        to_prev[r][c][1].wait_recv()
        far_on[r][c][1].start()

    def all_here(r, c):
        to_next[r][c][1].wait_recv()
        to_prev[r][c][0].wait_recv()
        arrive(far_on[r][c])

    def row_out(r, c):
        for h in range(2):
            to_next[r][c][h].start()
            to_prev[r][c][1 - h].start()

    start(z_out[0])
    img_next.start()
    img_prev.start()
    row_out(0, 0)
    img_sib[0].start()
    row_out(0, 1)
    for h in range(2):
        z_out[0][h].wait_recv()
        z_on[0][h].start()
    far_forward(0, 0)
    img_next.wait_recv()
    img_sib[1].start()
    img_prev.wait_recv()
    img_sib[2].start()
    start(z_out[1])
    far_forward(0, 1)
    arrive(z_on[0])
    row_out(1, 0)
    arrive(img_sib)
    all_here(0, 0)
    both(0, 0)
    for h in range(2):
        z_out[1][h].wait_recv()
        z_on[1][h].start()
    far_forward(1, 0)
    all_here(0, 1)
    both(0, 1)
    arrive(z_on[1])
    row_out(1, 1)
    all_here(1, 0)
    both(1, 0)
    reduce_begin(1, 0)
    far_forward(1, 1)
    reduce_middle(1, 0)
    all_here(1, 1)
    both(1, 1)

    reduce_begin(1, 1)
    column_home(0)
    image_partial(3 * rows)
    for k in (1, 2, 0):
        sib_s[k] = ig[pl.ds((3 + k) * rows, rows), :].astype(jnp.bfloat16)
        sib_back[k].start()
    sib_ls[...] = jnp.zeros_like(sib_ls)
    for k in range(3):
        sib_ls[pl.ds(k, 1), :] = loss_of(3 + k)
    sib_loss.start()
    reduce_middle(1, 1)
    image_partial(0)
    for h in range(2):
        z_back[0][h].wait_recv()
        z_home[0][h].start()
    column_home(1)
    sib_loss.wait_recv()
    for s in range(2):
        sib_back[s + 1].wait_recv()
        ret_s[s] = (ig[pl.ds((s + 1) * rows, rows), :] + sib_r[s + 1].astype(jnp.float32)).astype(jnp.bfloat16)
        ret[s].start()
        ret_ls[s] = jnp.broadcast_to(loss_of(s + 1) + sib_lr[pl.ds(s + 1, 1), :], ret_ls.shape[1:])
        ret_loss[s].start()
    for c in range(CHUNKS):
        reduce_begin(0, c)
    for h in range(2):
        z_back[1][h].wait_recv()
        z_home[1][h].start()
    for c in range(CHUNKS):
        reduce_middle(0, c)

    scale_row = jnp.exp(jnp.full((1, width), ls_ref[0], jnp.float32))

    def backprop(raw, grads):
        unit, inverse = unit_of(raw)
        grads = scale_row * grads
        return (grads - unit * jnp.sum(unit * grads, axis=1, keepdims=True)) * inverse

    def finish_text(c):
        for h in range(2):
            near = reduce_end(0, c, h)
            z_home[c][h].wait_recv()
            gt_ref[piece(c, h), :] = backprop(txt_ref[piece(c, h), :], near + col_r[piece(c, h), :].astype(jnp.float32))

    finish_text(0)
    sib_back[0].wait_recv()
    for s in range(2):
        ret_loss[s].wait_recv()
        ret[s].wait_recv()
    loss_ref[...] = loss_of(0) + sib_lr[pl.ds(0, 1), :] + ret_lr[0, pl.ds(0, 1), :] + ret_lr[1, pl.ds(0, 1), :]
    for c in range(CHUNKS):
        for h in range(2):
            here = piece(c, h)
            grads = (
                (ig[here, :] + sib_r[0, here, :].astype(jnp.float32))
                + (ret_r[0, here, :].astype(jnp.float32) + ret_r[1, here, :].astype(jnp.float32))
            )
            gi_ref[here, :] = backprop(img_ref[here, :], grads)
    finish_text(1)
    for sent in messages:
        sent.wait_send()


N_MESSAGES = 77


def per_device(groups, image_emb, text_emb, log_scale, bias):
    rows, width = image_emb.shape
    half_type, full = jnp.bfloat16, jnp.float32
    vmem = pl.BlockSpec(memory_space=pltpu.VMEM)
    smem = pl.BlockSpec(memory_space=pltpu.SMEM)
    loss, grad_image, grad_text = pl.pallas_call(
        lambda *refs: kernel(groups, *refs),
        out_shape=(
            jax.ShapeDtypeStruct((1, rows), full),
            jax.ShapeDtypeStruct((rows, width), full),
            jax.ShapeDtypeStruct((rows, width), full),
        ),
        in_specs=[smem, smem, vmem, vmem],
        out_specs=(vmem, vmem, vmem),
        scratch_shapes=[
            pltpu.VMEM((8 * rows, width), half_type),
            pltpu.VMEM((6 * rows, width), half_type),
            pltpu.VMEM((8 * rows, 6 * rows), half_type),
            pltpu.VMEM((8 * rows, width), full),
            pltpu.VMEM((6 * rows, width), full),
            pltpu.VMEM((3, 8, 2 * rows), full),
            pltpu.VMEM((rows, width), half_type),
            pltpu.VMEM((2, rows, width), half_type),
            pltpu.VMEM((2, rows, width), half_type),
            pltpu.VMEM((2, 2, rows, width), half_type),
            pltpu.VMEM((2, 2, rows, width), half_type),
            pltpu.VMEM((rows, width), half_type),
            pltpu.VMEM((rows, width), half_type),
            pltpu.VMEM((rows, width), half_type),
            pltpu.VMEM((3, rows, width), half_type),
            pltpu.VMEM((3, rows, width), half_type),
            pltpu.VMEM((8, rows), full),
            pltpu.VMEM((8, rows), full),
            pltpu.VMEM((2, rows, width), half_type),
            pltpu.VMEM((2, rows, width), half_type),
            pltpu.VMEM((2, 8, rows), full),
            pltpu.VMEM((2, 8, rows), full),
            pltpu.SemaphoreType.DMA((N_MESSAGES,)),
            pltpu.SemaphoreType.DMA((N_MESSAGES,)),
        ],
        compiler_params=pltpu.CompilerParams(
            collective_id=0, has_side_effects=True, vmem_limit_bytes=48 * 1024 * 1024
        ),
    )(log_scale, bias, image_emb, text_emb)
    return (loss.reshape(rows), grad_image, grad_text)


def solution(mesh):
    groups = mesh.shape["outer"]
    in_specs = (P(("outer", "inner"), None), P(("outer", "inner"), None), P(), P())
    out_specs = (P(("outer", "inner")), P(("outer", "inner"), None), P(("outer", "inner"), None))
    return jax.shard_map(
        lambda *args: per_device(groups, *args),
        mesh=mesh, in_specs=in_specs, out_specs=out_specs, check_vma=False,
    )
```

```python
import jax
import jax.numpy as jnp
from jax import lax
from jax.experimental import pallas as pl
from jax.experimental.pallas import tpu as pltpu
from jax.sharding import PartitionSpec as P

MESH = pl.DeviceIdType.MESH
EPS = 1e-06

X_N = 4
Z_LO = 4
Z_N = 8

OWN, FAR, PREV, NEXT = 0, 1, 2, 3

CHUNKS = 4
UNITS = 2
BOTH = CHUNKS // UNITS


def unit_of(raw):
    wide = raw.astype(jnp.float32)
    inverse = lax.rsqrt(jnp.sum(wide * wide, axis=1, keepdims=True) + EPS)
    return wide * inverse, inverse


def places(groups):
    outer = lax.axis_index("outer")
    inner = lax.axis_index("inner")
    y, z_lo = outer // Z_LO, outer % Z_LO
    x, z_hi, core = inner // 4, (inner // 2) % 2, inner % 2

    def inner_of(x, z_hi, core):
        return x * 4 + z_hi * 2 + core

    def along_z(by):
        z = (z_hi * Z_LO + z_lo + by + Z_N) % Z_N
        return (y * Z_LO + z % Z_LO, inner_of(x, z // Z_LO, core))

    last = (z_lo == Z_LO - 1).astype(jnp.int32)
    first = (z_lo == 0).astype(jnp.int32)
    return {
        "xn": (outer, inner_of((x + 1) % X_N, z_hi, core)),
        "xp": (outer, inner_of((x + X_N - 1) % X_N, z_hi, core)),
        "zn": along_z(2),
        "zp": along_z(-2),
        "sib": (outer, inner_of(x, z_hi, 1 - core)),
        "gn": ((outer + 1) % groups, inner_of(x, (z_hi + last) % 2, core)),
        "gp": ((outer + groups - 1) % groups, inner_of(x, (z_hi + first) % 2, core)),
    }


def kernel(
    groups, ls_ref, b_ref, img_ref, txt_ref, loss_ref, gi_ref, gt_ref,
    texts, images, wt, tg, ig, loss_acc, relay, far_s, far_r, row_s, row_r, col_s, back, col_r,
    sib_s, sib_r, sib_ls, sib_lr, ret_s, ret_r, ret_ls, ret_lr, ssem, rsem,
):
    rows, width = img_ref.shape
    sub = rows // CHUNKS
    half = sub // 2
    pair = 2 * rows
    part = rows // UNITS
    unit = 4 * part
    tile = width // 3 if width % 384 == 0 else width
    peers = places(groups)
    messages = []

    def message(src, dst, peer):
        index = len(messages)
        messages.append(
            pltpu.make_async_remote_copy(
                src_ref=src, dst_ref=dst, send_sem=ssem.at[index], recv_sem=rsem.at[index],
                device_id=peers[peer], device_id_type=MESH,
            )
        )
        return messages[-1]

    def base(r, u):
        return (r * UNITS + u) * unit

    def place(r, c, k):
        return base(r, c // BOTH) + k * part + (c % BOTH) * sub

    def text(r, c, k, h):
        return texts.at[pl.ds(place(r, c, k) + h * half, half), :]

    def chunk(r, c, k):
        return texts.at[pl.ds(place(r, c, k), sub), :]

    def piece(c, h):
        return pl.ds(c * sub + h * half, half)

    def whole_piece(c):
        return pl.ds(c * sub, sub)

    def image(k):
        return images.at[pl.ds(k * rows, rows), :]

    def each(make):
        return [[make(c, h) for h in range(2)] for c in range(CHUNKS)]

    def each_row(make):
        return [each(lambda c, h: make(r, c, h)) for r in range(2)]

    z_out = each(lambda c, h: message(text(0, c, OWN, h), relay.at[piece(c, h), :], ("zn", "zp")[h]))
    z_on = each(lambda c, h: message(relay.at[piece(c, h), :], text(1, c, OWN, h), ("zn", "zp")[h]))
    to_side = each_row(lambda r, c, s: message(chunk(r, c, OWN), chunk(r, c, (PREV, NEXT)[s]), ("xn", "xp")[s]))
    far_on = each_row(lambda r, c, h: message(text(r, c, (PREV, NEXT)[h], h), text(r, c, FAR, h), ("xn", "xp")[h]))
    img_next = message(image(0), image(1), "gn")
    img_prev = message(image(0), image(2), "gp")
    img_sib = [message(image(k), image(3 + k), "sib") for k in range(3)]
    far_back = each_row(lambda r, c, h: message(far_s.at[r, piece(c, h), :], far_r.at[r, piece(c, h), :], ("xp", "xn")[h]))
    row_back = each_row(
        lambda r, c, s: message(row_s.at[r, s, whole_piece(c), :], row_r.at[r, s, whole_piece(c), :], ("xp", "xn")[s])
    )
    z_back = each(lambda c, h: message(col_s.at[piece(c, h), :], back.at[piece(c, h), :], ("zp", "zn")[h]))
    z_home = each(lambda c, h: message(back.at[piece(c, h), :], col_r.at[piece(c, h), :], ("zp", "zn")[h]))
    sib_back = [message(sib_s.at[k], sib_r.at[k], "sib") for k in range(3)]
    sib_loss = message(sib_ls, sib_lr, "sib")
    ret = [message(ret_s.at[0], ret_r.at[1], "gp"), message(ret_s.at[1], ret_r.at[0], "gn")]
    ret_loss = [message(ret_ls.at[0], ret_lr.at[1], "gp"), message(ret_ls.at[1], ret_lr.at[0], "gn")]

    barrier = pltpu.get_barrier_semaphore()
    for peer in peers.values():
        pl.semaphore_signal(barrier, inc=1, device_id=peer, device_id_type=MESH)

    own = unit_of(txt_ref[...])[0].astype(jnp.bfloat16)
    for c in range(CHUNKS):
        texts[pl.ds(place(0, c, OWN), sub), :] = own[c * sub:(c + 1) * sub]
    images[pl.ds(0, rows), :] = unit_of(img_ref[...])[0].astype(jnp.bfloat16)
    loss_acc[...] = jnp.zeros_like(loss_acc)
    scale = jnp.exp(jnp.full((1, pair), ls_ref[0], jnp.float32))
    offset = b_ref[0]
    pl.semaphore_wait(barrier, len(peers))

    def start(*pairs):
        for one in pairs:
            for copy in one:
                copy.start()

    def arrive(*pairs):
        for one in pairs:
            for copy in one:
                copy.wait_recv()

    def weigh(u, start, j, diagonal):
        columns = pl.ds(j * pair, pair)
        dots = lax.dot_general(
            texts[pl.ds(start, unit), :], images[columns, :], (((1,), (1,)), ((), ())),
            preferred_element_type=jnp.float32,
        )
        logits = scale * dots + offset
        grown = jnp.exp(logits)
        whole = 1.0 + grown
        weights = grown / whole
        if diagonal:
            row = lax.broadcasted_iota(jnp.int32, (unit, pair), 0)
            column = lax.broadcasted_iota(jnp.int32, (unit, pair), 1)
            positive = (row + u * part == column) & (row < part)
            weights = weights - positive.astype(jnp.float32)
            whole = jnp.where(positive, 1.0 + jnp.exp(-logits), whole)
        wt[pl.ds(start, unit), columns] = weights.astype(jnp.bfloat16)
        q = unit // 4
        product = (whole[:q] * whole[q:2 * q]) * (whole[2 * q:3 * q] * whole[3 * q:])
        loss_acc[j] += jnp.sum(jnp.log(product).reshape(q // 8, 8, pair), axis=0)

    def both(r, u):
        begin = base(r, u)
        for j in range(3):
            weigh(u, begin, j, r == 0 and j == 0)
        for n in range(width // tile):
            columns = pl.ds(n * tile, tile)
            tg[pl.ds(begin, unit), columns] = jnp.dot(
                wt[pl.ds(begin, unit), :], images[:, columns], preferred_element_type=jnp.float32
            )

    def image_partial(first):
        for n in range(width // tile):
            columns = pl.ds(n * tile, tile)
            ig[pl.ds(first, 3 * rows), columns] = lax.dot_general(
                wt[:, pl.ds(first, 3 * rows)], texts[:, columns], (((0,), (0,)), ((), ())),
                preferred_element_type=jnp.float32,
            )

    def partial(r, c, k, h):
        return tg[pl.ds(place(r, c, k) + h * half, half), :]

    def reduce_begin(r, c):
        for h in range(2):
            far_s[r, piece(c, h), :] = partial(r, c, FAR, h).astype(jnp.bfloat16)
            far_back[r][c][h].start()
        for s in range(2):
            row_s[r, s, piece(c, 1 - s), :] = partial(r, c, (PREV, NEXT)[s], 1 - s).astype(jnp.bfloat16)

    def reduce_middle(r, c):
        for s in range(2):
            far_back[r][c][s].wait_recv()
            total = partial(r, c, (PREV, NEXT)[s], s) + far_r[r, piece(c, s), :].astype(jnp.float32)
            row_s[r, s, piece(c, s), :] = total.astype(jnp.bfloat16)
            row_back[r][c][s].start()

    def reduce_end(r, c):
        arrive(row_back[r][c])
        return (
            tg[pl.ds(place(r, c, OWN), sub), :]
            + row_r[r, 0, whole_piece(c), :].astype(jnp.float32)
            + row_r[r, 1, whole_piece(c), :].astype(jnp.float32)
        )

    def column_home(c):
        col_s[whole_piece(c), :] = reduce_end(1, c).astype(jnp.bfloat16)
        start(z_back[c])

    def pass_on(arrivals, onward):
        for here, there in zip(arrivals, onward):
            here.wait_recv()
            there.start()

    def loss_of(k):
        block = loss_acc[k // 2]
        return jnp.sum(block[:, (k % 2) * rows:(k % 2 + 1) * rows], axis=0, keepdims=True)

    def all_here(r, u):
        for c in range(u * BOTH, (u + 1) * BOTH):
            arrive(far_on[r][c])

    start(z_out[0], z_out[1])
    start(to_side[0][0])
    img_next.start()
    img_prev.start()
    img_sib[0].start()
    start(to_side[0][1], to_side[0][2], to_side[0][3])
    for c in range(2):
        pass_on(z_out[c], z_on[c])
    pass_on(to_side[0][0], far_on[0][0])
    pass_on(to_side[0][1], far_on[0][1])
    for c in range(2):
        arrive(z_on[c])
        start(to_side[1][c])
        start(z_out[2 + c])
    pass_on([img_next, img_prev], img_sib[1:])
    pass_on(to_side[0][2], far_on[0][2])
    pass_on(to_side[0][3], far_on[0][3])
    pass_on(z_out[2], z_on[2])
    pass_on(to_side[1][0], far_on[1][0])
    pass_on(z_out[3], z_on[3])
    pass_on(to_side[1][1], far_on[1][1])
    arrive(img_sib)
    all_here(0, 0)
    both(0, 0)
    for c in (2, 3):
        arrive(z_on[c])
        start(to_side[1][c])
    all_here(1, 0)
    both(1, 0)
    for c in (0, 1):
        reduce_begin(1, c)
    for c in (2, 3):
        pass_on(to_side[1][c], far_on[1][c])
    for c in (0, 1):
        reduce_middle(1, c)
    all_here(0, 1)
    both(0, 1)
    for c in (0, 1):
        column_home(c)
    all_here(1, 1)
    both(1, 1)

    for c in (2, 3):
        reduce_begin(1, c)
    for c in (0, 1):
        pass_on(z_back[c], z_home[c])
    image_partial(3 * rows)
    for k in (1, 2, 0):
        sib_s[k] = ig[pl.ds((3 + k) * rows, rows), :].astype(jnp.bfloat16)
        sib_back[k].start()
    sib_ls[...] = jnp.zeros_like(sib_ls)
    for k in range(3):
        sib_ls[pl.ds(k, 1), :] = loss_of(3 + k)
    sib_loss.start()
    for c in (2, 3):
        reduce_middle(1, c)
    image_partial(0)
    for c in (2, 3):
        column_home(c)
    sib_loss.wait_recv()
    for s in range(2):
        sib_back[s + 1].wait_recv()
        ret_s[s] = (ig[pl.ds((s + 1) * rows, rows), :] + sib_r[s + 1].astype(jnp.float32)).astype(jnp.bfloat16)
        ret[s].start()
        ret_ls[s] = jnp.broadcast_to(loss_of(s + 1) + sib_lr[pl.ds(s + 1, 1), :], ret_ls.shape[1:])
        ret_loss[s].start()
    for c in range(CHUNKS):
        reduce_begin(0, c)
    for c in (2, 3):
        pass_on(z_back[c], z_home[c])
    for c in range(CHUNKS):
        reduce_middle(0, c)

    scale_row = jnp.exp(jnp.full((1, width), ls_ref[0], jnp.float32))

    def backprop(raw, grads):
        unit, inverse = unit_of(raw)
        grads = scale_row * grads
        return (grads - unit * jnp.sum(unit * grads, axis=1, keepdims=True)) * inverse

    def finish_text(c):
        here = whole_piece(c)
        near = reduce_end(0, c)
        arrive(z_home[c])
        gt_ref[here, :] = backprop(txt_ref[here, :], near + col_r[here, :].astype(jnp.float32))

    finish_text(0)
    finish_text(1)
    sib_back[0].wait_recv()
    for s in range(2):
        ret_loss[s].wait_recv()
        ret[s].wait_recv()
    loss_ref[...] = loss_of(0) + sib_lr[pl.ds(0, 1), :] + ret_lr[0, pl.ds(0, 1), :] + ret_lr[1, pl.ds(0, 1), :]
    for c in range(CHUNKS):
        here = whole_piece(c)
        grads = (
            (ig[here, :] + sib_r[0, here, :].astype(jnp.float32))
            + (ret_r[0, here, :].astype(jnp.float32) + ret_r[1, here, :].astype(jnp.float32))
        )
        gi_ref[here, :] = backprop(img_ref[here, :], grads)
    finish_text(2)
    finish_text(3)
    for sent in messages:
        sent.wait_send()


N_MESSAGES = 109


def per_device(groups, image_emb, text_emb, log_scale, bias):
    rows, width = image_emb.shape
    half_type, full = jnp.bfloat16, jnp.float32
    vmem = pl.BlockSpec(memory_space=pltpu.VMEM)
    smem = pl.BlockSpec(memory_space=pltpu.SMEM)
    loss, grad_image, grad_text = pl.pallas_call(
        lambda *refs: kernel(groups, *refs),
        out_shape=(
            jax.ShapeDtypeStruct((1, rows), full),
            jax.ShapeDtypeStruct((rows, width), full),
            jax.ShapeDtypeStruct((rows, width), full),
        ),
        in_specs=[smem, smem, vmem, vmem],
        out_specs=(vmem, vmem, vmem),
        scratch_shapes=[
            pltpu.VMEM((8 * rows, width), half_type),
            pltpu.VMEM((6 * rows, width), half_type),
            pltpu.VMEM((8 * rows, 6 * rows), half_type),
            pltpu.VMEM((8 * rows, width), full),
            pltpu.VMEM((6 * rows, width), full),
            pltpu.VMEM((3, 8, 2 * rows), full),
            pltpu.VMEM((rows, width), half_type),
            pltpu.VMEM((2, rows, width), half_type),
            pltpu.VMEM((2, rows, width), half_type),
            pltpu.VMEM((2, 2, rows, width), half_type),
            pltpu.VMEM((2, 2, rows, width), half_type),
            pltpu.VMEM((rows, width), half_type),
            pltpu.VMEM((rows, width), half_type),
            pltpu.VMEM((rows, width), half_type),
            pltpu.VMEM((3, rows, width), half_type),
            pltpu.VMEM((3, rows, width), half_type),
            pltpu.VMEM((8, rows), full),
            pltpu.VMEM((8, rows), full),
            pltpu.VMEM((2, rows, width), half_type),
            pltpu.VMEM((2, rows, width), half_type),
            pltpu.VMEM((2, 8, rows), full),
            pltpu.VMEM((2, 8, rows), full),
            pltpu.SemaphoreType.DMA((N_MESSAGES,)),
            pltpu.SemaphoreType.DMA((N_MESSAGES,)),
        ],
        compiler_params=pltpu.CompilerParams(
            collective_id=0, has_side_effects=True, vmem_limit_bytes=48 * 1024 * 1024
        ),
    )(log_scale, bias, image_emb, text_emb)
    return (loss.reshape(rows), grad_image, grad_text)


def solution(mesh):
    groups = mesh.shape["outer"]
    in_specs = (P(("outer", "inner"), None), P(("outer", "inner"), None), P(), P())
    out_specs = (P(("outer", "inner")), P(("outer", "inner"), None), P(("outer", "inner"), None))
    return jax.shard_map(
        lambda *args: per_device(groups, *args),
        mesh=mesh, in_specs=in_specs, out_specs=out_specs, check_vma=False,
    )
```

```python
import jax
import jax.numpy as jnp
from jax import lax
from jax.experimental import pallas as pl
from jax.experimental.pallas import tpu as pltpu
from jax.sharding import PartitionSpec as P

MESH = pl.DeviceIdType.MESH
EPS = 1e-06

X_N = 4
Z_LO = 4
Z_N = 8

OWN, FAR, PREV, NEXT = 0, 1, 2, 3

CHUNKS = 2
UNITS = 2
BOTH = CHUNKS // UNITS


def unit_of(raw):
    wide = raw.astype(jnp.float32)
    inverse = lax.rsqrt(jnp.sum(wide * wide, axis=1, keepdims=True) + EPS)
    return wide * inverse, inverse


def places(groups):
    outer = lax.axis_index("outer")
    inner = lax.axis_index("inner")
    y, z_lo = outer // Z_LO, outer % Z_LO
    x, z_hi, core = inner // 4, (inner // 2) % 2, inner % 2

    def inner_of(x, z_hi, core):
        return x * 4 + z_hi * 2 + core

    def along_z(by):
        z = (z_hi * Z_LO + z_lo + by + Z_N) % Z_N
        return (y * Z_LO + z % Z_LO, inner_of(x, z // Z_LO, core))

    last = (z_lo == Z_LO - 1).astype(jnp.int32)
    first = (z_lo == 0).astype(jnp.int32)
    return {
        "xn": (outer, inner_of((x + 1) % X_N, z_hi, core)),
        "xp": (outer, inner_of((x + X_N - 1) % X_N, z_hi, core)),
        "zn": along_z(2),
        "zp": along_z(-2),
        "sib": (outer, inner_of(x, z_hi, 1 - core)),
        "gn": ((outer + 1) % groups, inner_of(x, (z_hi + last) % 2, core)),
        "gp": ((outer + groups - 1) % groups, inner_of(x, (z_hi + first) % 2, core)),
    }


def kernel(
    groups, ls_ref, b_ref, img_ref, txt_ref, loss_ref, gi_ref, gt_ref,
    texts, images, wt, tg, ig, loss_acc, relay, far_s, far_r, row_s, row_r, col_s, back, col_r,
    sib_s, sib_r, sib_ls, sib_lr, ret_s, ret_r, ret_ls, ret_lr, ssem, rsem,
):
    rows, width = img_ref.shape
    sub = rows // CHUNKS
    half = sub // 2
    pair = 2 * rows
    part = rows // UNITS
    unit = 4 * part
    peers = places(groups)
    messages = []

    def message(src, dst, peer):
        index = len(messages)
        messages.append(
            pltpu.make_async_remote_copy(
                src_ref=src, dst_ref=dst, send_sem=ssem.at[index], recv_sem=rsem.at[index],
                device_id=peers[peer], device_id_type=MESH,
            )
        )
        return messages[-1]

    def base(r, u):
        return (r * UNITS + u) * unit

    def place(r, c, k):
        return base(r, c // BOTH) + k * part + (c % BOTH) * sub

    def text(r, c, k, h):
        return texts.at[pl.ds(place(r, c, k) + h * half, half), :]

    def chunk(r, c, k):
        return texts.at[pl.ds(place(r, c, k), sub), :]

    def piece(c, h):
        return pl.ds(c * sub + h * half, half)

    def whole_piece(c):
        return pl.ds(c * sub, sub)

    def image(k):
        return images.at[pl.ds(k * rows, rows), :]

    def each(make):
        return [[make(c, h) for h in range(2)] for c in range(CHUNKS)]

    def each_row(make):
        return [each(lambda c, h: make(r, c, h)) for r in range(2)]

    z_out = each(lambda c, h: message(text(0, c, OWN, h), relay.at[piece(c, h), :], ("zn", "zp")[h]))
    z_on = each(lambda c, h: message(relay.at[piece(c, h), :], text(1, c, OWN, h), ("zn", "zp")[h]))
    to_side = each_row(lambda r, c, s: message(chunk(r, c, OWN), chunk(r, c, (PREV, NEXT)[s]), ("xn", "xp")[s]))
    far_on = each_row(lambda r, c, h: message(text(r, c, (PREV, NEXT)[h], h), text(r, c, FAR, h), ("xn", "xp")[h]))
    img_next = message(image(0), image(1), "gn")
    img_prev = message(image(0), image(2), "gp")
    img_sib = [message(image(k), image(3 + k), "sib") for k in range(3)]
    far_back = each_row(lambda r, c, h: message(far_s.at[r, piece(c, h), :], far_r.at[r, piece(c, h), :], ("xp", "xn")[h]))
    row_back = each_row(
        lambda r, c, s: message(row_s.at[r, s, whole_piece(c), :], row_r.at[r, s, whole_piece(c), :], ("xp", "xn")[s])
    )
    z_back = each(lambda c, h: message(col_s.at[piece(c, h), :], back.at[piece(c, h), :], ("zp", "zn")[h]))
    z_home = each(lambda c, h: message(back.at[piece(c, h), :], col_r.at[piece(c, h), :], ("zp", "zn")[h]))
    sib_back = [message(sib_s.at[k], sib_r.at[k], "sib") for k in range(3)]
    sib_loss = message(sib_ls, sib_lr, "sib")
    ret = [message(ret_s.at[0], ret_r.at[1], "gp"), message(ret_s.at[1], ret_r.at[0], "gn")]
    ret_loss = [message(ret_ls.at[0], ret_lr.at[1], "gp"), message(ret_ls.at[1], ret_lr.at[0], "gn")]

    barrier = pltpu.get_barrier_semaphore()
    for peer in peers.values():
        pl.semaphore_signal(barrier, inc=1, device_id=peer, device_id_type=MESH)

    own = unit_of(txt_ref[...])[0].astype(jnp.bfloat16)
    for c in range(CHUNKS):
        texts[pl.ds(place(0, c, OWN), sub), :] = own[c * sub:(c + 1) * sub]
    images[pl.ds(0, rows), :] = unit_of(img_ref[...])[0].astype(jnp.bfloat16)
    loss_acc[...] = jnp.zeros_like(loss_acc)
    scale = jnp.exp(jnp.full((1, pair), ls_ref[0], jnp.float32))
    offset = b_ref[0]
    pl.semaphore_wait(barrier, len(peers))

    def start(*pairs):
        for one in pairs:
            for copy in one:
                copy.start()

    def arrive(*pairs):
        for one in pairs:
            for copy in one:
                copy.wait_recv()

    def weigh(u, start, j, diagonal):
        columns = pl.ds(j * pair, pair)
        dots = lax.dot_general(
            texts[pl.ds(start, unit), :], images[columns, :], (((1,), (1,)), ((), ())),
            preferred_element_type=jnp.float32,
        )
        logits = scale * dots + offset
        grown = jnp.exp(logits)
        whole = 1.0 + grown
        weights = grown / whole
        if diagonal:
            row = lax.broadcasted_iota(jnp.int32, (unit, pair), 0)
            column = lax.broadcasted_iota(jnp.int32, (unit, pair), 1)
            positive = (row + u * part == column) & (row < part)
            weights = weights - positive.astype(jnp.float32)
            whole = jnp.where(positive, 1.0 + jnp.exp(-logits), whole)
        wt[pl.ds(start, unit), columns] = weights.astype(jnp.bfloat16)
        q = unit // 4
        product = (whole[:q] * whole[q:2 * q]) * (whole[2 * q:3 * q] * whole[3 * q:])
        loss_acc[j] += jnp.sum(jnp.log(product).reshape(q // 8, 8, pair), axis=0)

    def both(r, u):
        begin = base(r, u)
        for j in range(3):
            weigh(u, begin, j, r == 0 and j == 0)
        tg[pl.ds(begin, unit), :] = jnp.dot(
            wt[pl.ds(begin, unit), :], images[...], preferred_element_type=jnp.float32
        )

    def image_partial(r, u, first):
        begin = base(r, u)
        term = lax.dot_general(
            wt[pl.ds(begin, unit), pl.ds(first, 3 * rows)], texts[pl.ds(begin, unit), :], (((0,), (0,)), ((), ())),
            preferred_element_type=jnp.float32,
        )
        if r == 0 and u == 0:
            ig[pl.ds(first, 3 * rows), :] = term
        else:
            ig[pl.ds(first, 3 * rows), :] += term

    def image_partials(r, u):
        image_partial(r, u, 3 * rows)
        image_partial(r, u, 0)

    def partial(r, c, k, h):
        return tg[pl.ds(place(r, c, k) + h * half, half), :]

    def reduce_begin(r, c):
        for h in range(2):
            far_s[r, piece(c, h), :] = partial(r, c, FAR, h).astype(jnp.bfloat16)
            far_back[r][c][h].start()
        for s in range(2):
            row_s[r, s, piece(c, 1 - s), :] = partial(r, c, (PREV, NEXT)[s], 1 - s).astype(jnp.bfloat16)

    def reduce_middle(r, c):
        for s in range(2):
            far_back[r][c][s].wait_recv()
            total = partial(r, c, (PREV, NEXT)[s], s) + far_r[r, piece(c, s), :].astype(jnp.float32)
            row_s[r, s, piece(c, s), :] = total.astype(jnp.bfloat16)
            row_back[r][c][s].start()

    def reduce_end(r, c):
        arrive(row_back[r][c])
        return (
            tg[pl.ds(place(r, c, OWN), sub), :]
            + row_r[r, 0, whole_piece(c), :].astype(jnp.float32)
            + row_r[r, 1, whole_piece(c), :].astype(jnp.float32)
        )

    def column_home(c):
        col_s[whole_piece(c), :] = reduce_end(1, c).astype(jnp.bfloat16)
        start(z_back[c])

    def pass_on(arrivals, onward):
        for here, there in zip(arrivals, onward):
            here.wait_recv()
            there.start()

    def loss_of(k):
        block = loss_acc[k // 2]
        return jnp.sum(block[:, (k % 2) * rows:(k % 2 + 1) * rows], axis=0, keepdims=True)

    def all_here(r, u):
        for c in range(u * BOTH, (u + 1) * BOTH):
            arrive(far_on[r][c])

    start(z_out[0], to_side[0][0])
    img_next.start()
    img_prev.start()
    img_sib[0].start()
    start(to_side[0][1])
    pass_on(z_out[0], z_on[0])
    pass_on(to_side[0][0], far_on[0][0])
    pass_on([img_next, img_prev], img_sib[1:])
    pass_on(to_side[0][1], far_on[0][1])
    arrive(z_on[0])
    start(to_side[1][0], z_out[1])
    arrive(img_sib)
    all_here(0, 0)
    both(0, 0)
    pass_on(z_out[1], z_on[1])
    image_partials(0, 0)
    pass_on(to_side[1][0], far_on[1][0])
    all_here(0, 1)
    both(0, 1)
    arrive(z_on[1])
    start(to_side[1][1])
    image_partials(0, 1)
    all_here(1, 0)
    both(1, 0)
    reduce_begin(1, 0)
    pass_on(to_side[1][1], far_on[1][1])
    image_partials(1, 0)
    reduce_middle(1, 0)
    all_here(1, 1)
    both(1, 1)

    reduce_begin(1, 1)
    column_home(0)
    image_partial(1, 1, 3 * rows)
    for k in (1, 2, 0):
        sib_s[k] = ig[pl.ds((3 + k) * rows, rows), :].astype(jnp.bfloat16)
        sib_back[k].start()
    reduce_middle(1, 1)
    sib_ls[...] = jnp.zeros_like(sib_ls)
    for k in range(3):
        sib_ls[pl.ds(k, 1), :] = loss_of(3 + k)
    sib_loss.start()
    image_partial(1, 1, 0)
    pass_on(z_back[0], z_home[0])
    column_home(1)
    sib_loss.wait_recv()
    for s in range(2):
        sib_back[s + 1].wait_recv()
        ret_s[s] = (ig[pl.ds((s + 1) * rows, rows), :] + sib_r[s + 1].astype(jnp.float32)).astype(jnp.bfloat16)
        ret[s].start()
        ret_ls[s] = jnp.broadcast_to(loss_of(s + 1) + sib_lr[pl.ds(s + 1, 1), :], ret_ls.shape[1:])
        ret_loss[s].start()
    for c in range(CHUNKS):
        reduce_begin(0, c)
    pass_on(z_back[1], z_home[1])
    for c in range(CHUNKS):
        reduce_middle(0, c)

    scale_row = jnp.exp(jnp.full((1, width), ls_ref[0], jnp.float32))

    def backprop(raw, grads):
        unit, inverse = unit_of(raw)
        grads = scale_row * grads
        return (grads - unit * jnp.sum(unit * grads, axis=1, keepdims=True)) * inverse

    def finish_text(c):
        here = whole_piece(c)
        near = reduce_end(0, c)
        arrive(z_home[c])
        gt_ref[here, :] = backprop(txt_ref[here, :], near + col_r[here, :].astype(jnp.float32))

    finish_text(0)
    sib_back[0].wait_recv()
    for s in range(2):
        ret_loss[s].wait_recv()
        ret[s].wait_recv()
    loss_ref[...] = loss_of(0) + sib_lr[pl.ds(0, 1), :] + ret_lr[0, pl.ds(0, 1), :] + ret_lr[1, pl.ds(0, 1), :]
    for c in range(CHUNKS):
        here = whole_piece(c)
        grads = (
            (ig[here, :] + sib_r[0, here, :].astype(jnp.float32))
            + (ret_r[0, here, :].astype(jnp.float32) + ret_r[1, here, :].astype(jnp.float32))
        )
        gi_ref[here, :] = backprop(img_ref[here, :], grads)
    finish_text(1)
    for sent in messages:
        sent.wait_send()


N_MESSAGES = 61


def per_device(groups, image_emb, text_emb, log_scale, bias):
    rows, width = image_emb.shape
    half_type, full = jnp.bfloat16, jnp.float32
    vmem = pl.BlockSpec(memory_space=pltpu.VMEM)
    smem = pl.BlockSpec(memory_space=pltpu.SMEM)
    loss, grad_image, grad_text = pl.pallas_call(
        lambda *refs: kernel(groups, *refs),
        out_shape=(
            jax.ShapeDtypeStruct((1, rows), full),
            jax.ShapeDtypeStruct((rows, width), full),
            jax.ShapeDtypeStruct((rows, width), full),
        ),
        in_specs=[smem, smem, vmem, vmem],
        out_specs=(vmem, vmem, vmem),
        scratch_shapes=[
            pltpu.VMEM((8 * rows, width), half_type),
            pltpu.VMEM((6 * rows, width), half_type),
            pltpu.VMEM((8 * rows, 6 * rows), half_type),
            pltpu.VMEM((8 * rows, width), full),
            pltpu.VMEM((6 * rows, width), full),
            pltpu.VMEM((3, 8, 2 * rows), full),
            pltpu.VMEM((rows, width), half_type),
            pltpu.VMEM((2, rows, width), half_type),
            pltpu.VMEM((2, rows, width), half_type),
            pltpu.VMEM((2, 2, rows, width), half_type),
            pltpu.VMEM((2, 2, rows, width), half_type),
            pltpu.VMEM((rows, width), half_type),
            pltpu.VMEM((rows, width), half_type),
            pltpu.VMEM((rows, width), half_type),
            pltpu.VMEM((3, rows, width), half_type),
            pltpu.VMEM((3, rows, width), half_type),
            pltpu.VMEM((8, rows), full),
            pltpu.VMEM((8, rows), full),
            pltpu.VMEM((2, rows, width), half_type),
            pltpu.VMEM((2, rows, width), half_type),
            pltpu.VMEM((2, 8, rows), full),
            pltpu.VMEM((2, 8, rows), full),
            pltpu.SemaphoreType.DMA((N_MESSAGES,)),
            pltpu.SemaphoreType.DMA((N_MESSAGES,)),
        ],
        compiler_params=pltpu.CompilerParams(
            collective_id=0, has_side_effects=True, vmem_limit_bytes=48 * 1024 * 1024
        ),
    )(log_scale, bias, image_emb, text_emb)
    return (loss.reshape(rows), grad_image, grad_text)


def solution(mesh):
    groups = mesh.shape["outer"]
    in_specs = (P(("outer", "inner"), None), P(("outer", "inner"), None), P(), P())
    out_specs = (P(("outer", "inner")), P(("outer", "inner"), None), P(("outer", "inner"), None))
    return jax.shard_map(
        lambda *args: per_device(groups, *args),
        mesh=mesh, in_specs=in_specs, out_specs=out_specs, check_vma=False,
    )
```

```python
import jax
import jax.numpy as jnp
from jax import lax
from jax.experimental import pallas as pl
from jax.experimental.pallas import tpu as pltpu
from jax.sharding import PartitionSpec as P

MESH = pl.DeviceIdType.MESH
EPS = 1e-06

X_N = 4
Z_LO = 4
Z_N = 8

OWN, FAR, PREV, NEXT = 0, 1, 2, 3
UP1, DOWN1, UP3, DOWN3, OVER = 1, 2, 3, 4, 5

CHUNKS = 2
PARTS = 2


def unit_of(raw):
    wide = raw.astype(jnp.float32)
    inverse = lax.rsqrt(jnp.sum(wide * wide, axis=1, keepdims=True) + EPS)
    return wide * inverse, inverse


def places(groups):
    outer = lax.axis_index("outer")
    inner = lax.axis_index("inner")
    z_lo = outer % Z_LO
    x, z_hi, core = inner // 4, (inner // 2) % 2, inner % 2

    def inner_of(x, z_hi, core):
        return x * 4 + z_hi * 2 + core

    def group_by(by):
        z = (z_hi * Z_LO + z_lo + by + Z_N) % Z_N
        step = by if by in (1, -1) else -by
        return ((outer + step + groups) % groups, inner_of(x, z // Z_LO, core))

    return {
        "xn": (outer, inner_of((x + 1) % X_N, z_hi, core)),
        "xp": (outer, inner_of((x + X_N - 1) % X_N, z_hi, core)),
        "sib": (outer, inner_of(x, z_hi, 1 - core)),
        "gn": group_by(1),
        "gp": group_by(-1),
        "tn": group_by(2),
        "tp": group_by(-2),
    }


def kernel(
    groups, ls_ref, b_ref, img_ref, txt_ref, loss_ref, gi_ref, gt_ref,
    texts, images, wt, tg, ig, loss_acc, over_s, over_r, three_s, three_r, one_s, one_r,
    sib_s, sib_r, far_s, far_r, row_s, row_r, over_ls, over_lr, three_ls, three_lr, one_ls, one_lr, ssem, rsem,
):
    rows, width = img_ref.shape
    sub = rows // CHUNKS
    half = sub // 2
    part = rows // PARTS
    edge = part // 2
    tile = 2 * rows
    row_texts = 4 * rows
    peers = places(groups)
    messages = []

    def message(src, dst, peer):
        index = len(messages)
        messages.append(
            pltpu.make_async_remote_copy(
                src_ref=src, dst_ref=dst, send_sem=ssem.at[index], recv_sem=rsem.at[index],
                device_id=peers[peer], device_id_type=MESH,
            )
        )
        return messages[-1]

    def at(c, k, h=0):
        return (c * 6 + k) * sub + h * half

    def image(c, k):
        return images.at[pl.ds(at(c, k), sub), :]

    def image_half(c, k, h):
        return images.at[pl.ds(at(c, k, h), half), :]

    def text(q, j):
        return texts.at[pl.ds((q * 4 + j) * rows, rows), :]

    def text_part(j, p):
        return texts.at[pl.ds(j * rows + p * part, part), :]

    def text_edge(j, p, e):
        return texts.at[pl.ds(j * rows + p * part + e * edge, edge), :]

    def halves(h):
        return pl.ds(h * half, half)

    def parts(p):
        return pl.ds(p * part, part)

    def edges(p, e):
        return pl.ds(p * part + e * edge, edge)

    z1 = [[message(image(c, OWN), image(c, UP1), "gn"), message(image(c, OWN), image(c, DOWN1), "gp")] for c in range(CHUNKS)]
    z3 = [[message(image(c, UP1), image(c, UP3), "tn"), message(image(c, DOWN1), image(c, DOWN3), "tp")] for c in range(CHUNKS)]
    z4 = [
        [message(image_half(c, UP3, 0), image_half(c, OVER, 0), "gn"), message(image_half(c, DOWN3, 1), image_half(c, OVER, 1), "gp")]
        for c in range(CHUNKS)
    ]
    x1 = [[message(text_part(OWN, p), text_part((PREV, NEXT)[s], p), ("xn", "xp")[s]) for s in range(2)] for p in range(PARTS)]
    x2 = [
        [message(text_edge((PREV, NEXT)[s], p, s), text_edge(FAR, p, s), ("xn", "xp")[s]) for s in range(2)]
        for p in range(PARTS)
    ]
    across = [message(text(0, j), text(1, j), "sib") for j in range(4)]
    b4 = [[message(over_s.at[c, halves(h), :], over_r.at[c, halves(h), :], ("gp", "gn")[h]) for h in range(2)] for c in range(CHUNKS)]
    b3 = [[message(three_s.at[c, h], three_r.at[c, h], ("tp", "tn")[h]) for h in range(2)] for c in range(CHUNKS)]
    b1 = [[message(one_s.at[c, h], one_r.at[c, h], ("gp", "gn")[h]) for h in range(2)] for c in range(CHUNKS)]
    back = [[message(sib_s.at[j, parts(p), :], sib_r.at[j, parts(p), :], "sib") for j in range(4)] for p in range(PARTS)]
    t2 = [[message(far_s.at[edges(p, s), :], far_r.at[edges(p, s), :], ("xp", "xn")[s]) for s in range(2)] for p in range(PARTS)]
    t1 = [[message(row_s.at[s, parts(p), :], row_r.at[s, parts(p), :], ("xp", "xn")[s]) for s in range(2)] for p in range(PARTS)]
    l4 = [message(over_ls, over_lr.at[h], ("gp", "gn")[h]) for h in range(2)]
    l3 = [message(three_ls.at[h], three_lr.at[h], ("tp", "tn")[h]) for h in range(2)]
    l1 = [message(one_ls.at[h], one_lr.at[h], ("gp", "gn")[h]) for h in range(2)]

    def start(copies):
        for copy in copies:
            copy.start()

    def arrive(copies):
        for copy in copies:
            copy.wait_recv()

    def pass_on(arrivals, onward):
        for here, there in zip(arrivals, onward):
            here.wait_recv()
            there.start()

    barrier = pltpu.get_barrier_semaphore()
    for peer in peers.values():
        pl.semaphore_signal(barrier, inc=1, device_id=peer, device_id_type=MESH)
    own = unit_of(img_ref[...])[0].astype(jnp.bfloat16)
    for c in range(CHUNKS):
        images[pl.ds(at(c, OWN), sub), :] = own[c * sub:(c + 1) * sub]
    texts[pl.ds(0, rows), :] = unit_of(txt_ref[...])[0].astype(jnp.bfloat16)
    scale = jnp.exp(jnp.full((1, tile), ls_ref[0], jnp.float32))
    offset = b_ref[0]
    pl.semaphore_wait(barrier, len(peers))

    def weigh(begin, size, c, diagonal):
        here = pl.ds(begin, size)
        product = None
        for n in range(4):
            columns = pl.ds(n * tile, tile)
            dots = lax.dot_general(
                images[here, :], texts[columns, :], (((1,), (1,)), ((), ())), preferred_element_type=jnp.float32
            )
            logits = scale * dots + offset
            grown = jnp.exp(logits)
            whole = 1.0 + grown
            weights = grown / whole
            if diagonal and n == 0:
                row = lax.broadcasted_iota(jnp.int32, (size, tile), 0)
                column = lax.broadcasted_iota(jnp.int32, (size, tile), 1)
                positive = (row + c * sub == column) & (row < sub)
                weights = weights - positive.astype(jnp.float32)
                whole = jnp.where(positive, 1.0 + jnp.exp(-logits), whole)
            wt[here, columns] = weights.astype(jnp.bfloat16)
            product = whole if product is None else product * whole
        logs = jnp.log(product)
        loss_acc[here, :] = logs[:, :rows] + logs[:, rows:]
        ig[here, :] = jnp.dot(wt[here, :], texts[...], preferred_element_type=jnp.float32)

    def text_partial(c, q):
        these = pl.ds(at(c, 0), 6 * sub)
        columns = pl.ds(q * row_texts, row_texts)
        term = lax.dot_general(
            wt[these, columns], images[these, :], (((0,), (0,)), ((), ())), preferred_element_type=jnp.float32
        )
        if c == 0:
            tg[columns, :] = term
        else:
            tg[columns, :] += term

    def gradient(c, k):
        return ig[pl.ds(at(c, k), sub), :]

    def begin_back(c):
        over_s[c] = gradient(c, OVER).astype(jnp.bfloat16)
        start(b4[c])

    def middle_back(c):
        for h in range(2):
            b4[c][h].wait_recv()
            k = (UP3, DOWN3)[h]
            came = pl.ds(at(c, k, h), half)
            kept = pl.ds(at(c, k, 1 - h), half)
            three_s[c, h, halves(h), :] = (ig[came, :] + over_r[c, halves(h), :].astype(jnp.float32)).astype(jnp.bfloat16)
            three_s[c, h, halves(1 - h), :] = ig[kept, :].astype(jnp.bfloat16)
            b3[c][h].start()

    def end_back(c):
        for h in range(2):
            b3[c][h].wait_recv()
            one_s[c, h] = (gradient(c, (UP1, DOWN1)[h]) + three_r[c, h].astype(jnp.float32)).astype(jnp.bfloat16)
            b1[c][h].start()

    def loss_of(k):
        block = jnp.concatenate([loss_acc[pl.ds(at(c, k), sub), :] for c in range(CHUNKS)], axis=0)
        return jnp.sum(block.T, axis=0, keepdims=True)

    def give_loss(dst, row):
        dst[...] = jnp.broadcast_to(row, dst.shape)

    def partial(j, where):
        return tg[pl.ds(j * rows + where.start, where.size), :] + sib_r[j, where, :].astype(jnp.float32)

    def text_begin(p):
        arrive([back[p][FAR]])
        for s in range(2):
            far_s[edges(p, s), :] = partial(FAR, edges(p, s)).astype(jnp.bfloat16)
            t2[p][s].start()

    def text_middle(p):
        for s in range(2):
            j = (PREV, NEXT)[s]
            arrive([back[p][j]])
            row_s[s, edges(p, 1 - s), :] = partial(j, edges(p, 1 - s)).astype(jnp.bfloat16)
            t2[p][s].wait_recv()
            total = partial(j, edges(p, s)) + far_r[edges(p, s), :].astype(jnp.float32)
            row_s[s, edges(p, s), :] = total.astype(jnp.bfloat16)
            t1[p][s].start()

    for c in range(CHUNKS):
        start(z1[c])
    for p in range(PARTS):
        start(x1[p])
    across[OWN].start()
    pass_on(z1[0], z3[0])
    for p in range(PARTS):
        pass_on(x1[p], x2[p])
    across[PREV].start()
    across[NEXT].start()
    pass_on(z1[1], z3[1])
    for p in range(PARTS):
        arrive(x2[p])
    across[FAR].start()
    arrive(across)
    weigh(at(0, OWN), 3 * sub, 0, True)
    pass_on(z3[0], z4[0])
    weigh(at(0, UP3), 2 * sub, 0, False)
    weigh(at(1, OWN), 3 * sub, 1, True)
    arrive(z4[0])
    weigh(at(0, OVER), sub, 0, False)
    begin_back(0)
    pass_on(z3[1], z4[1])
    weigh(at(1, UP3), 2 * sub, 1, False)
    middle_back(0)
    for q in (1, 0):
        text_partial(0, q)
    arrive(z4[1])
    weigh(at(1, OVER), sub, 1, False)
    begin_back(1)

    end_back(0)
    text_partial(1, 1)
    for p in range(PARTS):
        for j in (FAR, PREV, NEXT, OWN):
            sib_s[j, parts(p), :] = tg[pl.ds(row_texts + j * rows + p * part, part), :].astype(jnp.bfloat16)
            back[p][j].start()
    give_loss(over_ls, loss_of(OVER))
    start(l4)
    middle_back(1)
    text_partial(1, 0)
    for p in range(PARTS):
        text_begin(p)
    lane = lax.broadcasted_iota(jnp.int32, (1, rows), 1)
    for h in range(2):
        l4[h].wait_recv()
        mine = (lane // half) % 2 == h
        give_loss(three_ls.at[h], loss_of((UP3, DOWN3)[h]) + jnp.where(mine, over_lr[h, pl.ds(0, 1), :], 0.0))
        l3[h].start()
    end_back(1)
    for p in range(PARTS):
        text_middle(p)
    for h in range(2):
        l3[h].wait_recv()
        give_loss(one_ls.at[h], loss_of((UP1, DOWN1)[h]) + three_lr[h, pl.ds(0, 1), :])
        l1[h].start()

    scale_row = jnp.exp(jnp.full((1, width), ls_ref[0], jnp.float32))

    def backprop(raw, grads):
        unit, inverse = unit_of(raw)
        grads = scale_row * grads
        return (grads - unit * jnp.sum(unit * grads, axis=1, keepdims=True)) * inverse

    def finish_image(c):
        here = pl.ds(c * sub, sub)
        arrive(b1[c])
        grads = gradient(c, OWN) + (one_r[c, 0].astype(jnp.float32) + one_r[c, 1].astype(jnp.float32))
        gi_ref[here, :] = backprop(img_ref[here, :], grads)

    def finish_text(p):
        here = parts(p)
        arrive([back[p][OWN]])
        arrive(t1[p])
        grads = partial(OWN, here) + (row_r[0, here, :].astype(jnp.float32) + row_r[1, here, :].astype(jnp.float32))
        gt_ref[here, :] = backprop(txt_ref[here, :], grads)

    finish_image(0)
    for p in range(PARTS):
        finish_text(p)
    arrive(l1)
    loss_ref[...] = loss_of(OWN) + one_lr[0, pl.ds(0, 1), :] + one_lr[1, pl.ds(0, 1), :]
    finish_image(1)
    for sent in messages:
        sent.wait_send()


N_MESSAGES = 58


def per_device(groups, image_emb, text_emb, log_scale, bias):
    rows, width = image_emb.shape
    sub = rows // CHUNKS
    half_type, full = jnp.bfloat16, jnp.float32
    vmem = pl.BlockSpec(memory_space=pltpu.VMEM)
    smem = pl.BlockSpec(memory_space=pltpu.SMEM)
    loss, grad_image, grad_text = pl.pallas_call(
        lambda *refs: kernel(groups, *refs),
        out_shape=(
            jax.ShapeDtypeStruct((1, rows), full),
            jax.ShapeDtypeStruct((rows, width), full),
            jax.ShapeDtypeStruct((rows, width), full),
        ),
        in_specs=[smem, smem, vmem, vmem],
        out_specs=(vmem, vmem, vmem),
        scratch_shapes=[
            pltpu.VMEM((8 * rows, width), half_type),
            pltpu.VMEM((6 * rows, width), half_type),
            pltpu.VMEM((6 * rows, 8 * rows), half_type),
            pltpu.VMEM((8 * rows, width), full),
            pltpu.VMEM((6 * rows, width), full),
            pltpu.VMEM((6 * rows, rows), full),
            pltpu.VMEM((CHUNKS, sub, width), half_type),
            pltpu.VMEM((CHUNKS, sub, width), half_type),
            pltpu.VMEM((CHUNKS, 2, sub, width), half_type),
            pltpu.VMEM((CHUNKS, 2, sub, width), half_type),
            pltpu.VMEM((CHUNKS, 2, sub, width), half_type),
            pltpu.VMEM((CHUNKS, 2, sub, width), half_type),
            pltpu.VMEM((4, rows, width), half_type),
            pltpu.VMEM((4, rows, width), half_type),
            pltpu.VMEM((rows, width), half_type),
            pltpu.VMEM((rows, width), half_type),
            pltpu.VMEM((2, rows, width), half_type),
            pltpu.VMEM((2, rows, width), half_type),
            pltpu.VMEM((8, rows), full),
            pltpu.VMEM((2, 8, rows), full),
            pltpu.VMEM((2, 8, rows), full),
            pltpu.VMEM((2, 8, rows), full),
            pltpu.VMEM((2, 8, rows), full),
            pltpu.VMEM((2, 8, rows), full),
            pltpu.SemaphoreType.DMA((N_MESSAGES,)),
            pltpu.SemaphoreType.DMA((N_MESSAGES,)),
        ],
        compiler_params=pltpu.CompilerParams(
            collective_id=0, has_side_effects=True, vmem_limit_bytes=48 * 1024 * 1024
        ),
    )(log_scale, bias, image_emb, text_emb)
    return (loss.reshape(rows), grad_image, grad_text)


def solution(mesh):
    groups = mesh.shape["outer"]
    in_specs = (P(("outer", "inner"), None), P(("outer", "inner"), None), P(), P())
    out_specs = (P(("outer", "inner")), P(("outer", "inner"), None), P(("outer", "inner"), None))
    return jax.shard_map(
        lambda *args: per_device(groups, *args),
        mesh=mesh, in_specs=in_specs, out_specs=out_specs, check_vma=False,
    )
```

```python
import jax
import jax.numpy as jnp
from jax import lax
from jax.experimental import pallas as pl
from jax.experimental.pallas import tpu as pltpu
from jax.sharding import PartitionSpec as P

MESH = pl.DeviceIdType.MESH
EPS = 1e-06
LOG2_E = 1.4426950408889634

X_N = 4
Z_LO = 4
Z_N = 8

OWN, FAR, PREV, NEXT = 0, 1, 2, 3
UP1, DOWN1, UP3, DOWN3, OVER = 1, 2, 3, 4, 5

CHUNKS = 2
PARTS = 1


def unit_of(raw):
    wide = raw.astype(jnp.float32)
    inverse = lax.rsqrt(jnp.sum(wide * wide, axis=1, keepdims=True) + EPS)
    return wide * inverse, inverse


def places(groups):
    outer = lax.axis_index("outer")
    inner = lax.axis_index("inner")
    z_lo = outer % Z_LO
    x, z_hi, core = inner // 4, (inner // 2) % 2, inner % 2

    def inner_of(x, z_hi, core):
        return x * 4 + z_hi * 2 + core

    def group_by(by):
        z = (z_hi * Z_LO + z_lo + by + Z_N) % Z_N
        step = by if by in (1, -1) else -by
        return ((outer + step + groups) % groups, inner_of(x, z // Z_LO, core))

    return {
        "xn": (outer, inner_of((x + 1) % X_N, z_hi, core)),
        "xp": (outer, inner_of((x + X_N - 1) % X_N, z_hi, core)),
        "sib": (outer, inner_of(x, z_hi, 1 - core)),
        "gn": group_by(1),
        "gp": group_by(-1),
        "tn": group_by(2),
        "tp": group_by(-2),
    }


def kernel(
    groups, ls_ref, b_ref, img_ref, txt_ref, loss_ref, gi_ref, gt_ref,
    texts, images, wt, tg, ig, loss_acc, over_s, over_r, three_s, three_r, one_s, one_r,
    sib_s, sib_r, far_s, far_r, row_s, row_r, over_ls, over_lr, three_ls, three_lr, one_ls, one_lr, ssem, rsem,
):
    rows, width = img_ref.shape
    sub = rows // CHUNKS
    half = sub // 2
    part = rows // PARTS
    edge = part // 2
    tile = 2 * rows
    row_texts = 4 * rows
    peers = places(groups)
    messages = []

    def message(src, dst, peer):
        index = len(messages)
        messages.append(
            pltpu.make_async_remote_copy(
                src_ref=src, dst_ref=dst, send_sem=ssem.at[index], recv_sem=rsem.at[index],
                device_id=peers[peer], device_id_type=MESH,
            )
        )
        return messages[-1]

    def at(c, k, h=0):
        return (c * 3 + k % 3) * sub + (k // 3) * 3 * rows + h * half

    def image(c, k):
        return images.at[pl.ds(at(c, k), sub), :]

    def image_half(c, k, h):
        return images.at[pl.ds(at(c, k, h), half), :]

    def text(q, j):
        return texts.at[pl.ds((q * 4 + j) * rows, rows), :]

    def text_part(j, p):
        return texts.at[pl.ds(j * rows + p * part, part), :]

    def text_edge(j, p, e):
        return texts.at[pl.ds(j * rows + p * part + e * edge, edge), :]

    def halves(h):
        return pl.ds(h * half, half)

    def parts(p):
        return pl.ds(p * part, part)

    def edges(p, e):
        return pl.ds(p * part + e * edge, edge)

    z1 = [[message(image(c, OWN), image(c, UP1), "gn"), message(image(c, OWN), image(c, DOWN1), "gp")] for c in range(CHUNKS)]
    z3 = [[message(image(c, UP1), image(c, UP3), "tn"), message(image(c, DOWN1), image(c, DOWN3), "tp")] for c in range(CHUNKS)]
    z4 = [
        [message(image_half(c, UP3, 0), image_half(c, OVER, 0), "gn"), message(image_half(c, DOWN3, 1), image_half(c, OVER, 1), "gp")]
        for c in range(CHUNKS)
    ]
    x1 = [[message(text_part(OWN, p), text_part((PREV, NEXT)[s], p), ("xn", "xp")[s]) for s in range(2)] for p in range(PARTS)]
    x2 = [
        [message(text_edge((PREV, NEXT)[s], p, s), text_edge(FAR, p, s), ("xn", "xp")[s]) for s in range(2)]
        for p in range(PARTS)
    ]
    across = [message(text(0, j), text(1, j), "sib") for j in range(4)]
    b4 = [[message(over_s.at[c, halves(h), :], over_r.at[c, halves(h), :], ("gp", "gn")[h]) for h in range(2)] for c in range(CHUNKS)]
    b3 = [[message(three_s.at[c, h], three_r.at[c, h], ("tp", "tn")[h]) for h in range(2)] for c in range(CHUNKS)]
    b1 = [[message(one_s.at[c, h], one_r.at[c, h], ("gp", "gn")[h]) for h in range(2)] for c in range(CHUNKS)]
    back = [[message(sib_s.at[j, parts(p), :], sib_r.at[j, parts(p), :], "sib") for j in range(4)] for p in range(PARTS)]
    t2 = [[message(far_s.at[edges(p, s), :], far_r.at[edges(p, s), :], ("xp", "xn")[s]) for s in range(2)] for p in range(PARTS)]
    t1 = [[message(row_s.at[s, parts(p), :], row_r.at[s, parts(p), :], ("xp", "xn")[s]) for s in range(2)] for p in range(PARTS)]
    l4 = [message(over_ls, over_lr.at[h], ("gp", "gn")[h]) for h in range(2)]
    l3 = [message(three_ls.at[h], three_lr.at[h], ("tp", "tn")[h]) for h in range(2)]
    l1 = [message(one_ls.at[h], one_lr.at[h], ("gp", "gn")[h]) for h in range(2)]

    def start(copies):
        for copy in copies:
            copy.start()

    def arrive(copies):
        for copy in copies:
            copy.wait_recv()

    def pass_on(arrivals, onward):
        for here, there in zip(arrivals, onward):
            here.wait_recv()
            there.start()

    barrier = pltpu.get_barrier_semaphore()
    for peer in peers.values():
        pl.semaphore_signal(barrier, inc=1, device_id=peer, device_id_type=MESH)
    own = unit_of(img_ref[...])[0].astype(jnp.bfloat16)
    for c in range(CHUNKS):
        images[pl.ds(at(c, OWN), sub), :] = own[c * sub:(c + 1) * sub]
    texts[pl.ds(0, rows), :] = unit_of(txt_ref[...])[0].astype(jnp.bfloat16)
    scale = jnp.exp(jnp.full((1, tile), ls_ref[0], jnp.float32)) * LOG2_E
    offset = b_ref[0] * LOG2_E
    pl.semaphore_wait(barrier, len(peers))

    def weigh(begin, size, n, diagonal):
        here = pl.ds(begin, size)
        columns = pl.ds(n * tile, tile)
        dots = lax.dot_general(
            images[here, :], texts[columns, :], (((1,), (1,)), ((), ())), preferred_element_type=jnp.float32
        )
        grown = jnp.exp2(scale * dots + offset)
        whole = 1.0 + grown
        inverse = pl.reciprocal(whole, approx=True)
        weights = grown * (inverse * (2.0 - whole * inverse))
        if diagonal:
            row = lax.broadcasted_iota(jnp.int32, (size, tile), 0)
            column = lax.broadcasted_iota(jnp.int32, (size, tile), 1)
            positive = row < 0
            for c in range(CHUNKS):
                first = at(c, OWN)
                positive |= (row - first == column - c * sub) & (row >= first) & (row < first + sub)
            weights = weights - positive.astype(jnp.float32)
            whole = jnp.where(positive, 1.0 + 1.0 / grown, whole)
        wt[here, columns] = weights.astype(jnp.bfloat16)
        return whole

    def loss_part(begin, size, wholes):
        here = pl.ds(begin, size)
        logs = jnp.log((wholes[0] * wholes[1]) * (wholes[2] * wholes[3]))
        loss_acc[here, :] = logs[:, :rows] + logs[:, rows:]

    def image_partial(begin, size):
        here = pl.ds(begin, size)
        ig[here, :] = jnp.dot(wt[here, :], texts[...], preferred_element_type=jnp.float32)

    def far(c):
        begin, size = at(c, UP3), 3 * sub
        loss_part(begin, size, [weigh(begin, size, n, False) for n in range(4)])
        image_partial(begin, size)

    def text_partial(far_ones, q):
        these = pl.ds(far_ones * 3 * rows, 3 * rows)
        columns = pl.ds(q * row_texts, row_texts)
        term = lax.dot_general(
            wt[these, columns], images[these, :], (((0,), (0,)), ((), ())), preferred_element_type=jnp.float32
        )
        if far_ones:
            tg[columns, :] += term
        else:
            tg[columns, :] = term

    def gradient(c, k):
        return ig[pl.ds(at(c, k), sub), :]

    def begin_back(c):
        over_s[c] = gradient(c, OVER).astype(jnp.bfloat16)
        start(b4[c])

    def middle_back(c):
        for h in range(2):
            b4[c][h].wait_recv()
            k = (UP3, DOWN3)[h]
            came = pl.ds(at(c, k, h), half)
            kept = pl.ds(at(c, k, 1 - h), half)
            three_s[c, h, halves(h), :] = (ig[came, :] + over_r[c, halves(h), :].astype(jnp.float32)).astype(jnp.bfloat16)
            three_s[c, h, halves(1 - h), :] = ig[kept, :].astype(jnp.bfloat16)
            b3[c][h].start()

    def end_back(c):
        for h in range(2):
            b3[c][h].wait_recv()
            one_s[c, h] = (gradient(c, (UP1, DOWN1)[h]) + three_r[c, h].astype(jnp.float32)).astype(jnp.bfloat16)
            b1[c][h].start()

    def loss_of(k):
        block = jnp.concatenate([loss_acc[pl.ds(at(c, k), sub), :] for c in range(CHUNKS)], axis=0)
        return jnp.sum(block.T, axis=0, keepdims=True)

    def give_loss(dst, row):
        dst[...] = jnp.broadcast_to(row, dst.shape)

    def partial(j, where):
        return tg[pl.ds(j * rows + where.start, where.size), :] + sib_r[j, where, :].astype(jnp.float32)

    def text_begin(p):
        arrive([back[p][FAR]])
        for s in range(2):
            far_s[edges(p, s), :] = partial(FAR, edges(p, s)).astype(jnp.bfloat16)
            t2[p][s].start()

    def text_middle(p):
        for s in range(2):
            j = (PREV, NEXT)[s]
            arrive([back[p][j]])
            row_s[s, edges(p, 1 - s), :] = partial(j, edges(p, 1 - s)).astype(jnp.bfloat16)
            t2[p][s].wait_recv()
            total = partial(j, edges(p, s)) + far_r[edges(p, s), :].astype(jnp.float32)
            row_s[s, edges(p, s), :] = total.astype(jnp.bfloat16)
            t1[p][s].start()

    for c in range(CHUNKS):
        start(z1[c])
    for p in range(PARTS):
        start(x1[p])
    across[OWN].start()
    pass_on(z1[0], z3[0])
    for p in range(PARTS):
        pass_on(x1[p], x2[p])
    across[PREV].start()
    across[NEXT].start()
    pass_on(z1[1], z3[1])
    wholes = [weigh(0, 3 * rows, 1, False)]
    arrive([across[PREV], across[NEXT]])
    wholes.append(weigh(0, 3 * rows, 3, False))
    for p in range(PARTS):
        arrive(x2[p])
    across[FAR].start()
    wholes.append(weigh(0, 3 * rows, 0, True))
    arrive([across[OWN], across[FAR]])
    wholes.append(weigh(0, 3 * rows, 2, False))
    loss_part(0, 3 * rows, wholes)
    pass_on(z3[0], z4[0])
    image_partial(0, 3 * rows)
    pass_on(z3[1], z4[1])
    for q in (1, 0):
        text_partial(0, q)
    for c in range(CHUNKS):
        arrive(z4[c])
        far(c)
        begin_back(c)

    middle_back(0)
    text_partial(1, 1)
    for p in range(PARTS):
        for j in (FAR, PREV, NEXT, OWN):
            sib_s[j, parts(p), :] = tg[pl.ds(row_texts + j * rows + p * part, part), :].astype(jnp.bfloat16)
            back[p][j].start()
    middle_back(1)
    give_loss(over_ls, loss_of(OVER))
    start(l4)
    text_partial(1, 0)
    for p in range(PARTS):
        text_begin(p)
    end_back(0)
    lane = lax.broadcasted_iota(jnp.int32, (1, rows), 1)
    for h in range(2):
        l4[h].wait_recv()
        mine = (lane // half) % 2 == h
        give_loss(three_ls.at[h], loss_of((UP3, DOWN3)[h]) + jnp.where(mine, over_lr[h, pl.ds(0, 1), :], 0.0))
        l3[h].start()
    for p in range(PARTS):
        text_middle(p)
    end_back(1)
    for h in range(2):
        l3[h].wait_recv()
        give_loss(one_ls.at[h], loss_of((UP1, DOWN1)[h]) + three_lr[h, pl.ds(0, 1), :])
        l1[h].start()

    scale_row = jnp.exp(jnp.full((1, width), ls_ref[0], jnp.float32))

    def backprop(raw, grads):
        unit, inverse = unit_of(raw)
        grads = scale_row * grads
        return (grads - unit * jnp.sum(unit * grads, axis=1, keepdims=True)) * inverse

    def finish_image(c):
        here = pl.ds(c * sub, sub)
        arrive(b1[c])
        grads = gradient(c, OWN) + (one_r[c, 0].astype(jnp.float32) + one_r[c, 1].astype(jnp.float32))
        gi_ref[here, :] = backprop(img_ref[here, :], grads)

    def finish_text(p):
        here = parts(p)
        arrive([back[p][OWN]])
        arrive(t1[p])
        grads = partial(OWN, here) + (row_r[0, here, :].astype(jnp.float32) + row_r[1, here, :].astype(jnp.float32))
        gt_ref[here, :] = backprop(txt_ref[here, :], grads)

    for p in range(PARTS):
        finish_text(p)
    finish_image(0)
    arrive(l1)
    loss_ref[...] = loss_of(OWN) + one_lr[0, pl.ds(0, 1), :] + one_lr[1, pl.ds(0, 1), :]
    finish_image(1)
    for sent in messages:
        sent.wait_send()


N_MESSAGES = 46


def per_device(groups, image_emb, text_emb, log_scale, bias):
    rows, width = image_emb.shape
    sub = rows // CHUNKS
    half_type, full = jnp.bfloat16, jnp.float32
    vmem = pl.BlockSpec(memory_space=pltpu.VMEM)
    smem = pl.BlockSpec(memory_space=pltpu.SMEM)
    loss, grad_image, grad_text = pl.pallas_call(
        lambda *refs: kernel(groups, *refs),
        out_shape=(
            jax.ShapeDtypeStruct((1, rows), full),
            jax.ShapeDtypeStruct((rows, width), full),
            jax.ShapeDtypeStruct((rows, width), full),
        ),
        in_specs=[smem, smem, vmem, vmem],
        out_specs=(vmem, vmem, vmem),
        scratch_shapes=[
            pltpu.VMEM((8 * rows, width), half_type),
            pltpu.VMEM((6 * rows, width), half_type),
            pltpu.VMEM((6 * rows, 8 * rows), half_type),
            pltpu.VMEM((8 * rows, width), full),
            pltpu.VMEM((6 * rows, width), full),
            pltpu.VMEM((6 * rows, rows), full),
            pltpu.VMEM((CHUNKS, sub, width), half_type),
            pltpu.VMEM((CHUNKS, sub, width), half_type),
            pltpu.VMEM((CHUNKS, 2, sub, width), half_type),
            pltpu.VMEM((CHUNKS, 2, sub, width), half_type),
            pltpu.VMEM((CHUNKS, 2, sub, width), half_type),
            pltpu.VMEM((CHUNKS, 2, sub, width), half_type),
            pltpu.VMEM((4, rows, width), half_type),
            pltpu.VMEM((4, rows, width), half_type),
            pltpu.VMEM((rows, width), half_type),
            pltpu.VMEM((rows, width), half_type),
            pltpu.VMEM((2, rows, width), half_type),
            pltpu.VMEM((2, rows, width), half_type),
            pltpu.VMEM((8, rows), full),
            pltpu.VMEM((2, 8, rows), full),
            pltpu.VMEM((2, 8, rows), full),
            pltpu.VMEM((2, 8, rows), full),
            pltpu.VMEM((2, 8, rows), full),
            pltpu.VMEM((2, 8, rows), full),
            pltpu.SemaphoreType.DMA((N_MESSAGES,)),
            pltpu.SemaphoreType.DMA((N_MESSAGES,)),
        ],
        compiler_params=pltpu.CompilerParams(
            collective_id=0, has_side_effects=True, vmem_limit_bytes=48 * 1024 * 1024
        ),
    )(log_scale, bias, image_emb, text_emb)
    return (loss.reshape(rows), grad_image, grad_text)


def solution(mesh):
    groups = mesh.shape["outer"]
    in_specs = (P(("outer", "inner"), None), P(("outer", "inner"), None), P(), P())
    out_specs = (P(("outer", "inner")), P(("outer", "inner"), None), P(("outer", "inner"), None))
    return jax.shard_map(
        lambda *args: per_device(groups, *args),
        mesh=mesh, in_specs=in_specs, out_specs=out_specs, check_vma=False,
    )
```

```python
import jax
import jax.numpy as jnp
from jax import lax
from jax.experimental import pallas as pl
from jax.experimental.pallas import tpu as pltpu
from jax.sharding import PartitionSpec as P

MESH = pl.DeviceIdType.MESH
EPS = 1e-06
LOG2_E = 1.4426950408889634

X_N = 4
Z_LO = 4
Z_N = 8

OWN, FAR, PREV, NEXT = 0, 1, 2, 3

CHUNKS = 2


def unit_of(raw):
    wide = raw.astype(jnp.float32)
    inverse = lax.rsqrt(jnp.sum(wide * wide, axis=1, keepdims=True) + EPS)
    return wide * inverse, inverse


def places(groups):
    outer = lax.axis_index("outer")
    inner = lax.axis_index("inner")
    y, z_lo = outer // Z_LO, outer % Z_LO
    x, z_hi, core = inner // 4, (inner // 2) % 2, inner % 2

    def inner_of(x, z_hi, core):
        return x * 4 + z_hi * 2 + core

    def along_z(by):
        z = (z_hi * Z_LO + z_lo + by + Z_N) % Z_N
        return (y * Z_LO + z % Z_LO, inner_of(x, z // Z_LO, core))

    last = (z_lo == Z_LO - 1).astype(jnp.int32)
    first = (z_lo == 0).astype(jnp.int32)
    return {
        "xn": (outer, inner_of((x + 1) % X_N, z_hi, core)),
        "xp": (outer, inner_of((x + X_N - 1) % X_N, z_hi, core)),
        "zn": along_z(2),
        "zp": along_z(-2),
        "sib": (outer, inner_of(x, z_hi, 1 - core)),
        "gn": ((outer + 1) % groups, inner_of(x, (z_hi + last) % 2, core)),
        "gp": ((outer + groups - 1) % groups, inner_of(x, (z_hi + first) % 2, core)),
    }


def kernel(
    groups, ls_ref, b_ref, img_hbm, txt_hbm, loss_hbm, gi_hbm, gt_hbm,
    img_ref, txt_ref, loss_ref, gi_ref, gt_ref, texts, images, wt, tg, ig, loss_acc, relay, far_s, far_r, row_s, row_r, col_s, back, col_r,
    sib_s, sib_r, sib_ls, sib_lr, ret_s, ret_r, ret_ls, ret_lr, ssem, rsem, io_sem,
):
    rows, width = img_ref.shape
    sub = rows // CHUNKS
    half = sub // 2
    pair = 2 * rows
    unit = 4 * sub
    peers = places(groups)
    messages = []

    def message(src, dst, peer):
        index = len(messages)
        messages.append(
            pltpu.make_async_remote_copy(
                src_ref=src, dst_ref=dst, send_sem=ssem.at[index], recv_sem=rsem.at[index],
                device_id=peers[peer], device_id_type=MESH,
            )
        )
        return messages[-1]

    def base(r, c):
        return (r * CHUNKS + c) * unit

    def text(r, c, k, h):
        return texts.at[pl.ds(base(r, c) + k * sub + h * half, half), :]

    def piece(c, h):
        return pl.ds(c * sub + h * half, half)

    def image(k):
        return images.at[pl.ds(k * rows, rows), :]

    def each(make):
        return [[make(c, h) for h in range(2)] for c in range(CHUNKS)]

    def each_row(make):
        return [each(lambda c, h: make(r, c, h)) for r in range(2)]

    z_out = each(lambda c, h: message(text(0, c, OWN, h), relay.at[piece(c, h), :], ("zn", "zp")[h]))
    z_on = each(lambda c, h: message(relay.at[piece(c, h), :], text(1, c, OWN, h), ("zn", "zp")[h]))
    to_next = each_row(lambda r, c, h: message(text(r, c, OWN, h), text(r, c, PREV, h), "xn"))
    to_prev = each_row(lambda r, c, h: message(text(r, c, OWN, h), text(r, c, NEXT, h), "xp"))
    far_on = each_row(lambda r, c, h: message(text(r, c, (PREV, NEXT)[h], h), text(r, c, FAR, h), ("xn", "xp")[h]))
    img_next = message(image(0), image(1), "gn")
    img_prev = message(image(0), image(2), "gp")
    img_sib = [message(image(k), image(3 + k), "sib") for k in range(3)]
    far_back = each_row(lambda r, c, h: message(far_s.at[r, piece(c, h), :], far_r.at[r, piece(c, h), :], ("xp", "xn")[h]))
    row_back = [
        each_row(lambda r, c, h: message(row_s.at[r, s, piece(c, h), :], row_r.at[r, s, piece(c, h), :], ("xp", "xn")[s]))
        for s in range(2)
    ]
    z_back = each(lambda c, h: message(col_s.at[piece(c, h), :], back.at[piece(c, h), :], ("zp", "zn")[h]))
    z_home = each(lambda c, h: message(back.at[piece(c, h), :], col_r.at[piece(c, h), :], ("zp", "zn")[h]))
    sib_back = [message(sib_s.at[k], sib_r.at[k], "sib") for k in range(3)]
    sib_loss = message(sib_ls, sib_lr, "sib")
    ret = [message(ret_s.at[0], ret_r.at[1], "gp"), message(ret_s.at[1], ret_r.at[0], "gn")]
    ret_loss = [message(ret_ls.at[0], ret_lr.at[1], "gp"), message(ret_ls.at[1], ret_lr.at[0], "gn")]

    def start(*pairs):
        for one in pairs:
            for copy in one:
                copy.start()

    fetch = [pltpu.make_async_copy(txt_hbm, txt_ref, io_sem.at[0]), pltpu.make_async_copy(img_hbm, img_ref, io_sem.at[1])]
    start(fetch)
    barrier = pltpu.get_barrier_semaphore()
    for peer in peers.values():
        pl.semaphore_signal(barrier, inc=1, device_id=peer, device_id_type=MESH)

    fetch[0].wait()
    own = unit_of(txt_ref[...])[0].astype(jnp.bfloat16)
    for c in range(CHUNKS):
        texts[pl.ds(base(0, c), sub), :] = own[c * sub:(c + 1) * sub]
    fetch[1].wait()
    images[pl.ds(0, rows), :] = unit_of(img_ref[...])[0].astype(jnp.bfloat16)
    loss_acc[...] = jnp.zeros_like(loss_acc)
    scale = jnp.exp(jnp.full((1, pair), ls_ref[0], jnp.float32)) * LOG2_E
    offset = b_ref[0] * LOG2_E
    pl.semaphore_wait(barrier, len(peers))

    def arrive(*pairs):
        for one in pairs:
            for copy in one:
                copy.wait_recv()

    def weigh(c, start, j, diagonal):
        columns = pl.ds(j * pair, pair)
        dots = lax.dot_general(
            texts[pl.ds(start, unit), :], images[columns, :], (((1,), (1,)), ((), ())),
            preferred_element_type=jnp.float32,
        )
        grown = jnp.exp2(scale * dots + offset)
        whole = 1.0 + grown
        inverse = pl.reciprocal(whole, approx=True)
        weights = grown * (inverse * (2.0 - whole * inverse))
        if diagonal:
            row = lax.broadcasted_iota(jnp.int32, (unit, pair), 0)
            column = lax.broadcasted_iota(jnp.int32, (unit, pair), 1)
            positive = (row + c * sub == column) & (row < sub)
            weights = weights - positive.astype(jnp.float32)
            whole = jnp.where(positive, 1.0 + 1.0 / grown, whole)
        wt[pl.ds(start, unit), columns] = weights.astype(jnp.bfloat16)
        q = unit // 4
        product = (whole[:q] * whole[q:2 * q]) * (whole[2 * q:3 * q] * whole[3 * q:])
        loss_acc[j] += jnp.sum(jnp.log(product).reshape(q // 8, 8, pair), axis=0)

    def both(r, c):
        begin = base(r, c)
        for j in range(3):
            weigh(c, begin, j, r == 0 and j == 0)
        tg[pl.ds(begin, unit), :] = jnp.dot(
            wt[pl.ds(begin, unit), :], images[...], preferred_element_type=jnp.float32
        )

    def image_partial(first):
        ig[pl.ds(first, 3 * rows), :] = lax.dot_general(
            wt[:, pl.ds(first, 3 * rows)], texts[...], (((0,), (0,)), ((), ())), preferred_element_type=jnp.float32
        )

    def partial(r, c, k, h):
        return tg[pl.ds(base(r, c) + k * sub + h * half, half), :]

    def reduce_begin(r, c):
        for h in range(2):
            far_s[r, piece(c, h), :] = partial(r, c, FAR, h).astype(jnp.bfloat16)
            far_back[r][c][h].start()
        for s in range(2):
            row_s[r, s, piece(c, 1 - s), :] = partial(r, c, (PREV, NEXT)[s], 1 - s).astype(jnp.bfloat16)
            row_back[s][r][c][1 - s].start()

    def reduce_middle(r, c):
        for s in range(2):
            far_back[r][c][s].wait_recv()
            total = partial(r, c, (PREV, NEXT)[s], s) + far_r[r, piece(c, s), :].astype(jnp.float32)
            row_s[r, s, piece(c, s), :] = total.astype(jnp.bfloat16)
            row_back[s][r][c][s].start()

    def reduce_end(r, c, h):
        row_back[0][r][c][h].wait_recv()
        row_back[1][r][c][h].wait_recv()
        return (
            partial(r, c, OWN, h)
            + row_r[r, 0, piece(c, h), :].astype(jnp.float32)
            + row_r[r, 1, piece(c, h), :].astype(jnp.float32)
        )

    def column_home(c):
        for h in range(2):
            col_s[piece(c, h), :] = reduce_end(1, c, h).astype(jnp.bfloat16)
            z_back[c][h].start()

    def loss_of(k):
        block = loss_acc[k // 2]
        return jnp.sum(block[:, (k % 2) * rows:(k % 2 + 1) * rows], axis=0, keepdims=True)

    def far_forward(r, c):
        to_next[r][c][0].wait_recv()
        far_on[r][c][0].start()
        to_prev[r][c][1].wait_recv()
        far_on[r][c][1].start()

    def all_here(r, c):
        to_next[r][c][1].wait_recv()
        to_prev[r][c][0].wait_recv()
        arrive(far_on[r][c])

    def row_out(r, c):
        for h in range(2):
            to_next[r][c][h].start()
            to_prev[r][c][1 - h].start()

    start(z_out[0])
    img_next.start()
    img_prev.start()
    row_out(0, 0)
    img_sib[0].start()
    row_out(0, 1)
    for h in range(2):
        z_out[0][h].wait_recv()
        z_on[0][h].start()
    far_forward(0, 0)
    img_next.wait_recv()
    img_sib[1].start()
    img_prev.wait_recv()
    img_sib[2].start()
    start(z_out[1])
    far_forward(0, 1)
    arrive(z_on[0])
    row_out(1, 0)
    arrive(img_sib)
    all_here(0, 0)
    both(0, 0)
    for h in range(2):
        z_out[1][h].wait_recv()
        z_on[1][h].start()
    reduce_begin(0, 0)
    far_forward(1, 0)
    all_here(0, 1)
    both(0, 1)
    arrive(z_on[1])
    row_out(1, 1)
    all_here(1, 0)
    both(1, 0)
    reduce_begin(1, 0)
    far_forward(1, 1)
    reduce_middle(1, 0)
    all_here(1, 1)
    both(1, 1)

    reduce_begin(1, 1)
    column_home(0)
    reduce_begin(0, 1)
    image_partial(3 * rows)
    for k in (1, 2, 0):
        sib_s[k] = ig[pl.ds((3 + k) * rows, rows), :].astype(jnp.bfloat16)
        sib_back[k].start()
    sib_ls[...] = jnp.zeros_like(sib_ls)
    for k in range(3):
        sib_ls[pl.ds(k, 1), :] = loss_of(3 + k)
    sib_loss.start()
    reduce_middle(1, 1)
    image_partial(0)
    for h in range(2):
        z_back[0][h].wait_recv()
        z_home[0][h].start()
    column_home(1)
    sib_loss.wait_recv()
    for s in range(2):
        sib_back[s + 1].wait_recv()
        ret_s[s] = (ig[pl.ds((s + 1) * rows, rows), :] + sib_r[s + 1].astype(jnp.float32)).astype(jnp.bfloat16)
        ret[s].start()
        ret_ls[s] = jnp.broadcast_to(loss_of(s + 1) + sib_lr[pl.ds(s + 1, 1), :], ret_ls.shape[1:])
        ret_loss[s].start()
    for c in range(CHUNKS):
        reduce_middle(0, c)
    for h in range(2):
        z_back[1][h].wait_recv()
        z_home[1][h].start()

    scale_row = jnp.exp(jnp.full((1, width), ls_ref[0], jnp.float32))

    def backprop(raw, grads):
        unit, inverse = unit_of(raw)
        grads = scale_row * grads
        return (grads - unit * jnp.sum(unit * grads, axis=1, keepdims=True)) * inverse

    put = [pltpu.make_async_copy(loss_ref, loss_hbm, io_sem.at[2])]
    for c in range(CHUNKS):
        here = pl.ds(c * sub, sub)
        put.append(pltpu.make_async_copy(gi_ref.at[here, :], gi_hbm.at[here, :], io_sem.at[3 + 2 * c]))
        put.append(pltpu.make_async_copy(gt_ref.at[here, :], gt_hbm.at[here, :], io_sem.at[4 + 2 * c]))

    def finish_text(c):
        for h in range(2):
            near = reduce_end(0, c, h)
            z_home[c][h].wait_recv()
            gt_ref[piece(c, h), :] = backprop(txt_ref[piece(c, h), :], near + col_r[piece(c, h), :].astype(jnp.float32))
        put[2 + 2 * c].start()

    finish_text(0)
    sib_back[0].wait_recv()
    for s in range(2):
        ret_loss[s].wait_recv()
        ret[s].wait_recv()
    loss_ref[...] = loss_of(0) + sib_lr[pl.ds(0, 1), :] + ret_lr[0, pl.ds(0, 1), :] + ret_lr[1, pl.ds(0, 1), :]
    put[0].start()
    for c in range(CHUNKS):
        for h in range(2):
            here = piece(c, h)
            grads = (
                (ig[here, :] + sib_r[0, here, :].astype(jnp.float32))
                + (ret_r[0, here, :].astype(jnp.float32) + ret_r[1, here, :].astype(jnp.float32))
            )
            gi_ref[here, :] = backprop(img_ref[here, :], grads)
        put[1 + 2 * c].start()
    finish_text(1)
    for sent in messages:
        sent.wait_send()
    for copy in put:
        copy.wait()


def write_out(*refs):
    sources, results, sem = refs[:3], refs[3:6], refs[6]
    copies = [pltpu.make_async_copy(src, dst, sem.at[n]) for n, (src, dst) in enumerate(zip(sources, results))]
    for copy in copies:
        copy.start()
    for copy in copies:
        copy.wait()


N_MESSAGES = 77


def per_device(groups, image_emb, text_emb, log_scale, bias):
    rows, width = image_emb.shape
    half_type, full = jnp.bfloat16, jnp.float32
    smem = pl.BlockSpec(memory_space=pltpu.SMEM)
    anywhere = pl.BlockSpec(memory_space=pl.ANY)
    out_shape = (
        jax.ShapeDtypeStruct((1, rows), full),
        jax.ShapeDtypeStruct((rows, width), full),
        jax.ShapeDtypeStruct((rows, width), full),
    )
    results = pl.pallas_call(
        lambda *refs: kernel(groups, *refs),
        out_shape=out_shape,
        in_specs=[smem, smem, anywhere, anywhere],
        out_specs=(anywhere,) * 3,
        scratch_shapes=[
            pltpu.VMEM((rows, width), half_type),
            pltpu.VMEM((rows, width), half_type),
            pltpu.VMEM((1, rows), full),
            pltpu.VMEM((rows, width), full),
            pltpu.VMEM((rows, width), full),
            pltpu.VMEM((8 * rows, width), half_type),
            pltpu.VMEM((6 * rows, width), half_type),
            pltpu.VMEM((8 * rows, 6 * rows), half_type),
            pltpu.VMEM((8 * rows, width), full),
            pltpu.VMEM((6 * rows, width), full),
            pltpu.VMEM((3, 8, 2 * rows), full),
            pltpu.VMEM((rows, width), half_type),
            pltpu.VMEM((2, rows, width), half_type),
            pltpu.VMEM((2, rows, width), half_type),
            pltpu.VMEM((2, 2, rows, width), half_type),
            pltpu.VMEM((2, 2, rows, width), half_type),
            pltpu.VMEM((rows, width), half_type),
            pltpu.VMEM((rows, width), half_type),
            pltpu.VMEM((rows, width), half_type),
            pltpu.VMEM((3, rows, width), half_type),
            pltpu.VMEM((3, rows, width), half_type),
            pltpu.VMEM((8, rows), full),
            pltpu.VMEM((8, rows), full),
            pltpu.VMEM((2, rows, width), half_type),
            pltpu.VMEM((2, rows, width), half_type),
            pltpu.VMEM((2, 8, rows), full),
            pltpu.VMEM((2, 8, rows), full),
            pltpu.SemaphoreType.DMA((N_MESSAGES,)),
            pltpu.SemaphoreType.DMA((N_MESSAGES,)),
            pltpu.SemaphoreType.DMA((3 + 2 * CHUNKS,)),
        ],
        compiler_params=pltpu.CompilerParams(
            collective_id=0, has_side_effects=True, vmem_limit_bytes=60 * 1024 * 1024
        ),
    )(log_scale, bias, image_emb, text_emb)
    loss, grad_image, grad_text = pl.pallas_call(
        write_out,
        out_shape=out_shape,
        in_specs=[anywhere] * 3,
        out_specs=(anywhere,) * 3,
        scratch_shapes=[pltpu.SemaphoreType.DMA((3,))],
        compiler_params=pltpu.CompilerParams(vmem_limit_bytes=60 * 1024 * 1024),
    )(*results)
    return (loss.reshape(rows), grad_image, grad_text)


def solution(mesh):
    groups = mesh.shape["outer"]
    in_specs = (P(("outer", "inner"), None), P(("outer", "inner"), None), P(), P())
    out_specs = (P(("outer", "inner")), P(("outer", "inner"), None), P(("outer", "inner"), None))
    return jax.shard_map(
        lambda *args: per_device(groups, *args),
        mesh=mesh, in_specs=in_specs, out_specs=out_specs, check_vma=False,
    )
```

```python
import jax
import jax.numpy as jnp
from jax import lax
from jax.experimental import pallas as pl
from jax.experimental.pallas import tpu as pltpu
from jax.sharding import PartitionSpec as P

MESH = pl.DeviceIdType.MESH
EPS = 1e-06
LOG2_E = 1.4426950408889634

X_N = 4
Z_LO = 4
Z_N = 8

OWN, FAR, PREV, NEXT = 0, 1, 2, 3
UP1, DOWN1, UP3, DOWN3, OVER = 1, 2, 3, 4, 5

CHUNKS = 2
PARTS = 1
SPLIT = 4
SMALLEST = 16


def unit_of(raw):
    wide = raw.astype(jnp.float32)
    inverse = lax.rsqrt(jnp.sum(wide * wide, axis=1, keepdims=True) + EPS)
    return wide * inverse, inverse


def places(groups):
    outer = lax.axis_index("outer")
    inner = lax.axis_index("inner")
    z_lo = outer % Z_LO
    x, z_hi, core = inner // 4, (inner // 2) % 2, inner % 2

    def inner_of(x, z_hi, core):
        return x * 4 + z_hi * 2 + core

    def group_by(by):
        z = (z_hi * Z_LO + z_lo + by + Z_N) % Z_N
        step = by if by in (1, -1) else -by
        return ((outer + step + groups) % groups, inner_of(x, z // Z_LO, core))

    return {
        "xn": (outer, inner_of((x + 1) % X_N, z_hi, core)),
        "xp": (outer, inner_of((x + X_N - 1) % X_N, z_hi, core)),
        "sib": (outer, inner_of(x, z_hi, 1 - core)),
        "gn": group_by(1),
        "gp": group_by(-1),
        "tn": group_by(2),
        "tp": group_by(-2),
    }


class Message:
    def __init__(self, src, dst, peer, ssem, rsem, first):
        n = src.shape[-2]
        count = max(1, min(SPLIT, n // SMALLEST))
        size = n // count
        self.copies = [
            pltpu.make_async_remote_copy(
                src_ref=src.at[pl.ds(i * size, size), :], dst_ref=dst.at[pl.ds(i * size, size), :],
                send_sem=ssem.at[first + i], recv_sem=rsem.at[first + i], device_id=peer, device_id_type=MESH,
            )
            for i in range(count)
        ]

    def start(self):
        for copy in self.copies:
            copy.start()

    def wait_recv(self):
        for copy in self.copies:
            copy.wait_recv()

    def wait_send(self):
        for copy in self.copies:
            copy.wait_send()


def kernel(
    groups, ls_ref, b_ref, img_ref, txt_ref, loss_ref, gi_ref, gt_ref,
    texts, images, wt, tg, ig, loss_acc, over_s, over_r, three_s, three_r, one_s, one_r,
    sib_s, sib_r, far_s, far_r, row_s, row_r, over_ls, over_lr, three_ls, three_lr, one_ls, one_lr, ssem, rsem,
):
    rows, width = img_ref.shape
    sub = rows // CHUNKS
    half = sub // 2
    part = rows // PARTS
    edge = part // 2
    tile = 2 * rows
    row_texts = 4 * rows
    peers = places(groups)
    messages = []

    def message(src, dst, peer):
        messages.append(Message(src, dst, peers[peer], ssem, rsem, sum(len(one.copies) for one in messages)))
        return messages[-1]

    def at(c, k, h=0):
        return (c * 3 + k % 3) * sub + (k // 3) * 3 * rows + h * half

    def image(c, k):
        return images.at[pl.ds(at(c, k), sub), :]

    def image_half(c, k, h):
        return images.at[pl.ds(at(c, k, h), half), :]

    def text(q, j):
        return texts.at[pl.ds((q * 4 + j) * rows, rows), :]

    def text_part(j, p):
        return texts.at[pl.ds(j * rows + p * part, part), :]

    def text_edge(j, p, e):
        return texts.at[pl.ds(j * rows + p * part + e * edge, edge), :]

    def halves(h):
        return pl.ds(h * half, half)

    def parts(p):
        return pl.ds(p * part, part)

    def edges(p, e):
        return pl.ds(p * part + e * edge, edge)

    z1 = [[message(image(c, OWN), image(c, UP1), "gn"), message(image(c, OWN), image(c, DOWN1), "gp")] for c in range(CHUNKS)]
    z3 = [[message(image(c, UP1), image(c, UP3), "tn"), message(image(c, DOWN1), image(c, DOWN3), "tp")] for c in range(CHUNKS)]
    z4 = [
        [message(image_half(c, UP3, 0), image_half(c, OVER, 0), "gn"), message(image_half(c, DOWN3, 1), image_half(c, OVER, 1), "gp")]
        for c in range(CHUNKS)
    ]
    x1 = [[message(text_part(OWN, p), text_part((PREV, NEXT)[s], p), ("xn", "xp")[s]) for s in range(2)] for p in range(PARTS)]
    x2 = [
        [message(text_edge((PREV, NEXT)[s], p, s), text_edge(FAR, p, s), ("xn", "xp")[s]) for s in range(2)]
        for p in range(PARTS)
    ]
    across = [message(text(0, j), text(1, j), "sib") for j in range(4)]
    b4 = [[message(over_s.at[c, halves(h), :], over_r.at[c, halves(h), :], ("gp", "gn")[h]) for h in range(2)] for c in range(CHUNKS)]
    b3 = [[message(three_s.at[c, h], three_r.at[c, h], ("tp", "tn")[h]) for h in range(2)] for c in range(CHUNKS)]
    b1 = [[message(one_s.at[c, h], one_r.at[c, h], ("gp", "gn")[h]) for h in range(2)] for c in range(CHUNKS)]
    back = [[message(sib_s.at[j, parts(p), :], sib_r.at[j, parts(p), :], "sib") for j in range(4)] for p in range(PARTS)]
    t2 = [[message(far_s.at[edges(p, s), :], far_r.at[edges(p, s), :], ("xp", "xn")[s]) for s in range(2)] for p in range(PARTS)]
    t1 = [[message(row_s.at[s, parts(p), :], row_r.at[s, parts(p), :], ("xp", "xn")[s]) for s in range(2)] for p in range(PARTS)]
    l4 = [message(over_ls, over_lr.at[h], ("gp", "gn")[h]) for h in range(2)]
    l3 = [message(three_ls.at[h], three_lr.at[h], ("tp", "tn")[h]) for h in range(2)]
    l1 = [message(one_ls.at[h], one_lr.at[h], ("gp", "gn")[h]) for h in range(2)]

    def start(copies):
        for copy in copies:
            copy.start()

    def arrive(copies):
        for copy in copies:
            copy.wait_recv()

    def pass_on(arrivals, onward):
        for here, there in zip(arrivals, onward):
            here.wait_recv()
            there.start()

    barrier = pltpu.get_barrier_semaphore()
    for peer in peers.values():
        pl.semaphore_signal(barrier, inc=1, device_id=peer, device_id_type=MESH)
    own = unit_of(img_ref[...])[0].astype(jnp.bfloat16)
    for c in range(CHUNKS):
        images[pl.ds(at(c, OWN), sub), :] = own[c * sub:(c + 1) * sub]
    texts[pl.ds(0, rows), :] = unit_of(txt_ref[...])[0].astype(jnp.bfloat16)
    scale = jnp.exp(jnp.full((1, tile), ls_ref[0], jnp.float32)) * LOG2_E
    offset = b_ref[0] * LOG2_E
    pl.semaphore_wait(barrier, len(peers))

    def weigh(begin, size, n, diagonal):
        here = pl.ds(begin, size)
        columns = pl.ds(n * tile, tile)
        dots = lax.dot_general(
            images[here, :], texts[columns, :], (((1,), (1,)), ((), ())), preferred_element_type=jnp.float32
        )
        grown = jnp.exp2(scale * dots + offset)
        whole = 1.0 + grown
        inverse = pl.reciprocal(whole, approx=True)
        weights = grown * (inverse * (2.0 - whole * inverse))
        if diagonal:
            row = lax.broadcasted_iota(jnp.int32, (size, tile), 0)
            column = lax.broadcasted_iota(jnp.int32, (size, tile), 1)
            positive = row < 0
            for c in range(CHUNKS):
                first = at(c, OWN)
                positive |= (row - first == column - c * sub) & (row >= first) & (row < first + sub)
            weights = weights - positive.astype(jnp.float32)
            whole = jnp.where(positive, 1.0 + 1.0 / grown, whole)
        wt[here, columns] = weights.astype(jnp.bfloat16)
        return whole

    def loss_part(begin, size, wholes):
        here = pl.ds(begin, size)
        logs = jnp.log((wholes[0] * wholes[1]) * (wholes[2] * wholes[3]))
        loss_acc[here, :] = logs[:, :rows] + logs[:, rows:]

    def image_partial(begin, size):
        here = pl.ds(begin, size)
        ig[here, :] = jnp.dot(wt[here, :], texts[...], preferred_element_type=jnp.float32)

    def far(c):
        begin, size = at(c, UP3), 3 * sub
        loss_part(begin, size, [weigh(begin, size, n, False) for n in range(4)])
        image_partial(begin, size)

    def text_partial(far_ones, q):
        these = pl.ds(far_ones * 3 * rows, 3 * rows)
        columns = pl.ds(q * row_texts, row_texts)
        term = lax.dot_general(
            wt[these, columns], images[these, :], (((0,), (0,)), ((), ())), preferred_element_type=jnp.float32
        )
        if far_ones:
            tg[columns, :] += term
        else:
            tg[columns, :] = term

    def gradient(c, k):
        return ig[pl.ds(at(c, k), sub), :]

    def begin_back(c):
        over_s[c] = gradient(c, OVER).astype(jnp.bfloat16)
        start(b4[c])

    def middle_back(c):
        for h in range(2):
            b4[c][h].wait_recv()
            k = (UP3, DOWN3)[h]
            came = pl.ds(at(c, k, h), half)
            kept = pl.ds(at(c, k, 1 - h), half)
            three_s[c, h, halves(h), :] = (ig[came, :] + over_r[c, halves(h), :].astype(jnp.float32)).astype(jnp.bfloat16)
            three_s[c, h, halves(1 - h), :] = ig[kept, :].astype(jnp.bfloat16)
            b3[c][h].start()

    def end_back(c):
        for h in range(2):
            b3[c][h].wait_recv()
            one_s[c, h] = (gradient(c, (UP1, DOWN1)[h]) + three_r[c, h].astype(jnp.float32)).astype(jnp.bfloat16)
            b1[c][h].start()

    def loss_of(k):
        block = jnp.concatenate([loss_acc[pl.ds(at(c, k), sub), :] for c in range(CHUNKS)], axis=0)
        return jnp.sum(block.T, axis=0, keepdims=True)

    def give_loss(dst, row):
        dst[...] = jnp.broadcast_to(row, dst.shape)

    def partial(j, where):
        return tg[pl.ds(j * rows + where.start, where.size), :] + sib_r[j, where, :].astype(jnp.float32)

    def text_begin(p):
        arrive([back[p][FAR]])
        for s in range(2):
            far_s[edges(p, s), :] = partial(FAR, edges(p, s)).astype(jnp.bfloat16)
            t2[p][s].start()

    def text_middle(p):
        for s in range(2):
            j = (PREV, NEXT)[s]
            arrive([back[p][j]])
            row_s[s, edges(p, 1 - s), :] = partial(j, edges(p, 1 - s)).astype(jnp.bfloat16)
            t2[p][s].wait_recv()
            total = partial(j, edges(p, s)) + far_r[edges(p, s), :].astype(jnp.float32)
            row_s[s, edges(p, s), :] = total.astype(jnp.bfloat16)
            t1[p][s].start()

    for c in range(CHUNKS):
        start(z1[c])
    for p in range(PARTS):
        start(x1[p])
    across[OWN].start()
    pass_on(z1[0], z3[0])
    for p in range(PARTS):
        pass_on(x1[p], x2[p])
    across[PREV].start()
    across[NEXT].start()
    pass_on(z1[1], z3[1])
    wholes = [weigh(0, 3 * rows, 1, False)]
    arrive([across[PREV], across[NEXT]])
    wholes.append(weigh(0, 3 * rows, 3, False))
    for p in range(PARTS):
        arrive(x2[p])
    across[FAR].start()
    wholes.append(weigh(0, 3 * rows, 0, True))
    arrive([across[OWN], across[FAR]])
    wholes.append(weigh(0, 3 * rows, 2, False))
    loss_part(0, 3 * rows, wholes)
    pass_on(z3[0], z4[0])
    image_partial(0, 3 * rows)
    pass_on(z3[1], z4[1])
    for q in (1, 0):
        text_partial(0, q)
    for c in range(CHUNKS):
        arrive(z4[c])
        far(c)
        begin_back(c)

    middle_back(0)
    text_partial(1, 1)
    for p in range(PARTS):
        for j in (FAR, PREV, NEXT, OWN):
            sib_s[j, parts(p), :] = tg[pl.ds(row_texts + j * rows + p * part, part), :].astype(jnp.bfloat16)
            back[p][j].start()
    middle_back(1)
    give_loss(over_ls, loss_of(OVER))
    start(l4)
    text_partial(1, 0)
    for p in range(PARTS):
        text_begin(p)
    end_back(0)
    lane = lax.broadcasted_iota(jnp.int32, (1, rows), 1)
    for h in range(2):
        l4[h].wait_recv()
        mine = (lane // half) % 2 == h
        give_loss(three_ls.at[h], loss_of((UP3, DOWN3)[h]) + jnp.where(mine, over_lr[h, pl.ds(0, 1), :], 0.0))
        l3[h].start()
    for p in range(PARTS):
        text_middle(p)
    end_back(1)
    for h in range(2):
        l3[h].wait_recv()
        give_loss(one_ls.at[h], loss_of((UP1, DOWN1)[h]) + three_lr[h, pl.ds(0, 1), :])
        l1[h].start()

    scale_row = jnp.exp(jnp.full((1, width), ls_ref[0], jnp.float32))

    def backprop(raw, grads):
        unit, inverse = unit_of(raw)
        grads = scale_row * grads
        return (grads - unit * jnp.sum(unit * grads, axis=1, keepdims=True)) * inverse

    def finish_image(c):
        here = pl.ds(c * sub, sub)
        arrive(b1[c])
        grads = gradient(c, OWN) + (one_r[c, 0].astype(jnp.float32) + one_r[c, 1].astype(jnp.float32))
        gi_ref[here, :] = backprop(img_ref[here, :], grads)

    def finish_text(p):
        here = parts(p)
        arrive([back[p][OWN]])
        arrive(t1[p])
        grads = partial(OWN, here) + (row_r[0, here, :].astype(jnp.float32) + row_r[1, here, :].astype(jnp.float32))
        gt_ref[here, :] = backprop(txt_ref[here, :], grads)

    for p in range(PARTS):
        finish_text(p)
    finish_image(0)
    arrive(l1)
    loss_ref[...] = loss_of(OWN) + one_lr[0, pl.ds(0, 1), :] + one_lr[1, pl.ds(0, 1), :]
    finish_image(1)
    for sent in messages:
        sent.wait_send()


N_COPIES = 160


def per_device(groups, image_emb, text_emb, log_scale, bias):
    rows, width = image_emb.shape
    sub = rows // CHUNKS
    half_type, full = jnp.bfloat16, jnp.float32
    vmem = pl.BlockSpec(memory_space=pltpu.VMEM)
    smem = pl.BlockSpec(memory_space=pltpu.SMEM)
    loss, grad_image, grad_text = pl.pallas_call(
        lambda *refs: kernel(groups, *refs),
        out_shape=(
            jax.ShapeDtypeStruct((1, rows), full),
            jax.ShapeDtypeStruct((rows, width), full),
            jax.ShapeDtypeStruct((rows, width), full),
        ),
        in_specs=[smem, smem, vmem, vmem],
        out_specs=(vmem, vmem, vmem),
        scratch_shapes=[
            pltpu.VMEM((8 * rows, width), half_type),
            pltpu.VMEM((6 * rows, width), half_type),
            pltpu.VMEM((6 * rows, 8 * rows), half_type),
            pltpu.VMEM((8 * rows, width), full),
            pltpu.VMEM((6 * rows, width), full),
            pltpu.VMEM((6 * rows, rows), full),
            pltpu.VMEM((CHUNKS, sub, width), half_type),
            pltpu.VMEM((CHUNKS, sub, width), half_type),
            pltpu.VMEM((CHUNKS, 2, sub, width), half_type),
            pltpu.VMEM((CHUNKS, 2, sub, width), half_type),
            pltpu.VMEM((CHUNKS, 2, sub, width), half_type),
            pltpu.VMEM((CHUNKS, 2, sub, width), half_type),
            pltpu.VMEM((4, rows, width), half_type),
            pltpu.VMEM((4, rows, width), half_type),
            pltpu.VMEM((rows, width), half_type),
            pltpu.VMEM((rows, width), half_type),
            pltpu.VMEM((2, rows, width), half_type),
            pltpu.VMEM((2, rows, width), half_type),
            pltpu.VMEM((8, rows), full),
            pltpu.VMEM((2, 8, rows), full),
            pltpu.VMEM((2, 8, rows), full),
            pltpu.VMEM((2, 8, rows), full),
            pltpu.VMEM((2, 8, rows), full),
            pltpu.VMEM((2, 8, rows), full),
            pltpu.SemaphoreType.DMA((N_COPIES,)),
            pltpu.SemaphoreType.DMA((N_COPIES,)),
        ],
        compiler_params=pltpu.CompilerParams(
            collective_id=0, has_side_effects=True, vmem_limit_bytes=48 * 1024 * 1024
        ),
    )(log_scale, bias, image_emb, text_emb)
    return (loss.reshape(rows), grad_image, grad_text)


def solution(mesh):
    groups = mesh.shape["outer"]
    in_specs = (P(("outer", "inner"), None), P(("outer", "inner"), None), P(), P())
    out_specs = (P(("outer", "inner")), P(("outer", "inner"), None), P(("outer", "inner"), None))
    return jax.shard_map(
        lambda *args: per_device(groups, *args),
        mesh=mesh, in_specs=in_specs, out_specs=out_specs, check_vma=False,
    )
```

```python
import jax
import jax.numpy as jnp
from jax import lax
from jax.experimental import pallas as pl
from jax.experimental.pallas import tpu as pltpu
from jax.sharding import PartitionSpec as P

MESH = pl.DeviceIdType.MESH
EPS = 1e-06
LOG2_E = 1.4426950408889634

X_N = 4
Z_LO = 4
Z_N = 8

OWN, FAR, PREV, NEXT = 0, 1, 2, 3
UP1, DOWN1, UP3, DOWN3, OVER = 1, 2, 3, 4, 5

CHUNKS = 2
PARTS = 1


def unit_of(raw):
    wide = raw.astype(jnp.float32)
    inverse = lax.rsqrt(jnp.sum(wide * wide, axis=1, keepdims=True) + EPS)
    return wide * inverse, inverse


def places(groups):
    outer = lax.axis_index("outer")
    inner = lax.axis_index("inner")
    z_lo = outer % Z_LO
    x, z_hi, core = inner // 4, (inner // 2) % 2, inner % 2

    def inner_of(x, z_hi, core):
        return x * 4 + z_hi * 2 + core

    def group_by(by):
        z = (z_hi * Z_LO + z_lo + by + Z_N) % Z_N
        step = by if by in (1, -1) else -by
        return ((outer + step + groups) % groups, inner_of(x, z // Z_LO, core))

    return {
        "xn": (outer, inner_of((x + 1) % X_N, z_hi, core)),
        "xp": (outer, inner_of((x + X_N - 1) % X_N, z_hi, core)),
        "sib": (outer, inner_of(x, z_hi, 1 - core)),
        "gn": group_by(1),
        "gp": group_by(-1),
        "tn": group_by(2),
        "tp": group_by(-2),
    }


def kernel(
    groups, ls_ref, b_ref, img_ref, txt_ref, loss_ref, gi_ref, gt_ref,
    texts, images, wt, tg, ig, loss_acc, five_s, five_r, over_s, over_r, three_s, three_r, one_s, one_r,
    sib_s, sib_r, far_s, far_r, row_s, row_r, five_ls, five_lr, over_ls, over_lr, three_ls, three_lr, one_ls, one_lr, ssem, rsem,
):
    rows, width = img_ref.shape
    sub = rows // CHUNKS
    half = sub // 2
    part = rows // PARTS
    edge = part // 2
    tile = 2 * rows
    row_texts = 4 * rows
    peers = places(groups)
    messages = []

    def message(src, dst, peer):
        index = len(messages)
        messages.append(
            pltpu.make_async_remote_copy(
                src_ref=src, dst_ref=dst, send_sem=ssem.at[index], recv_sem=rsem.at[index],
                device_id=peers[peer], device_id_type=MESH,
            )
        )
        return messages[-1]

    def at(c, k, h=0):
        return (c * 3 + k % 3) * sub + (k // 3) * 3 * rows + h * half

    def image(c, k):
        return images.at[pl.ds(at(c, k), sub), :]

    def image_half(c, k, h):
        return images.at[pl.ds(at(c, k, h), half), :]

    def text(q, j):
        return texts.at[pl.ds((q * 4 + j) * rows, rows), :]

    def text_part(j, p):
        return texts.at[pl.ds(j * rows + p * part, part), :]

    def text_edge(j, p, e):
        return texts.at[pl.ds(j * rows + p * part + e * edge, edge), :]

    def halves(h):
        return pl.ds(h * half, half)

    def parts(p):
        return pl.ds(p * part, part)

    def edges(p, e):
        return pl.ds(p * part + e * edge, edge)

    z1 = [[message(image_half(c, OWN, h), image_half(c, (UP1, DOWN1)[h], h), ("gn", "gp")[h]) for h in range(2)] for c in range(CHUNKS)]
    z1_other = [
        [message(image_half(c, OWN, 1 - h), image_half(c, (UP1, DOWN1)[h], 1 - h), ("gn", "gp")[h]) for h in range(2)]
        for c in range(CHUNKS)
    ]
    z3 = [
        [message(image_half(c, (UP1, DOWN1)[h], h), image_half(c, (UP3, DOWN3)[h], h), ("tn", "tp")[h]) for h in range(2)]
        for c in range(CHUNKS)
    ]
    z4 = [
        [message(image_half(c, (UP3, DOWN3)[h], h), image_half(c, OVER, h), ("gn", "gp")[h]) for h in range(2)]
        for c in range(CHUNKS)
    ]
    z5 = [
        [message(image_half(c, OVER, h), image_half(c, (DOWN3, UP3)[h], h), ("gn", "gp")[h]) for h in range(2)]
        for c in range(CHUNKS)
    ]
    x1 = [[message(text_part(OWN, p), text_part((PREV, NEXT)[s], p), ("xn", "xp")[s]) for s in range(2)] for p in range(PARTS)]
    x2 = [
        [message(text_edge((PREV, NEXT)[s], p, s), text_edge(FAR, p, s), ("xn", "xp")[s]) for s in range(2)]
        for p in range(PARTS)
    ]
    across = [message(text(0, j), text(1, j), "sib") for j in range(4)]
    b5 = [[message(five_s.at[c, halves(h), :], five_r.at[c, halves(h), :], ("gp", "gn")[h]) for h in range(2)] for c in range(CHUNKS)]
    b4 = [[message(over_s.at[c, halves(h), :], over_r.at[c, halves(h), :], ("gp", "gn")[h]) for h in range(2)] for c in range(CHUNKS)]
    b3 = [[message(three_s.at[c, halves(h), :], three_r.at[c, halves(h), :], ("tp", "tn")[h]) for h in range(2)] for c in range(CHUNKS)]
    b1 = [[message(one_s.at[c, h, halves(h), :], one_r.at[c, h, halves(h), :], ("gp", "gn")[h]) for h in range(2)] for c in range(CHUNKS)]
    b1_other = [
        [message(one_s.at[c, h, halves(1 - h), :], one_r.at[c, h, halves(1 - h), :], ("gp", "gn")[h]) for h in range(2)]
        for c in range(CHUNKS)
    ]
    back = [[message(sib_s.at[j, parts(p), :], sib_r.at[j, parts(p), :], "sib") for j in range(4)] for p in range(PARTS)]
    t2 = [[message(far_s.at[edges(p, s), :], far_r.at[edges(p, s), :], ("xp", "xn")[s]) for s in range(2)] for p in range(PARTS)]
    t1 = [[message(row_s.at[s, parts(p), :], row_r.at[s, parts(p), :], ("xp", "xn")[s]) for s in range(2)] for p in range(PARTS)]
    l5 = [message(five_ls.at[h], five_lr.at[h], ("gp", "gn")[h]) for h in range(2)]
    l4 = [message(over_ls, over_lr.at[h], ("gp", "gn")[h]) for h in range(2)]
    l3 = [message(three_ls.at[h], three_lr.at[h], ("tp", "tn")[h]) for h in range(2)]
    l1 = [message(one_ls.at[h], one_lr.at[h], ("gp", "gn")[h]) for h in range(2)]

    def start(copies):
        for copy in copies:
            copy.start()

    def arrive(copies):
        for copy in copies:
            copy.wait_recv()

    def pass_on(arrivals, onward):
        for here, there in zip(arrivals, onward):
            here.wait_recv()
            there.start()

    barrier = pltpu.get_barrier_semaphore()
    for peer in peers.values():
        pl.semaphore_signal(barrier, inc=1, device_id=peer, device_id_type=MESH)
    own = unit_of(img_ref[...])[0].astype(jnp.bfloat16)
    for c in range(CHUNKS):
        images[pl.ds(at(c, OWN), sub), :] = own[c * sub:(c + 1) * sub]
    texts[pl.ds(0, rows), :] = unit_of(txt_ref[...])[0].astype(jnp.bfloat16)
    scale = jnp.exp(jnp.full((1, tile), ls_ref[0], jnp.float32)) * LOG2_E
    offset = b_ref[0] * LOG2_E
    pl.semaphore_wait(barrier, len(peers))

    def weigh(begin, size, n, diagonal):
        here = pl.ds(begin, size)
        columns = pl.ds(n * tile, tile)
        dots = lax.dot_general(
            images[here, :], texts[columns, :], (((1,), (1,)), ((), ())), preferred_element_type=jnp.float32
        )
        grown = jnp.exp2(scale * dots + offset)
        whole = 1.0 + grown
        inverse = pl.reciprocal(whole, approx=True)
        weights = grown * (inverse * (2.0 - whole * inverse))
        if diagonal:
            row = lax.broadcasted_iota(jnp.int32, (size, tile), 0)
            column = lax.broadcasted_iota(jnp.int32, (size, tile), 1)
            positive = row < 0
            for c in range(CHUNKS):
                first = at(c, OWN)
                positive |= (row - first == column - c * sub) & (row >= first) & (row < first + sub)
            weights = weights - positive.astype(jnp.float32)
            whole = jnp.where(positive, 1.0 + 1.0 / grown, whole)
        wt[here, columns] = weights.astype(jnp.bfloat16)
        return whole

    def loss_part(begin, size, wholes):
        here = pl.ds(begin, size)
        logs = jnp.log((wholes[0] * wholes[1]) * (wholes[2] * wholes[3]))
        loss_acc[here, :] = logs[:, :rows] + logs[:, rows:]

    def image_partial(begin, size):
        here = pl.ds(begin, size)
        ig[here, :] = jnp.dot(wt[here, :], texts[...], preferred_element_type=jnp.float32)

    def far(c):
        begin, size = at(c, UP3), 3 * sub
        loss_part(begin, size, [weigh(begin, size, n, False) for n in range(4)])
        image_partial(begin, size)

    def text_partial(far_ones, q):
        these = pl.ds(far_ones * 3 * rows, 3 * rows)
        columns = pl.ds(q * row_texts, row_texts)
        term = lax.dot_general(
            wt[these, columns], images[these, :], (((0,), (0,)), ((), ())), preferred_element_type=jnp.float32
        )
        if far_ones:
            tg[columns, :] += term
        else:
            tg[columns, :] = term

    def gradient(c, k):
        return ig[pl.ds(at(c, k), sub), :]

    def send_back(sent, copies, c, h, k, came=None):
        total = ig[pl.ds(at(c, k, h), half), :]
        if came is not None:
            total = total + came.astype(jnp.float32)
        sent[halves(h), :] = total.astype(jnp.bfloat16)
        copies[c][h].start()

    def back_5(c):
        for h in range(2):
            send_back(five_s.at[c], b5, c, h, (DOWN3, UP3)[h])

    def back_4(c):
        for h in range(2):
            b5[c][h].wait_recv()
            send_back(over_s.at[c], b4, c, h, OVER, five_r[c, halves(h), :])

    def back_3(c):
        for h in range(2):
            b4[c][h].wait_recv()
            send_back(three_s.at[c], b3, c, h, (UP3, DOWN3)[h], over_r[c, halves(h), :])

    def back_1(c):
        for h in range(2):
            b3[c][h].wait_recv()
            send_back(one_s.at[c, h], b1, c, h, (UP1, DOWN1)[h], three_r[c, halves(h), :])

    def back_1_other(c):
        for h in range(2):
            one_s[c, h, halves(1 - h), :] = ig[pl.ds(at(c, (UP1, DOWN1)[h], 1 - h), half), :].astype(jnp.bfloat16)
            b1_other[c][h].start()

    def loss_of(k):
        block = jnp.concatenate([loss_acc[pl.ds(at(c, k), sub), :] for c in range(CHUNKS)], axis=0)
        return jnp.sum(block.T, axis=0, keepdims=True)

    def give_loss(dst, row):
        dst[...] = jnp.broadcast_to(row, dst.shape)

    def partial(j, where):
        return tg[pl.ds(j * rows + where.start, where.size), :] + sib_r[j, where, :].astype(jnp.float32)

    def text_begin(p):
        arrive([back[p][FAR]])
        for s in range(2):
            far_s[edges(p, s), :] = partial(FAR, edges(p, s)).astype(jnp.bfloat16)
            t2[p][s].start()

    def text_middle(p):
        for s in range(2):
            j = (PREV, NEXT)[s]
            arrive([back[p][j]])
            row_s[s, edges(p, 1 - s), :] = partial(j, edges(p, 1 - s)).astype(jnp.bfloat16)
            t2[p][s].wait_recv()
            total = partial(j, edges(p, s)) + far_r[edges(p, s), :].astype(jnp.float32)
            row_s[s, edges(p, s), :] = total.astype(jnp.bfloat16)
            t1[p][s].start()

    for c in range(CHUNKS):
        start(z1[c])
    start(x1[0])
    across[OWN].start()
    for c in range(CHUNKS):
        start(z1_other[c])
    pass_on(z1[0], z3[0])
    pass_on(z1[1], z3[1])
    pass_on(x1[0], x2[0])
    across[PREV].start()
    across[NEXT].start()
    for c in range(CHUNKS):
        arrive(z1_other[c])
    wholes = [weigh(0, 3 * rows, 1, False)]
    arrive([across[PREV], across[NEXT]])
    wholes.append(weigh(0, 3 * rows, 3, False))
    arrive(x2[0])
    across[FAR].start()
    wholes.append(weigh(0, 3 * rows, 0, True))
    arrive([across[OWN], across[FAR]])
    pass_on(z3[0], z4[0])
    wholes.append(weigh(0, 3 * rows, 2, False))
    loss_part(0, 3 * rows, wholes)
    pass_on(z3[1], z4[1])
    image_partial(0, 3 * rows)
    pass_on(z4[0], z5[0])
    text_partial(0, 1)
    pass_on(z4[1], z5[1])
    text_partial(0, 0)
    for c in range(CHUNKS):
        arrive(z5[c])
        far(c)
        back_5(c)

    back_4(0)
    for c in range(CHUNKS):
        back_1_other(c)
    text_partial(1, 1)
    for j in (FAR, PREV, NEXT, OWN):
        sib_s[j] = tg[pl.ds(row_texts + j * rows, rows), :].astype(jnp.bfloat16)
        back[0][j].start()
    back_4(1)
    for h in range(2):
        give_loss(five_ls.at[h], loss_of((DOWN3, UP3)[h]))
        l5[h].start()
    text_partial(1, 0)
    back_3(0)
    text_begin(0)
    lane = lax.broadcasted_iota(jnp.int32, (1, rows), 1)

    def of_half(h, came):
        return jnp.where((lane // half) % 2 == h, came[h, pl.ds(0, 1), :], 0.0)

    arrive(l5)
    give_loss(over_ls, loss_of(OVER) + of_half(0, five_lr) + of_half(1, five_lr))
    start(l4)
    back_3(1)
    text_middle(0)
    for h in range(2):
        l4[h].wait_recv()
        give_loss(three_ls.at[h], loss_of((UP3, DOWN3)[h]) + of_half(h, over_lr))
        l3[h].start()
    back_1(0)
    for h in range(2):
        l3[h].wait_recv()
        give_loss(one_ls.at[h], loss_of((UP1, DOWN1)[h]) + of_half(h, three_lr))
        l1[h].start()
    back_1(1)

    scale_row = jnp.exp(jnp.full((1, width), ls_ref[0], jnp.float32))

    def backprop(raw, grads):
        unit, inverse = unit_of(raw)
        grads = scale_row * grads
        return (grads - unit * jnp.sum(unit * grads, axis=1, keepdims=True)) * inverse

    def finish_image(c):
        here = pl.ds(c * sub, sub)
        arrive(b1[c])
        arrive(b1_other[c])
        grads = gradient(c, OWN) + (one_r[c, 0].astype(jnp.float32) + one_r[c, 1].astype(jnp.float32))
        gi_ref[here, :] = backprop(img_ref[here, :], grads)

    def finish_text(p):
        here = parts(p)
        arrive([back[p][OWN]])
        arrive(t1[p])
        grads = partial(OWN, here) + (row_r[0, here, :].astype(jnp.float32) + row_r[1, here, :].astype(jnp.float32))
        gt_ref[here, :] = backprop(txt_ref[here, :], grads)

    for p in range(PARTS):
        finish_text(p)
    finish_image(0)
    arrive(l1)
    loss_ref[...] = loss_of(OWN) + one_lr[0, pl.ds(0, 1), :] + one_lr[1, pl.ds(0, 1), :]
    finish_image(1)
    for sent in messages:
        sent.wait_send()


N_MESSAGES = 64


def per_device(groups, image_emb, text_emb, log_scale, bias):
    rows, width = image_emb.shape
    sub = rows // CHUNKS
    half_type, full = jnp.bfloat16, jnp.float32
    vmem = pl.BlockSpec(memory_space=pltpu.VMEM)
    smem = pl.BlockSpec(memory_space=pltpu.SMEM)
    loss, grad_image, grad_text = pl.pallas_call(
        lambda *refs: kernel(groups, *refs),
        out_shape=(
            jax.ShapeDtypeStruct((1, rows), full),
            jax.ShapeDtypeStruct((rows, width), full),
            jax.ShapeDtypeStruct((rows, width), full),
        ),
        in_specs=[smem, smem, vmem, vmem],
        out_specs=(vmem, vmem, vmem),
        scratch_shapes=[
            pltpu.VMEM((8 * rows, width), half_type),
            pltpu.VMEM((6 * rows, width), half_type),
            pltpu.VMEM((6 * rows, 8 * rows), half_type),
            pltpu.VMEM((8 * rows, width), full),
            pltpu.VMEM((6 * rows, width), full),
            pltpu.VMEM((6 * rows, rows), full),
            pltpu.VMEM((CHUNKS, sub, width), half_type),
            pltpu.VMEM((CHUNKS, sub, width), half_type),
            pltpu.VMEM((CHUNKS, sub, width), half_type),
            pltpu.VMEM((CHUNKS, sub, width), half_type),
            pltpu.VMEM((CHUNKS, sub, width), half_type),
            pltpu.VMEM((CHUNKS, sub, width), half_type),
            pltpu.VMEM((CHUNKS, 2, sub, width), half_type),
            pltpu.VMEM((CHUNKS, 2, sub, width), half_type),
            pltpu.VMEM((4, rows, width), half_type),
            pltpu.VMEM((4, rows, width), half_type),
            pltpu.VMEM((rows, width), half_type),
            pltpu.VMEM((rows, width), half_type),
            pltpu.VMEM((2, rows, width), half_type),
            pltpu.VMEM((2, rows, width), half_type),
            pltpu.VMEM((2, 8, rows), full),
            pltpu.VMEM((2, 8, rows), full),
            pltpu.VMEM((8, rows), full),
            pltpu.VMEM((2, 8, rows), full),
            pltpu.VMEM((2, 8, rows), full),
            pltpu.VMEM((2, 8, rows), full),
            pltpu.VMEM((2, 8, rows), full),
            pltpu.VMEM((2, 8, rows), full),
            pltpu.SemaphoreType.DMA((N_MESSAGES,)),
            pltpu.SemaphoreType.DMA((N_MESSAGES,)),
        ],
        compiler_params=pltpu.CompilerParams(
            collective_id=0, has_side_effects=True, vmem_limit_bytes=48 * 1024 * 1024
        ),
    )(log_scale, bias, image_emb, text_emb)
    return (loss.reshape(rows), grad_image, grad_text)


def solution(mesh):
    groups = mesh.shape["outer"]
    in_specs = (P(("outer", "inner"), None), P(("outer", "inner"), None), P(), P())
    out_specs = (P(("outer", "inner")), P(("outer", "inner"), None), P(("outer", "inner"), None))
    return jax.shard_map(
        lambda *args: per_device(groups, *args),
        mesh=mesh, in_specs=in_specs, out_specs=out_specs, check_vma=False,
    )
```

```python
import jax
import jax.numpy as jnp
from jax import lax
from jax.experimental import pallas as pl
from jax.experimental.pallas import tpu as pltpu
from jax.sharding import PartitionSpec as P

MESH = pl.DeviceIdType.MESH
EPS = 1e-06
LOG2_E = 1.4426950408889634

X_N = 4
Z_LO = 4
Z_N = 8

OWN, FAR, PREV, NEXT = 0, 1, 2, 3
UP1, DOWN1, UP3, DOWN3, OVER = 1, 2, 3, 4, 5

CHUNKS = 2
PARTS = 1


def unit_of(raw):
    wide = raw.astype(jnp.float32)
    inverse = lax.rsqrt(jnp.sum(wide * wide, axis=1, keepdims=True) + EPS)
    return wide * inverse, inverse


def places(groups):
    outer = lax.axis_index("outer")
    inner = lax.axis_index("inner")
    z_lo = outer % Z_LO
    x, z_hi, core = inner // 4, (inner // 2) % 2, inner % 2

    def inner_of(x, z_hi, core):
        return x * 4 + z_hi * 2 + core

    def group_by(by):
        z = (z_hi * Z_LO + z_lo + by + Z_N) % Z_N
        step = by if by in (1, -1) else -by
        return ((outer + step + groups) % groups, inner_of(x, z // Z_LO, core))

    return {
        "xn": (outer, inner_of((x + 1) % X_N, z_hi, core)),
        "xp": (outer, inner_of((x + X_N - 1) % X_N, z_hi, core)),
        "sib": (outer, inner_of(x, z_hi, 1 - core)),
        "gn": group_by(1),
        "gp": group_by(-1),
        "tn": group_by(2),
        "tp": group_by(-2),
    }


def kernel(
    groups, ls_ref, b_ref, img_ref, txt_ref, loss_ref, gi_ref, gt_ref,
    texts, images, wt, tg, ig, loss_acc, five_s, five_r, over_s, over_r, three_s, three_r, one_s, one_r,
    sib_s, sib_r, far_s, far_r, row_s, row_r, five_ls, five_lr, over_ls, over_lr, three_ls, three_lr, one_ls, one_lr, ssem, rsem,
):
    rows, width = img_ref.shape
    sub = rows // CHUNKS
    half = sub // 2
    part = rows // PARTS
    edge = part // 2
    tile = 2 * rows
    row_texts = 4 * rows
    peers = places(groups)
    messages = []

    def message(src, dst, peer):
        index = len(messages)
        messages.append(
            pltpu.make_async_remote_copy(
                src_ref=src, dst_ref=dst, send_sem=ssem.at[index], recv_sem=rsem.at[index],
                device_id=peers[peer], device_id_type=MESH,
            )
        )
        return messages[-1]

    def at(c, k, h=0):
        return (c * 3 + k % 3) * sub + (k // 3) * 3 * rows + h * half

    def image(c, k):
        return images.at[pl.ds(at(c, k), sub), :]

    def image_half(c, k, h):
        return images.at[pl.ds(at(c, k, h), half), :]

    def text(q, j):
        return texts.at[pl.ds((q * 4 + j) * rows, rows), :]

    def text_part(j, p):
        return texts.at[pl.ds(j * rows + p * part, part), :]

    def text_edge(j, p, e):
        return texts.at[pl.ds(j * rows + p * part + e * edge, edge), :]

    def halves(h):
        return pl.ds(h * half, half)

    def parts(p):
        return pl.ds(p * part, part)

    def edges(p, e):
        return pl.ds(p * part + e * edge, edge)

    z1 = [[message(image_half(c, OWN, h), image_half(c, (UP1, DOWN1)[h], h), ("gn", "gp")[h]) for h in range(2)] for c in range(CHUNKS)]
    z1_other = [
        [message(image_half(c, OWN, 1 - h), image_half(c, (UP1, DOWN1)[h], 1 - h), ("gn", "gp")[h]) for h in range(2)]
        for c in range(CHUNKS)
    ]
    z3 = [
        [message(image_half(c, (UP1, DOWN1)[h], h), image_half(c, (UP3, DOWN3)[h], h), ("tn", "tp")[h]) for h in range(2)]
        for c in range(CHUNKS)
    ]
    z4 = [
        [message(image_half(c, (UP3, DOWN3)[h], h), image_half(c, OVER, h), ("gn", "gp")[h]) for h in range(2)]
        for c in range(CHUNKS)
    ]
    z5 = [
        [message(image_half(c, OVER, h), image_half(c, (DOWN3, UP3)[h], h), ("gn", "gp")[h]) for h in range(2)]
        for c in range(CHUNKS)
    ]
    x1 = [[message(text_part(OWN, p), text_part((PREV, NEXT)[s], p), ("xn", "xp")[s]) for s in range(2)] for p in range(PARTS)]
    x2 = [
        [message(text_edge((PREV, NEXT)[s], p, s), text_edge(FAR, p, s), ("xn", "xp")[s]) for s in range(2)]
        for p in range(PARTS)
    ]
    across = [message(text(0, j), text(1, j), "sib") for j in range(4)]
    b5 = [[message(five_s.at[c, halves(h), :], five_r.at[c, halves(h), :], ("gp", "gn")[h]) for h in range(2)] for c in range(CHUNKS)]
    b4 = [[message(over_s.at[c, halves(h), :], over_r.at[c, halves(h), :], ("gp", "gn")[h]) for h in range(2)] for c in range(CHUNKS)]
    b3 = [[message(three_s.at[c, halves(h), :], three_r.at[c, halves(h), :], ("tp", "tn")[h]) for h in range(2)] for c in range(CHUNKS)]
    b1 = [[message(one_s.at[c, h, halves(h), :], one_r.at[c, h, halves(h), :], ("gp", "gn")[h]) for h in range(2)] for c in range(CHUNKS)]
    b1_other = [
        [message(one_s.at[c, h, halves(1 - h), :], one_r.at[c, h, halves(1 - h), :], ("gp", "gn")[h]) for h in range(2)]
        for c in range(CHUNKS)
    ]
    back = [[message(sib_s.at[j, parts(p), :], sib_r.at[j, parts(p), :], "sib") for j in range(4)] for p in range(PARTS)]
    t2 = [[message(far_s.at[edges(p, s), :], far_r.at[edges(p, s), :], ("xp", "xn")[s]) for s in range(2)] for p in range(PARTS)]
    t1 = [[message(row_s.at[s, parts(p), :], row_r.at[s, parts(p), :], ("xp", "xn")[s]) for s in range(2)] for p in range(PARTS)]
    l5 = [message(five_ls.at[h], five_lr.at[h], ("gp", "gn")[h]) for h in range(2)]
    l4 = [message(over_ls, over_lr.at[h], ("gp", "gn")[h]) for h in range(2)]
    l3 = [message(three_ls.at[h], three_lr.at[h], ("tp", "tn")[h]) for h in range(2)]
    l1 = [message(one_ls.at[h], one_lr.at[h], ("gp", "gn")[h]) for h in range(2)]

    def start(copies):
        for copy in copies:
            copy.start()

    def arrive(copies):
        for copy in copies:
            copy.wait_recv()

    def pass_on(arrivals, onward):
        for here, there in zip(arrivals, onward):
            here.wait_recv()
            there.start()

    barrier = pltpu.get_barrier_semaphore()
    for peer in peers.values():
        pl.semaphore_signal(barrier, inc=1, device_id=peer, device_id_type=MESH)
    own = unit_of(img_ref[...])[0].astype(jnp.bfloat16)
    for c in range(CHUNKS):
        images[pl.ds(at(c, OWN), sub), :] = own[c * sub:(c + 1) * sub]
    scale = jnp.exp(jnp.full((1, tile), ls_ref[0], jnp.float32)) * LOG2_E
    offset = b_ref[0] * LOG2_E
    pl.semaphore_wait(barrier, len(peers))

    def weigh(begin, size, n, diagonal):
        here = pl.ds(begin, size)
        columns = pl.ds(n * tile, tile)
        dots = lax.dot_general(
            images[here, :], texts[columns, :], (((1,), (1,)), ((), ())), preferred_element_type=jnp.float32
        )
        grown = jnp.exp2(scale * dots + offset)
        whole = 1.0 + grown
        inverse = pl.reciprocal(whole, approx=True)
        weights = grown * (inverse * (2.0 - whole * inverse))
        if diagonal:
            row = lax.broadcasted_iota(jnp.int32, (size, tile), 0)
            column = lax.broadcasted_iota(jnp.int32, (size, tile), 1)
            positive = row < 0
            for c in range(CHUNKS):
                first = at(c, OWN)
                positive |= (row - first == column - c * sub) & (row >= first) & (row < first + sub)
            weights = weights - positive.astype(jnp.float32)
            whole = jnp.where(positive, 1.0 + 1.0 / grown, whole)
        wt[here, columns] = weights.astype(jnp.bfloat16)
        return whole

    def loss_part(begin, size, wholes):
        here = pl.ds(begin, size)
        logs = jnp.log((wholes[0] * wholes[1]) * (wholes[2] * wholes[3]))
        loss_acc[here, :] = logs[:, :rows] + logs[:, rows:]

    def image_partial(begin, size):
        here = pl.ds(begin, size)
        ig[here, :] = jnp.dot(wt[here, :], texts[...], preferred_element_type=jnp.float32)

    def far(c):
        begin, size = at(c, UP3), 3 * sub
        loss_part(begin, size, [weigh(begin, size, n, False) for n in range(4)])
        image_partial(begin, size)

    def text_partial(far_ones, q):
        these = pl.ds(far_ones * 3 * rows, 3 * rows)
        columns = pl.ds(q * row_texts, row_texts)
        term = lax.dot_general(
            wt[these, columns], images[these, :], (((0,), (0,)), ((), ())), preferred_element_type=jnp.float32
        )
        if far_ones:
            tg[columns, :] += term
        else:
            tg[columns, :] = term

    def gradient(c, k):
        return ig[pl.ds(at(c, k), sub), :]

    def send_back(sent, copies, c, h, k, came=None):
        total = ig[pl.ds(at(c, k, h), half), :]
        if came is not None:
            total = total + came.astype(jnp.float32)
        sent[halves(h), :] = total.astype(jnp.bfloat16)
        copies[c][h].start()

    def back_5(c):
        for h in range(2):
            send_back(five_s.at[c], b5, c, h, (DOWN3, UP3)[h])

    def back_4(c):
        for h in range(2):
            b5[c][h].wait_recv()
            send_back(over_s.at[c], b4, c, h, OVER, five_r[c, halves(h), :])

    def back_3(c):
        for h in range(2):
            b4[c][h].wait_recv()
            send_back(three_s.at[c], b3, c, h, (UP3, DOWN3)[h], over_r[c, halves(h), :])

    def back_1(c):
        for h in range(2):
            b3[c][h].wait_recv()
            send_back(one_s.at[c, h], b1, c, h, (UP1, DOWN1)[h], three_r[c, halves(h), :])

    def back_1_other(c):
        for h in range(2):
            one_s[c, h, halves(1 - h), :] = ig[pl.ds(at(c, (UP1, DOWN1)[h], 1 - h), half), :].astype(jnp.bfloat16)
            b1_other[c][h].start()

    def loss_of(k):
        block = jnp.concatenate([loss_acc[pl.ds(at(c, k), sub), :] for c in range(CHUNKS)], axis=0)
        return jnp.sum(block.T, axis=0, keepdims=True)

    def give_loss(dst, row):
        dst[...] = jnp.broadcast_to(row, dst.shape)

    def partial(j, where):
        return tg[pl.ds(j * rows + where.start, where.size), :] + sib_r[j, where, :].astype(jnp.float32)

    def text_begin(p):
        arrive([back[p][FAR]])
        for s in range(2):
            far_s[edges(p, s), :] = partial(FAR, edges(p, s)).astype(jnp.bfloat16)
            t2[p][s].start()

    def text_middle(p):
        for s in range(2):
            j = (PREV, NEXT)[s]
            arrive([back[p][j]])
            row_s[s, edges(p, 1 - s), :] = partial(j, edges(p, 1 - s)).astype(jnp.bfloat16)
            t2[p][s].wait_recv()
            total = partial(j, edges(p, s)) + far_r[edges(p, s), :].astype(jnp.float32)
            row_s[s, edges(p, s), :] = total.astype(jnp.bfloat16)
            t1[p][s].start()

    for c in range(CHUNKS):
        start(z1[c])
    texts[pl.ds(0, rows), :] = unit_of(txt_ref[...])[0].astype(jnp.bfloat16)
    start(x1[0])
    across[OWN].start()
    for c in range(CHUNKS):
        start(z1_other[c])
    pass_on(z1[0], z3[0])
    pass_on(z1[1], z3[1])
    pass_on(x1[0], x2[0])
    across[PREV].start()
    across[NEXT].start()
    for c in range(CHUNKS):
        arrive(z1_other[c])
    wholes = [weigh(0, 3 * rows, 1, False)]
    arrive([across[PREV], across[NEXT]])
    wholes.append(weigh(0, 3 * rows, 3, False))
    arrive(x2[0])
    across[FAR].start()
    wholes.append(weigh(0, 3 * rows, 0, True))
    arrive([across[OWN], across[FAR]])
    wholes.append(weigh(0, 3 * rows, 2, False))
    loss_part(0, 3 * rows, wholes)
    pass_on(z3[0], z4[0])
    pass_on(z3[1], z4[1])
    image_partial(0, 3 * rows)
    pass_on(z4[0], z5[0])
    text_partial(0, 1)
    pass_on(z4[1], z5[1])
    text_partial(0, 0)
    for c in range(CHUNKS):
        arrive(z5[c])
        if c == 0:
            for early in range(CHUNKS):
                back_1_other(early)
        far(c)
        back_5(c)

    back_4(0)
    text_partial(1, 1)
    for j in (FAR, PREV, NEXT, OWN):
        sib_s[j] = tg[pl.ds(row_texts + j * rows, rows), :].astype(jnp.bfloat16)
        back[0][j].start()
    back_4(1)
    for h in range(2):
        give_loss(five_ls.at[h], loss_of((DOWN3, UP3)[h]))
        l5[h].start()
    text_partial(1, 0)
    back_3(0)
    text_begin(0)
    lane = lax.broadcasted_iota(jnp.int32, (1, rows), 1)

    def of_half(h, came):
        return jnp.where((lane // half) % 2 == h, came[h, pl.ds(0, 1), :], 0.0)

    arrive(l5)
    give_loss(over_ls, loss_of(OVER) + of_half(0, five_lr) + of_half(1, five_lr))
    start(l4)
    back_3(1)
    text_middle(0)
    for h in range(2):
        l4[h].wait_recv()
        give_loss(three_ls.at[h], loss_of((UP3, DOWN3)[h]) + of_half(h, over_lr))
        l3[h].start()
    back_1(0)
    for h in range(2):
        l3[h].wait_recv()
        give_loss(one_ls.at[h], loss_of((UP1, DOWN1)[h]) + of_half(h, three_lr))
        l1[h].start()
    back_1(1)

    scale_row = jnp.exp(jnp.full((1, width), ls_ref[0], jnp.float32))

    def backprop(raw, grads):
        unit, inverse = unit_of(raw)
        grads = scale_row * grads
        return (grads - unit * jnp.sum(unit * grads, axis=1, keepdims=True)) * inverse

    def finish_image(c):
        here = pl.ds(c * sub, sub)
        arrive(b1[c])
        arrive(b1_other[c])
        grads = gradient(c, OWN) + (one_r[c, 0].astype(jnp.float32) + one_r[c, 1].astype(jnp.float32))
        gi_ref[here, :] = backprop(img_ref[here, :], grads)

    def finish_text(p):
        here = parts(p)
        arrive([back[p][OWN]])
        arrive(t1[p])
        grads = partial(OWN, here) + (row_r[0, here, :].astype(jnp.float32) + row_r[1, here, :].astype(jnp.float32))
        gt_ref[here, :] = backprop(txt_ref[here, :], grads)

    for p in range(PARTS):
        finish_text(p)
    finish_image(0)
    arrive(l1)
    loss_ref[...] = loss_of(OWN) + one_lr[0, pl.ds(0, 1), :] + one_lr[1, pl.ds(0, 1), :]
    finish_image(1)
    for sent in messages:
        sent.wait_send()


N_MESSAGES = 64


def write_out(*refs):
    sources, results, sem = refs[:3], refs[3:6], refs[6]
    copies = [pltpu.make_async_copy(src, dst, sem.at[n]) for n, (src, dst) in enumerate(zip(sources, results))]
    for copy in copies:
        copy.start()
    for copy in copies:
        copy.wait()


def per_device(groups, image_emb, text_emb, log_scale, bias):
    rows, width = image_emb.shape
    sub = rows // CHUNKS
    half_type, full = jnp.bfloat16, jnp.float32
    vmem = pl.BlockSpec(memory_space=pltpu.VMEM)
    smem = pl.BlockSpec(memory_space=pltpu.SMEM)
    out_shape = (
        jax.ShapeDtypeStruct((1, rows), full),
        jax.ShapeDtypeStruct((rows, width), full),
        jax.ShapeDtypeStruct((rows, width), full),
    )
    results = pl.pallas_call(
        lambda *refs: kernel(groups, *refs),
        out_shape=out_shape,
        in_specs=[smem, smem, vmem, vmem],
        out_specs=(vmem, vmem, vmem),
        scratch_shapes=[
            pltpu.VMEM((8 * rows, width), half_type),
            pltpu.VMEM((6 * rows, width), half_type),
            pltpu.VMEM((6 * rows, 8 * rows), half_type),
            pltpu.VMEM((8 * rows, width), full),
            pltpu.VMEM((6 * rows, width), full),
            pltpu.VMEM((6 * rows, rows), full),
            pltpu.VMEM((CHUNKS, sub, width), half_type),
            pltpu.VMEM((CHUNKS, sub, width), half_type),
            pltpu.VMEM((CHUNKS, sub, width), half_type),
            pltpu.VMEM((CHUNKS, sub, width), half_type),
            pltpu.VMEM((CHUNKS, sub, width), half_type),
            pltpu.VMEM((CHUNKS, sub, width), half_type),
            pltpu.VMEM((CHUNKS, 2, sub, width), half_type),
            pltpu.VMEM((CHUNKS, 2, sub, width), half_type),
            pltpu.VMEM((4, rows, width), half_type),
            pltpu.VMEM((4, rows, width), half_type),
            pltpu.VMEM((rows, width), half_type),
            pltpu.VMEM((rows, width), half_type),
            pltpu.VMEM((2, rows, width), half_type),
            pltpu.VMEM((2, rows, width), half_type),
            pltpu.VMEM((2, 8, rows), full),
            pltpu.VMEM((2, 8, rows), full),
            pltpu.VMEM((8, rows), full),
            pltpu.VMEM((2, 8, rows), full),
            pltpu.VMEM((2, 8, rows), full),
            pltpu.VMEM((2, 8, rows), full),
            pltpu.VMEM((2, 8, rows), full),
            pltpu.VMEM((2, 8, rows), full),
            pltpu.SemaphoreType.DMA((N_MESSAGES,)),
            pltpu.SemaphoreType.DMA((N_MESSAGES,)),
        ],
        compiler_params=pltpu.CompilerParams(
            collective_id=0, has_side_effects=True, vmem_limit_bytes=48 * 1024 * 1024
        ),
    )(log_scale, bias, image_emb, text_emb)
    anywhere = pl.BlockSpec(memory_space=pl.ANY)
    loss, grad_image, grad_text = pl.pallas_call(
        write_out,
        out_shape=out_shape,
        in_specs=[vmem] * 3,
        out_specs=(anywhere,) * 3,
        scratch_shapes=[pltpu.SemaphoreType.DMA((3,))],
    )(*results)
    return (loss.reshape(rows), grad_image, grad_text)


def solution(mesh):
    groups = mesh.shape["outer"]
    in_specs = (P(("outer", "inner"), None), P(("outer", "inner"), None), P(), P())
    out_specs = (P(("outer", "inner")), P(("outer", "inner"), None), P(("outer", "inner"), None))
    return jax.shard_map(
        lambda *args: per_device(groups, *args),
        mesh=mesh, in_specs=in_specs, out_specs=out_specs, check_vma=False,
    )
```

```python
import jax
import jax.numpy as jnp
from jax import lax
from jax.experimental import pallas as pl
from jax.experimental.pallas import tpu as pltpu
from jax.sharding import PartitionSpec as P

MESH = pl.DeviceIdType.MESH
EPS = 1e-06
LOG2_E = 1.4426950408889634

X_N = 4
Z_LO = 4
Z_N = 8

OWN, FAR, PREV, NEXT = 0, 1, 2, 3
UP1, DOWN1, UP3, DOWN3, OVER = 1, 2, 3, 4, 5

CHUNKS = 2
PARTS = 1


def unit_of(raw):
    wide = raw.astype(jnp.float32)
    inverse = lax.rsqrt(jnp.sum(wide * wide, axis=1, keepdims=True) + EPS)
    return wide * inverse, inverse


def places(groups):
    outer = lax.axis_index("outer")
    inner = lax.axis_index("inner")
    z_lo = outer % Z_LO
    x, z_hi, core = inner // 4, (inner // 2) % 2, inner % 2

    def inner_of(x, z_hi, core):
        return x * 4 + z_hi * 2 + core

    def group_by(by):
        z = (z_hi * Z_LO + z_lo + by + Z_N) % Z_N
        step = by if by in (1, -1) else -by
        return ((outer + step + groups) % groups, inner_of(x, z // Z_LO, core))

    return {
        "xn": (outer, inner_of((x + 1) % X_N, z_hi, core)),
        "xp": (outer, inner_of((x + X_N - 1) % X_N, z_hi, core)),
        "sib": (outer, inner_of(x, z_hi, 1 - core)),
        "gn": group_by(1),
        "gp": group_by(-1),
        "tn": group_by(2),
        "tp": group_by(-2),
    }


def kernel(
    groups, ls_ref, b_ref, img_ref, txt_ref, loss_ref, gi_ref, gt_ref,
    texts, images, wt, tg, ig, loss_acc, five_s, five_r, over_s, over_r, three_s, three_r, one_s, one_r,
    sib_s, sib_r, far_s, far_r, row_s, row_r, five_ls, five_lr, over_ls, over_lr, three_ls, three_lr, one_ls, one_lr, ssem, rsem,
):
    rows, width = img_ref.shape
    sub = rows // CHUNKS
    half = sub // 2
    part = rows // PARTS
    edge = part // 2
    tile = 2 * rows
    row_texts = 4 * rows
    peers = places(groups)
    messages = []

    def message(src, dst, peer):
        index = len(messages)
        messages.append(
            pltpu.make_async_remote_copy(
                src_ref=src, dst_ref=dst, send_sem=ssem.at[index], recv_sem=rsem.at[index],
                device_id=peers[peer], device_id_type=MESH,
            )
        )
        return messages[-1]

    def at(c, k, h=0):
        if k < UP3:
            return (c * 3 + k) * sub + h * half
        if k == OVER:
            return 4 * rows + (c * 2 + h) * half
        first = 3 * rows if (k == UP3) == (h == 0) else 5 * rows
        return first + (c * 2 + (k == DOWN3)) * half

    def image_half(c, k, h):
        return images.at[pl.ds(at(c, k, h), half), :]

    def text(q, j):
        return texts.at[pl.ds((q * 4 + j) * rows, rows), :]

    def text_part(j, p):
        return texts.at[pl.ds(j * rows + p * part, part), :]

    def text_edge(j, p, e):
        return texts.at[pl.ds(j * rows + p * part + e * edge, edge), :]

    def halves(h):
        return pl.ds(h * half, half)

    def parts(p):
        return pl.ds(p * part, part)

    def edges(p, e):
        return pl.ds(p * part + e * edge, edge)

    z1 = [[message(image_half(c, OWN, h), image_half(c, (UP1, DOWN1)[h], h), ("gn", "gp")[h]) for h in range(2)] for c in range(CHUNKS)]
    z1_other = [
        [message(image_half(c, OWN, 1 - h), image_half(c, (UP1, DOWN1)[h], 1 - h), ("gn", "gp")[h]) for h in range(2)]
        for c in range(CHUNKS)
    ]
    z3 = [
        [message(image_half(c, (UP1, DOWN1)[h], h), image_half(c, (UP3, DOWN3)[h], h), ("tn", "tp")[h]) for h in range(2)]
        for c in range(CHUNKS)
    ]
    z4 = [
        [message(image_half(c, (UP3, DOWN3)[h], h), image_half(c, OVER, h), ("gn", "gp")[h]) for h in range(2)]
        for c in range(CHUNKS)
    ]
    z5 = [
        [message(image_half(c, OVER, h), image_half(c, (DOWN3, UP3)[h], h), ("gn", "gp")[h]) for h in range(2)]
        for c in range(CHUNKS)
    ]
    x1 = [[message(text_part(OWN, p), text_part((PREV, NEXT)[s], p), ("xn", "xp")[s]) for s in range(2)] for p in range(PARTS)]
    x2 = [
        [message(text_edge((PREV, NEXT)[s], p, s), text_edge(FAR, p, s), ("xn", "xp")[s]) for s in range(2)]
        for p in range(PARTS)
    ]
    across = [message(text(0, j), text(1, j), "sib") for j in range(4)]
    b5 = [[message(five_s.at[c, halves(h), :], five_r.at[c, halves(h), :], ("gp", "gn")[h]) for h in range(2)] for c in range(CHUNKS)]
    b4 = [[message(over_s.at[c, halves(h), :], over_r.at[c, halves(h), :], ("gp", "gn")[h]) for h in range(2)] for c in range(CHUNKS)]
    b3 = [[message(three_s.at[c, halves(h), :], three_r.at[c, halves(h), :], ("tp", "tn")[h]) for h in range(2)] for c in range(CHUNKS)]
    b1 = [[message(one_s.at[c, h, halves(h), :], one_r.at[c, h, halves(h), :], ("gp", "gn")[h]) for h in range(2)] for c in range(CHUNKS)]
    b1_other = [
        [message(one_s.at[c, h, halves(1 - h), :], one_r.at[c, h, halves(1 - h), :], ("gp", "gn")[h]) for h in range(2)]
        for c in range(CHUNKS)
    ]
    back = [[message(sib_s.at[j, parts(p), :], sib_r.at[j, parts(p), :], "sib") for j in range(4)] for p in range(PARTS)]
    t2 = [[message(far_s.at[edges(p, s), :], far_r.at[edges(p, s), :], ("xp", "xn")[s]) for s in range(2)] for p in range(PARTS)]
    t1 = [[message(row_s.at[s, parts(p), :], row_r.at[s, parts(p), :], ("xp", "xn")[s]) for s in range(2)] for p in range(PARTS)]
    l5 = [message(five_ls.at[h], five_lr.at[h], ("gp", "gn")[h]) for h in range(2)]
    l4 = [message(over_ls, over_lr.at[h], ("gp", "gn")[h]) for h in range(2)]
    l3 = [message(three_ls.at[h], three_lr.at[h], ("tp", "tn")[h]) for h in range(2)]
    l1 = [message(one_ls.at[h], one_lr.at[h], ("gp", "gn")[h]) for h in range(2)]

    def start(copies):
        for copy in copies:
            copy.start()

    def arrive(copies):
        for copy in copies:
            copy.wait_recv()

    def pass_on(arrivals, onward):
        for here, there in zip(arrivals, onward):
            here.wait_recv()
            there.start()

    barrier = pltpu.get_barrier_semaphore()
    for peer in peers.values():
        pl.semaphore_signal(barrier, inc=1, device_id=peer, device_id_type=MESH)
    own = unit_of(img_ref[...])[0].astype(jnp.bfloat16)
    for c in range(CHUNKS):
        images[pl.ds(at(c, OWN), sub), :] = own[c * sub:(c + 1) * sub]
    scale = jnp.exp(jnp.full((1, tile), ls_ref[0], jnp.float32)) * LOG2_E
    offset = b_ref[0] * LOG2_E
    pl.semaphore_wait(barrier, len(peers))

    def weigh(begin, size, n, diagonal):
        here = pl.ds(begin, size)
        columns = pl.ds(n * tile, tile)
        dots = lax.dot_general(
            images[here, :], texts[columns, :], (((1,), (1,)), ((), ())), preferred_element_type=jnp.float32
        )
        grown = jnp.exp2(scale * dots + offset)
        whole = 1.0 + grown
        inverse = pl.reciprocal(whole, approx=True)
        weights = grown * (inverse * (2.0 - whole * inverse))
        if diagonal:
            row = lax.broadcasted_iota(jnp.int32, (size, tile), 0)
            column = lax.broadcasted_iota(jnp.int32, (size, tile), 1)
            positive = row < 0
            for c in range(CHUNKS):
                first = at(c, OWN)
                positive |= (row - first == column - c * sub) & (row >= first) & (row < first + sub)
            weights = weights - positive.astype(jnp.float32)
            whole = jnp.where(positive, 1.0 + 1.0 / grown, whole)
        wt[here, columns] = weights.astype(jnp.bfloat16)
        return whole

    def loss_part(begin, size, wholes):
        here = pl.ds(begin, size)
        logs = jnp.log((wholes[0] * wholes[1]) * (wholes[2] * wholes[3]))
        loss_acc[here, :] = logs[:, :rows] + logs[:, rows:]

    def image_partial(begin, size):
        here = pl.ds(begin, size)
        ig[here, :] = jnp.dot(wt[here, :], texts[...], preferred_element_type=jnp.float32)

    def far(begin, size):
        loss_part(begin, size, [weigh(begin, size, n, False) for n in range(4)])
        image_partial(begin, size)

    def text_partial(far_ones, q):
        these = pl.ds(far_ones * 3 * rows, 3 * rows)
        columns = pl.ds(q * row_texts, row_texts)
        term = lax.dot_general(
            wt[these, columns], images[these, :], (((0,), (0,)), ((), ())), preferred_element_type=jnp.float32
        )
        if far_ones:
            tg[columns, :] += term
        else:
            tg[columns, :] = term

    def gradient(c, k):
        return ig[pl.ds(at(c, k), sub), :]

    def send_back(sent, copies, c, h, k, came=None):
        total = ig[pl.ds(at(c, k, h), half), :]
        if came is not None:
            total = total + came.astype(jnp.float32)
        sent[halves(h), :] = total.astype(jnp.bfloat16)
        copies[c][h].start()

    def back_5(c):
        for h in range(2):
            send_back(five_s.at[c], b5, c, h, (DOWN3, UP3)[h])

    def back_4(c):
        for h in range(2):
            b5[c][h].wait_recv()
            send_back(over_s.at[c], b4, c, h, OVER, five_r[c, halves(h), :])

    def back_3(c):
        for h in range(2):
            b4[c][h].wait_recv()
            send_back(three_s.at[c], b3, c, h, (UP3, DOWN3)[h], over_r[c, halves(h), :])

    def back_1(c):
        for h in range(2):
            b3[c][h].wait_recv()
            send_back(one_s.at[c, h], b1, c, h, (UP1, DOWN1)[h], three_r[c, halves(h), :])

    def back_1_other(c):
        for h in range(2):
            one_s[c, h, halves(1 - h), :] = ig[pl.ds(at(c, (UP1, DOWN1)[h], 1 - h), half), :].astype(jnp.bfloat16)
            b1_other[c][h].start()

    def loss_of(k):
        block = jnp.concatenate(
            [loss_acc[pl.ds(at(c, k, h), half), :] for c in range(CHUNKS) for h in range(2)], axis=0
        )
        return jnp.sum(block.T, axis=0, keepdims=True)

    def give_loss(dst, row):
        dst[...] = jnp.broadcast_to(row, dst.shape)

    def partial(j, where):
        return tg[pl.ds(j * rows + where.start, where.size), :] + sib_r[j, where, :].astype(jnp.float32)

    def text_begin(p):
        arrive([back[p][FAR]])
        for s in range(2):
            far_s[edges(p, s), :] = partial(FAR, edges(p, s)).astype(jnp.bfloat16)
            t2[p][s].start()

    def text_middle(p):
        for s in range(2):
            j = (PREV, NEXT)[s]
            arrive([back[p][j]])
            row_s[s, edges(p, 1 - s), :] = partial(j, edges(p, 1 - s)).astype(jnp.bfloat16)
            t2[p][s].wait_recv()
            total = partial(j, edges(p, s)) + far_r[edges(p, s), :].astype(jnp.float32)
            row_s[s, edges(p, s), :] = total.astype(jnp.bfloat16)
            t1[p][s].start()

    for c in range(CHUNKS):
        start(z1[c])
    texts[pl.ds(0, rows), :] = unit_of(txt_ref[...])[0].astype(jnp.bfloat16)
    start(x1[0])
    across[OWN].start()
    for c in range(CHUNKS):
        start(z1_other[c])
    pass_on(z1[0], z3[0])
    pass_on(z1[1], z3[1])
    pass_on(x1[0], x2[0])
    across[PREV].start()
    across[NEXT].start()
    for c in range(CHUNKS):
        arrive(z1_other[c])
    wholes = [weigh(0, 3 * rows, 1, False)]
    arrive([across[PREV], across[NEXT]])
    wholes.append(weigh(0, 3 * rows, 3, False))
    arrive(x2[0])
    across[FAR].start()
    wholes.append(weigh(0, 3 * rows, 0, True))
    arrive([across[OWN], across[FAR]])
    wholes.append(weigh(0, 3 * rows, 2, False))
    loss_part(0, 3 * rows, wholes)
    pass_on(z3[0], z4[0])
    pass_on(z3[1], z4[1])
    image_partial(0, 3 * rows)
    pass_on(z4[0], z5[0])
    text_partial(0, 1)
    pass_on(z4[1], z5[1])
    far(3 * rows, 2 * rows)
    arrive(z5[0])
    for c in range(CHUNKS):
        back_1_other(c)
    arrive(z5[1])
    far(5 * rows, rows)
    for c in range(CHUNKS):
        back_5(c)

    text_partial(0, 0)
    back_4(0)
    text_partial(1, 1)
    for j in (FAR, PREV, NEXT, OWN):
        sib_s[j] = tg[pl.ds(row_texts + j * rows, rows), :].astype(jnp.bfloat16)
        back[0][j].start()
    back_4(1)
    for h in range(2):
        give_loss(five_ls.at[h], loss_of((DOWN3, UP3)[h]))
        l5[h].start()
    text_partial(1, 0)
    back_3(0)
    text_begin(0)
    lane = lax.broadcasted_iota(jnp.int32, (1, rows), 1)

    def of_half(h, came):
        return jnp.where((lane // half) % 2 == h, came[h, pl.ds(0, 1), :], 0.0)

    arrive(l5)
    give_loss(over_ls, loss_of(OVER) + of_half(0, five_lr) + of_half(1, five_lr))
    start(l4)
    back_3(1)
    text_middle(0)
    for h in range(2):
        l4[h].wait_recv()
        give_loss(three_ls.at[h], loss_of((UP3, DOWN3)[h]) + of_half(h, over_lr))
        l3[h].start()
    back_1(0)
    for h in range(2):
        l3[h].wait_recv()
        give_loss(one_ls.at[h], loss_of((UP1, DOWN1)[h]) + of_half(h, three_lr))
        l1[h].start()
    back_1(1)

    scale_row = jnp.exp(jnp.full((1, width), ls_ref[0], jnp.float32))

    def backprop(raw, grads):
        unit, inverse = unit_of(raw)
        grads = scale_row * grads
        return (grads - unit * jnp.sum(unit * grads, axis=1, keepdims=True)) * inverse

    def finish_image(c):
        here = pl.ds(c * sub, sub)
        arrive(b1[c])
        arrive(b1_other[c])
        grads = gradient(c, OWN) + (one_r[c, 0].astype(jnp.float32) + one_r[c, 1].astype(jnp.float32))
        gi_ref[here, :] = backprop(img_ref[here, :], grads)

    def finish_text(p):
        here = parts(p)
        arrive([back[p][OWN]])
        arrive(t1[p])
        grads = partial(OWN, here) + (row_r[0, here, :].astype(jnp.float32) + row_r[1, here, :].astype(jnp.float32))
        gt_ref[here, :] = backprop(txt_ref[here, :], grads)

    for p in range(PARTS):
        finish_text(p)
    finish_image(0)
    arrive(l1)
    loss_ref[...] = loss_of(OWN) + one_lr[0, pl.ds(0, 1), :] + one_lr[1, pl.ds(0, 1), :]
    finish_image(1)
    for sent in messages:
        sent.wait_send()


N_MESSAGES = 64


def per_device(groups, image_emb, text_emb, log_scale, bias):
    rows, width = image_emb.shape
    sub = rows // CHUNKS
    half_type, full = jnp.bfloat16, jnp.float32
    vmem = pl.BlockSpec(memory_space=pltpu.VMEM)
    smem = pl.BlockSpec(memory_space=pltpu.SMEM)
    out_shape = (
        jax.ShapeDtypeStruct((1, rows), full),
        jax.ShapeDtypeStruct((rows, width), full),
        jax.ShapeDtypeStruct((rows, width), full),
    )
    loss, grad_image, grad_text = pl.pallas_call(
        lambda *refs: kernel(groups, *refs),
        out_shape=out_shape,
        in_specs=[smem, smem, vmem, vmem],
        out_specs=(vmem, vmem, vmem),
        scratch_shapes=[
            pltpu.VMEM((8 * rows, width), half_type),
            pltpu.VMEM((6 * rows, width), half_type),
            pltpu.VMEM((6 * rows, 8 * rows), half_type),
            pltpu.VMEM((8 * rows, width), full),
            pltpu.VMEM((6 * rows, width), full),
            pltpu.VMEM((6 * rows, rows), full),
            pltpu.VMEM((CHUNKS, sub, width), half_type),
            pltpu.VMEM((CHUNKS, sub, width), half_type),
            pltpu.VMEM((CHUNKS, sub, width), half_type),
            pltpu.VMEM((CHUNKS, sub, width), half_type),
            pltpu.VMEM((CHUNKS, sub, width), half_type),
            pltpu.VMEM((CHUNKS, sub, width), half_type),
            pltpu.VMEM((CHUNKS, 2, sub, width), half_type),
            pltpu.VMEM((CHUNKS, 2, sub, width), half_type),
            pltpu.VMEM((4, rows, width), half_type),
            pltpu.VMEM((4, rows, width), half_type),
            pltpu.VMEM((rows, width), half_type),
            pltpu.VMEM((rows, width), half_type),
            pltpu.VMEM((2, rows, width), half_type),
            pltpu.VMEM((2, rows, width), half_type),
            pltpu.VMEM((2, 8, rows), full),
            pltpu.VMEM((2, 8, rows), full),
            pltpu.VMEM((8, rows), full),
            pltpu.VMEM((2, 8, rows), full),
            pltpu.VMEM((2, 8, rows), full),
            pltpu.VMEM((2, 8, rows), full),
            pltpu.VMEM((2, 8, rows), full),
            pltpu.VMEM((2, 8, rows), full),
            pltpu.SemaphoreType.DMA((N_MESSAGES,)),
            pltpu.SemaphoreType.DMA((N_MESSAGES,)),
        ],
        compiler_params=pltpu.CompilerParams(
            collective_id=0, has_side_effects=True, vmem_limit_bytes=48 * 1024 * 1024
        ),
    )(log_scale, bias, image_emb, text_emb)
    return (loss.reshape(rows), grad_image, grad_text)


def solution(mesh):
    groups = mesh.shape["outer"]
    in_specs = (P(("outer", "inner"), None), P(("outer", "inner"), None), P(), P())
    out_specs = (P(("outer", "inner")), P(("outer", "inner"), None), P(("outer", "inner"), None))
    return jax.shard_map(
        lambda *args: per_device(groups, *args),
        mesh=mesh, in_specs=in_specs, out_specs=out_specs, check_vma=False,
    )
```

```python
import jax
import jax.numpy as jnp
from jax import lax
from jax.experimental import pallas as pl
from jax.experimental.pallas import tpu as pltpu
from jax.sharding import PartitionSpec as P

MESH = pl.DeviceIdType.MESH
EPS = 1e-06
LOG2_E = 1.4426950408889634

X_N = 4
Z_LO = 4
Z_N = 8

OWN, FAR, PREV, NEXT = 0, 1, 2, 3
UP1, DOWN1, UP3, DOWN3, OVER = 1, 2, 3, 4, 5

CHUNKS = 2
PARTS = 1


def unit_of(raw):
    wide = raw.astype(jnp.float32)
    inverse = lax.rsqrt(jnp.sum(wide * wide, axis=1, keepdims=True) + EPS)
    return wide * inverse, inverse


def places(groups):
    outer = lax.axis_index("outer")
    inner = lax.axis_index("inner")
    z_lo = outer % Z_LO
    x, z_hi, core = inner // 4, (inner // 2) % 2, inner % 2

    def inner_of(x, z_hi, core):
        return x * 4 + z_hi * 2 + core

    def group_by(by):
        z = (z_hi * Z_LO + z_lo + by + Z_N) % Z_N
        step = by if by in (1, -1) else -by
        return ((outer + step + groups) % groups, inner_of(x, z // Z_LO, core))

    return {
        "xn": (outer, inner_of((x + 1) % X_N, z_hi, core)),
        "xp": (outer, inner_of((x + X_N - 1) % X_N, z_hi, core)),
        "sib": (outer, inner_of(x, z_hi, 1 - core)),
        "gn": group_by(1),
        "gp": group_by(-1),
        "tn": group_by(2),
        "tp": group_by(-2),
    }


def kernel(
    groups, ls_ref, b_ref, img_ref, txt_ref, loss_ref, gi_ref, gt_ref,
    texts, images, wt, tg, ig, loss_acc, five_s, five_r, over_s, over_r, three_s, three_r, one_s, one_r,
    sib_s, sib_r, far_s, far_r, row_s, row_r, five_ls, five_lr, over_ls, over_lr, three_ls, three_lr, one_ls, one_lr, ssem, rsem,
):
    rows, width = img_ref.shape
    sub = rows // CHUNKS
    half = sub // 2
    part = rows // PARTS
    edge = part // 2
    tile = 2 * rows
    row_texts = 4 * rows
    peers = places(groups)
    messages = []

    def message(src, dst, peer):
        index = len(messages)
        messages.append(
            pltpu.make_async_remote_copy(
                src_ref=src, dst_ref=dst, send_sem=ssem.at[index], recv_sem=rsem.at[index],
                device_id=peers[peer], device_id_type=MESH,
            )
        )
        return messages[-1]

    def at(c, k, h=0):
        if k < UP3:
            return (c * 3 + k) * sub + h * half
        if k == OVER:
            return 4 * rows + (c * 2 + h) * half
        first = 3 * rows if (k == UP3) == (h == 0) else 5 * rows
        return first + (c * 2 + (k == DOWN3)) * half

    def image_half(c, k, h):
        return images.at[pl.ds(at(c, k, h), half), :]

    def text(q, j):
        return texts.at[pl.ds((q * 4 + j) * rows, rows), :]

    def text_part(j, p):
        return texts.at[pl.ds(j * rows + p * part, part), :]

    def text_edge(j, p, e):
        return texts.at[pl.ds(j * rows + p * part + e * edge, edge), :]

    def halves(h):
        return pl.ds(h * half, half)

    def parts(p):
        return pl.ds(p * part, part)

    def edges(p, e):
        return pl.ds(p * part + e * edge, edge)

    z1 = [[message(image_half(c, OWN, h), image_half(c, (UP1, DOWN1)[h], h), ("gn", "gp")[h]) for h in range(2)] for c in range(CHUNKS)]
    z1_other = [
        [message(image_half(c, OWN, 1 - h), image_half(c, (UP1, DOWN1)[h], 1 - h), ("gn", "gp")[h]) for h in range(2)]
        for c in range(CHUNKS)
    ]
    z3 = [
        [message(image_half(c, (UP1, DOWN1)[h], h), image_half(c, (UP3, DOWN3)[h], h), ("tn", "tp")[h]) for h in range(2)]
        for c in range(CHUNKS)
    ]
    z4 = [
        [message(image_half(c, (UP3, DOWN3)[h], h), image_half(c, OVER, h), ("gn", "gp")[h]) for h in range(2)]
        for c in range(CHUNKS)
    ]
    z5 = [
        [message(image_half(c, OVER, h), image_half(c, (DOWN3, UP3)[h], h), ("gn", "gp")[h]) for h in range(2)]
        for c in range(CHUNKS)
    ]
    x1 = [[message(text_part(OWN, p), text_part((PREV, NEXT)[s], p), ("xn", "xp")[s]) for s in range(2)] for p in range(PARTS)]
    x2 = [
        [message(text_edge((PREV, NEXT)[s], p, s), text_edge(FAR, p, s), ("xn", "xp")[s]) for s in range(2)]
        for p in range(PARTS)
    ]
    across = [message(text(0, j), text(1, j), "sib") for j in range(4)]
    b5 = [[message(five_s.at[c, halves(h), :], five_r.at[c, halves(h), :], ("gp", "gn")[h]) for h in range(2)] for c in range(CHUNKS)]
    b4 = [[message(over_s.at[c, halves(h), :], over_r.at[c, halves(h), :], ("gp", "gn")[h]) for h in range(2)] for c in range(CHUNKS)]
    b3 = [[message(three_s.at[c, halves(h), :], three_r.at[c, halves(h), :], ("tp", "tn")[h]) for h in range(2)] for c in range(CHUNKS)]
    b1 = [[message(one_s.at[c, h, halves(h), :], one_r.at[c, h, halves(h), :], ("gp", "gn")[h]) for h in range(2)] for c in range(CHUNKS)]
    b1_other = [
        [message(one_s.at[c, h, halves(1 - h), :], one_r.at[c, h, halves(1 - h), :], ("gp", "gn")[h]) for h in range(2)]
        for c in range(CHUNKS)
    ]
    back = [[message(sib_s.at[j, parts(p), :], sib_r.at[j, parts(p), :], "sib") for j in range(4)] for p in range(PARTS)]
    t2 = [[message(far_s.at[edges(p, s), :], far_r.at[edges(p, s), :], ("xp", "xn")[s]) for s in range(2)] for p in range(PARTS)]
    t1 = [[message(row_s.at[s, parts(p), :], row_r.at[s, parts(p), :], ("xp", "xn")[s]) for s in range(2)] for p in range(PARTS)]
    l5 = [message(five_ls.at[h], five_lr.at[h], ("gp", "gn")[h]) for h in range(2)]
    l4 = [message(over_ls, over_lr.at[h], ("gp", "gn")[h]) for h in range(2)]
    l3 = [message(three_ls.at[h], three_lr.at[h], ("tp", "tn")[h]) for h in range(2)]
    l1 = [message(one_ls.at[h], one_lr.at[h], ("gp", "gn")[h]) for h in range(2)]

    def start(copies):
        for copy in copies:
            copy.start()

    def arrive(copies):
        for copy in copies:
            copy.wait_recv()

    def pass_on(arrivals, onward):
        for here, there in zip(arrivals, onward):
            here.wait_recv()
            there.start()

    barrier = pltpu.get_barrier_semaphore()
    for peer in peers.values():
        pl.semaphore_signal(barrier, inc=1, device_id=peer, device_id_type=MESH)
    own = unit_of(img_ref[...])[0].astype(jnp.bfloat16)
    for c in range(CHUNKS):
        images[pl.ds(at(c, OWN), sub), :] = own[c * sub:(c + 1) * sub]
    scale = jnp.exp(jnp.full((1, tile), ls_ref[0], jnp.float32)) * LOG2_E
    offset = b_ref[0] * LOG2_E
    pl.semaphore_wait(barrier, len(peers))

    def weigh(begin, size, n, diagonal):
        here = pl.ds(begin, size)
        columns = pl.ds(n * tile, tile)
        dots = lax.dot_general(
            images[here, :], texts[columns, :], (((1,), (1,)), ((), ())), preferred_element_type=jnp.float32
        )
        grown = jnp.exp2(scale * dots + offset)
        whole = 1.0 + grown
        inverse = pl.reciprocal(whole, approx=True)
        weights = grown * (inverse * (2.0 - whole * inverse))
        if diagonal:
            row = lax.broadcasted_iota(jnp.int32, (size, tile), 0)
            column = lax.broadcasted_iota(jnp.int32, (size, tile), 1)
            positive = row < 0
            for c in range(CHUNKS):
                first = at(c, OWN)
                positive |= (row - first == column - c * sub) & (row >= first) & (row < first + sub)
            weights = weights - positive.astype(jnp.float32)
            whole = jnp.where(positive, 1.0 + 1.0 / grown, whole)
        wt[here, columns] = weights.astype(jnp.bfloat16)
        return whole

    def loss_part(begin, size, wholes):
        here = pl.ds(begin, size)
        logs = jnp.log((wholes[0] * wholes[1]) * (wholes[2] * wholes[3]))
        loss_acc[here, :] = logs[:, :rows] + logs[:, rows:]

    def image_partial(begin, size):
        here = pl.ds(begin, size)
        ig[here, :] = jnp.dot(wt[here, :], texts[...], preferred_element_type=jnp.float32)

    def far(begin, size):
        loss_part(begin, size, [weigh(begin, size, n, False) for n in range(4)])
        image_partial(begin, size)

    def text_partial(far_ones, q):
        these = pl.ds(far_ones * 3 * rows, 3 * rows)
        columns = pl.ds(q * row_texts, row_texts)
        term = lax.dot_general(
            wt[these, columns], images[these, :], (((0,), (0,)), ((), ())), preferred_element_type=jnp.float32
        )
        if far_ones:
            tg[columns, :] += term
        else:
            tg[columns, :] = term

    def gradient(c, k):
        return ig[pl.ds(at(c, k), sub), :]

    def send_back(sent, copies, c, h, k, came=None):
        total = ig[pl.ds(at(c, k, h), half), :]
        if came is not None:
            total = total + came.astype(jnp.float32)
        sent[halves(h), :] = total.astype(jnp.bfloat16)
        copies[c][h].start()

    def back_5(c):
        for h in range(2):
            send_back(five_s.at[c], b5, c, h, (DOWN3, UP3)[h])

    def back_4(c):
        for h in range(2):
            b5[c][h].wait_recv()
            send_back(over_s.at[c], b4, c, h, OVER, five_r[c, halves(h), :])

    def back_3(c):
        for h in range(2):
            b4[c][h].wait_recv()
            send_back(three_s.at[c], b3, c, h, (UP3, DOWN3)[h], over_r[c, halves(h), :])

    def back_1(c):
        for h in range(2):
            b3[c][h].wait_recv()
            send_back(one_s.at[c, h], b1, c, h, (UP1, DOWN1)[h], three_r[c, halves(h), :])

    def back_1_other(c):
        for h in range(2):
            one_s[c, h, halves(1 - h), :] = ig[pl.ds(at(c, (UP1, DOWN1)[h], 1 - h), half), :].astype(jnp.bfloat16)
            b1_other[c][h].start()

    def loss_of(k):
        block = jnp.concatenate(
            [loss_acc[pl.ds(at(c, k, h), half), :] for c in range(CHUNKS) for h in range(2)], axis=0
        )
        return jnp.sum(block.T, axis=0, keepdims=True)

    def give_loss(dst, row):
        dst[...] = jnp.broadcast_to(row, dst.shape)

    def partial(j, where):
        return tg[pl.ds(j * rows + where.start, where.size), :] + sib_r[j, where, :].astype(jnp.float32)

    def text_begin(p):
        arrive([back[p][FAR]])
        for s in range(2):
            far_s[edges(p, s), :] = partial(FAR, edges(p, s)).astype(jnp.bfloat16)
            t2[p][s].start()

    def text_middle(p):
        for s in range(2):
            j = (PREV, NEXT)[s]
            arrive([back[p][j]])
            row_s[s, edges(p, 1 - s), :] = partial(j, edges(p, 1 - s)).astype(jnp.bfloat16)
            t2[p][s].wait_recv()
            total = partial(j, edges(p, s)) + far_r[edges(p, s), :].astype(jnp.float32)
            row_s[s, edges(p, s), :] = total.astype(jnp.bfloat16)
            t1[p][s].start()

    start(z1[0])
    texts[pl.ds(0, rows), :] = unit_of(txt_ref[...])[0].astype(jnp.bfloat16)
    start(z1[1])
    start(x1[0])
    across[OWN].start()
    for c in range(CHUNKS):
        start(z1_other[c])
    pass_on(z1[0], z3[0])
    pass_on(z1[1], z3[1])
    pass_on(x1[0], x2[0])
    across[PREV].start()
    across[NEXT].start()
    for c in range(CHUNKS):
        arrive(z1_other[c])
    wholes = [weigh(0, 3 * rows, 1, False)]
    arrive([across[PREV], across[NEXT]])
    wholes.append(weigh(0, 3 * rows, 3, False))
    arrive(x2[0])
    across[FAR].start()
    wholes.append(weigh(0, 3 * rows, 0, True))
    arrive([across[OWN], across[FAR]])
    wholes.append(weigh(0, 3 * rows, 2, False))
    loss_part(0, 3 * rows, wholes)
    pass_on(z3[0], z4[0])
    pass_on(z3[1], z4[1])
    image_partial(0, 3 * rows)
    pass_on(z4[0], z5[0])
    text_partial(0, 1)
    pass_on(z4[1], z5[1])
    far(3 * rows, 2 * rows)
    arrive(z5[0])
    for c in range(CHUNKS):
        back_1_other(c)
    far(5 * rows, sub)
    back_5(0)
    arrive(z5[1])
    far(5 * rows + sub, sub)
    back_5(1)

    text_partial(0, 0)
    back_4(0)
    text_partial(1, 1)
    for j in (FAR, PREV, NEXT, OWN):
        sib_s[j] = tg[pl.ds(row_texts + j * rows, rows), :].astype(jnp.bfloat16)
        back[0][j].start()
    back_4(1)
    for h in range(2):
        give_loss(five_ls.at[h], loss_of((DOWN3, UP3)[h]))
        l5[h].start()
    text_partial(1, 0)
    back_3(0)
    text_begin(0)
    lane = lax.broadcasted_iota(jnp.int32, (1, rows), 1)

    def of_half(h, came):
        return jnp.where((lane // half) % 2 == h, came[h, pl.ds(0, 1), :], 0.0)

    arrive(l5)
    give_loss(over_ls, loss_of(OVER) + of_half(0, five_lr) + of_half(1, five_lr))
    start(l4)
    back_3(1)
    text_middle(0)
    for h in range(2):
        l4[h].wait_recv()
        give_loss(three_ls.at[h], loss_of((UP3, DOWN3)[h]) + of_half(h, over_lr))
        l3[h].start()
    back_1(0)
    for h in range(2):
        l3[h].wait_recv()
        give_loss(one_ls.at[h], loss_of((UP1, DOWN1)[h]) + of_half(h, three_lr))
        l1[h].start()
    back_1(1)

    scale_row = jnp.exp(jnp.full((1, width), ls_ref[0], jnp.float32))

    def backprop(raw, grads):
        unit, inverse = unit_of(raw)
        grads = scale_row * grads
        return (grads - unit * jnp.sum(unit * grads, axis=1, keepdims=True)) * inverse

    def finish_image(c):
        here = pl.ds(c * sub, sub)
        arrive(b1[c])
        arrive(b1_other[c])
        grads = gradient(c, OWN) + (one_r[c, 0].astype(jnp.float32) + one_r[c, 1].astype(jnp.float32))
        gi_ref[here, :] = backprop(img_ref[here, :], grads)

    def finish_text(p):
        here = parts(p)
        arrive([back[p][OWN]])
        arrive(t1[p])
        grads = partial(OWN, here) + (row_r[0, here, :].astype(jnp.float32) + row_r[1, here, :].astype(jnp.float32))
        gt_ref[here, :] = backprop(txt_ref[here, :], grads)

    for p in range(PARTS):
        finish_text(p)
    finish_image(0)
    arrive(l1)
    loss_ref[...] = loss_of(OWN) + one_lr[0, pl.ds(0, 1), :] + one_lr[1, pl.ds(0, 1), :]
    finish_image(1)
    for sent in messages:
        sent.wait_send()


N_MESSAGES = 64


def per_device(groups, image_emb, text_emb, log_scale, bias):
    rows, width = image_emb.shape
    sub = rows // CHUNKS
    half_type, full = jnp.bfloat16, jnp.float32
    vmem = pl.BlockSpec(memory_space=pltpu.VMEM)
    smem = pl.BlockSpec(memory_space=pltpu.SMEM)
    out_shape = (
        jax.ShapeDtypeStruct((1, rows), full),
        jax.ShapeDtypeStruct((rows, width), full),
        jax.ShapeDtypeStruct((rows, width), full),
    )
    loss, grad_image, grad_text = pl.pallas_call(
        lambda *refs: kernel(groups, *refs),
        out_shape=out_shape,
        in_specs=[smem, smem, vmem, vmem],
        out_specs=(vmem, vmem, vmem),
        scratch_shapes=[
            pltpu.VMEM((8 * rows, width), half_type),
            pltpu.VMEM((6 * rows, width), half_type),
            pltpu.VMEM((6 * rows, 8 * rows), half_type),
            pltpu.VMEM((8 * rows, width), full),
            pltpu.VMEM((6 * rows, width), full),
            pltpu.VMEM((6 * rows, rows), full),
            pltpu.VMEM((CHUNKS, sub, width), half_type),
            pltpu.VMEM((CHUNKS, sub, width), half_type),
            pltpu.VMEM((CHUNKS, sub, width), half_type),
            pltpu.VMEM((CHUNKS, sub, width), half_type),
            pltpu.VMEM((CHUNKS, sub, width), half_type),
            pltpu.VMEM((CHUNKS, sub, width), half_type),
            pltpu.VMEM((CHUNKS, 2, sub, width), half_type),
            pltpu.VMEM((CHUNKS, 2, sub, width), half_type),
            pltpu.VMEM((4, rows, width), half_type),
            pltpu.VMEM((4, rows, width), half_type),
            pltpu.VMEM((rows, width), half_type),
            pltpu.VMEM((rows, width), half_type),
            pltpu.VMEM((2, rows, width), half_type),
            pltpu.VMEM((2, rows, width), half_type),
            pltpu.VMEM((2, 8, rows), full),
            pltpu.VMEM((2, 8, rows), full),
            pltpu.VMEM((8, rows), full),
            pltpu.VMEM((2, 8, rows), full),
            pltpu.VMEM((2, 8, rows), full),
            pltpu.VMEM((2, 8, rows), full),
            pltpu.VMEM((2, 8, rows), full),
            pltpu.VMEM((2, 8, rows), full),
            pltpu.SemaphoreType.DMA((N_MESSAGES,)),
            pltpu.SemaphoreType.DMA((N_MESSAGES,)),
        ],
        compiler_params=pltpu.CompilerParams(
            collective_id=0, has_side_effects=True, vmem_limit_bytes=48 * 1024 * 1024
        ),
    )(log_scale, bias, image_emb, text_emb)
    return (loss.reshape(rows), grad_image, grad_text)


def solution(mesh):
    groups = mesh.shape["outer"]
    in_specs = (P(("outer", "inner"), None), P(("outer", "inner"), None), P(), P())
    out_specs = (P(("outer", "inner")), P(("outer", "inner"), None), P(("outer", "inner"), None))
    return jax.shard_map(
        lambda *args: per_device(groups, *args),
        mesh=mesh, in_specs=in_specs, out_specs=out_specs, check_vma=False,
    )
```
